32 devices in a mesh: stars: 32 (over z, y, x, core).
Axes of the slice: x: 2, y: 2, z: 4, core: 2. Of those that a mesh axis runs over, the one named last changes fastest.
Arguments:
- star_state: float32 [6, 131072], P(None, 'stars'), may hold values from -8 to 8
- old_force: float32 [6, 131072], P(None, 'stars'), may hold values from -3 to 3
- star_mass: float32 [131072], P('stars'), may hold values from 3.8146973e-06 to 1.5258789e-05
- elapsed: float32 [131072], P('stars'), may hold values from 0.02 to 0.08
- active_ids: int32 [256], P('stars'), may hold values from 0 to 131071, as said below
- neighbours: int32 [256, 128], P('stars'), may hold values from 0 to 131071, as said below
- list_length: int32 [256], P('stars'), may hold values from 64 to 128
Outputs:
- new_state: float32 [6, 256], P(None, 'stars')
- new_forces: float32 [12, 256], P(None, 'stars')
- corrector_terms: float32 [6, 256], P(None, 'stars')
The draws below stay inside these ranges and needn't reach their ends.
Inputs may be any that keep to these rules, and one draw needn't show every extreme that they name: `active_ids`: star id s is owned by the device holding column s of the star arrays, that is device s // 4096. `neighbours`: among the 1024 entries in the rows of one device, at most 64 are ids owned by any one device, and exactly 64 are owned by some device.
All inputs are finite; a program needn't handle non-finite values.
Results may differ from the reference program's by a relative error of at most 0.00026.
Values sent between devices are 32-bit elements; how exact they have to be, the bound alone decides.
No kernel may reach another device: no remote copies, remote signals or barrier semaphores. Data moves between devices by JAX's collectives and lax.ppermute only.
A program may use at most 192 MiB of HBM per device.

```python
import math
import jax
import jax.numpy as jnp
from jax import lax

STARS_DEV = 4096
ACTIVE_DEV = 8
NB = 128
STARS = 131072
ACTIVE = 256
CAP = 64
GROUPS = 256
N_STARS = 32


def common_ids(key):
    key_owner = jax.random.fold_in(key, 101)
    key_local = jax.random.fold_in(key, 102)
    root_draw = jax.random.randint(key_owner, (ACTIVE,), 0, 1024)
    owner_rank = root_draw * root_draw * N_STARS // 1048576
    active = owner_rank * STARS_DEV + jax.random.randint(key_local, (ACTIVE,), 0, STARS_DEV)
    residue = active % GROUPS
    block_len = ACTIVE_DEV * NB
    ticket_owner = jnp.arange(N_STARS * CAP) // CAP

    def one_block(block_index):
        block_key = jax.random.fold_in(jax.random.fold_in(key, 103), block_index)
        key_full, key_order, key_shuffle = jax.random.split(block_key, 3)
        full_owner = jax.random.randint(key_full, (), 0, N_STARS)
        priority = jax.random.permutation(key_order, N_STARS * CAP)
        priority = jnp.where(ticket_owner == full_owner, -1, priority)
        chosen = jnp.argsort(priority, stable=True)[:block_len]
        owners = ticket_owner[chosen]
        return owners[jax.random.permutation(key_shuffle, block_len)]
    listed_owner = jax.vmap(one_block)(jnp.arange(N_STARS)).reshape(ACTIVE, NB)
    member_step = jax.random.randint(jax.random.fold_in(key, 104), (ACTIVE, NB), 0, 16)
    listed = listed_owner * STARS_DEV + member_step * GROUPS + residue[:, None]
    return (active.astype(jnp.int32), listed.astype(jnp.int32))


def draw_active_ids(key, part):
    return common_ids(key)[0]


def draw_neighbours(key, part):
    return common_ids(key)[1]


def draw_star_state(key, part):
    spread = math.sqrt(0.6 * NB / STARS)
    reach = 0.9 * spread * GROUPS ** (1.0 / 3.0)
    key_centre = jax.random.fold_in(key, 201)
    key_drift = jax.random.fold_in(key, 202)
    key_offset = jax.random.fold_in(key, 203)
    centre = reach * jnp.clip(jax.random.normal(key_centre, (3, GROUPS), jnp.float32), -4.0, 4.0)
    drift = 0.25 * jnp.clip(jax.random.normal(key_drift, (3, GROUPS), jnp.float32), -4.0, 4.0)
    offset = jnp.clip(jax.random.normal(key_offset, (6, STARS), jnp.float32), -4.0, 4.0)
    member = jnp.arange(STARS) % GROUPS
    position = centre[:, member] + spread * offset[0:3]
    velocity = drift[:, member] + 4.0 * spread * offset[3:6]
    return jnp.concatenate([position, velocity], axis=0).astype(jnp.float32)


def touch_ends(values, stream_key, least, top_value):
    extent = values.shape
    place = [jax.random.randint(jax.random.fold_in(stream_key, axis), (), 0, extent[axis]) for axis in range(len(extent))]
    values = values.at[tuple(place)].set(least)
    longest = extent.index(max(extent))
    place[longest] = (place[longest] + 1) % extent[longest]
    return values.at[tuple(place)].set(top_value)


def levels(rng, shape, pieces, smallest, top_value):
    factor_of, own = 1.0, jax.random.fold_in(rng, 6)
    for dim, blocks in pieces:
        draws = jnp.exp(jax.random.uniform(jax.random.fold_in(own, dim), (blocks,), jnp.float32, smallest / len(pieces), top_value / len(pieces)))
        factor_of = factor_of * jnp.repeat(draws, shape[dim] // blocks).reshape([-1 if axis == dim else 1 for axis in range(len(shape))])
    return factor_of


def centred(own_key, shape, width, bound, shards=(), held_as=jnp.bfloat16):
    result = jax.random.normal(own_key, shape, jnp.float32) * width
    if len(shards) > 0:
        result = levels(own_key, shape, shards, -0.22, 0.18) * result
    return jnp.clip(result, min=-bound, max=bound).astype(held_as)


def setup_inputs(seed: int = 0) -> dict:
    key_list = jax.random.split(jax.random.key(seed), 8)
    return {
        "star_state": draw_star_state(jax.random.fold_in(key_list[7], 71), 0),
        "old_force": centred(key_list[1], (6, STARS), 0.5, 3.0, ((1, 32),), jnp.float32),
        "star_mass": jnp.clip(jnp.exp(math.log(1.52587890625e-05) - 1.3862944 * jax.random.uniform(key_list[2], (STARS,), jnp.float32) ** levels(key_list[2], (STARS,), ((0, 32),), -0.2, 0.2)), 3.814697265625e-06, 1.52587890625e-05),
        "elapsed": jnp.clip(jnp.exp(math.log(0.08) - 1.3862944 * jax.random.uniform(key_list[3], (STARS,), jnp.float32) ** levels(key_list[3], (STARS,), ((0, 32),), -0.2, 0.2)), 0.02, 0.08),
        "active_ids": draw_active_ids(jax.random.fold_in(key_list[7], 71), 0),
        "neighbours": draw_neighbours(jax.random.fold_in(key_list[7], 71), 0),
        "list_length": touch_ends(jax.random.randint(key_list[6], (ACTIVE,), NB // 2, NB + 1), jax.random.fold_in(key_list[6], 1), NB // 2, NB).astype(jnp.int32),
    }


def predict(star_state, old_force, star_mass, elapsed):
    step_one = elapsed[None, :]
    position = star_state[0:3] + step_one * (star_state[3:6] + step_one * (0.5 * old_force[0:3] + step_one * old_force[3:6] / 6.0))
    velocity = star_state[3:6] + step_one * (old_force[0:3] + 0.5 * step_one * old_force[3:6])
    return jnp.concatenate([position, velocity, star_mass[None, :]], axis=0)

def pair_terms(targets, sources, softening):
    separation = sources[0:3, None, :] - targets[0:3, :, None]
    relative = sources[3:6, None, :] - targets[3:6, :, None]
    dist_sq = lax.optimization_barrier(jnp.sum(separation * separation, axis=0)) + softening
    inverse = 1.0 / dist_sq
    strength = sources[6][None, :] * inverse * jnp.sqrt(inverse)
    radial = 3.0 * lax.optimization_barrier(jnp.sum(separation * relative, axis=0)) * inverse
    accel_sum = lax.optimization_barrier(jnp.sum(strength[None] * separation, axis=2))
    jerk_sum = lax.optimization_barrier(jnp.sum(strength[None] * (relative - radial[None] * separation), axis=2))
    return jnp.concatenate([accel_sum, jerk_sum], axis=0)

def listed_terms(targets, listed, in_list):
    separation = listed[0:3] - targets[0:3, :, None]
    relative = listed[3:6] - targets[3:6, :, None]
    dist_sq = lax.optimization_barrier(jnp.sum(separation * separation, axis=0)) + 0.0
    return (separation, relative, dist_sq)

def listed_sum(targets, listed, in_list, softening):
    separation, relative, dist_sq = listed_terms(targets, listed, in_list)
    inverse = 1.0 / (dist_sq + softening)
    strength = jnp.where(in_list, listed[6], 0.0) * inverse * jnp.sqrt(inverse)
    radial = 3.0 * lax.optimization_barrier(jnp.sum(separation * relative, axis=0)) * inverse
    accel_sum = lax.optimization_barrier(jnp.sum(strength[None] * separation, axis=2))
    jerk_sum = lax.optimization_barrier(jnp.sum(strength[None] * (relative - radial[None] * separation), axis=2))
    return jnp.concatenate([accel_sum, jerk_sum], axis=0)

def correct(own_rows, total_force, irregular):
    step_size = own_rows[12][None, :]
    change = total_force[0:3] - own_rows[6:9]
    second = 3.0 * change - step_size * (2.0 * own_rows[9:12] + total_force[3:6])
    third = -2.0 * change + step_size * (own_rows[9:12] + total_force[3:6])
    position = own_rows[0:3] + step_size * step_size * (second / 12.0 + third / 20.0)
    velocity = own_rows[3:6] + step_size * (second / 3.0 + third / 4.0)
    forces = jnp.concatenate([irregular, total_force - irregular], axis=0)
    return (jnp.concatenate([position, velocity], axis=0), forces, jnp.concatenate([second, third], axis=0))

def regular_sum(targets, predicted, softening):
    active_count = targets.shape[1]
    star_count = predicted.shape[1]
    target_block = math.gcd(active_count, 256)
    source_block = math.gcd(star_count, 8192)

    def per_block(first_col):
        chosen = lax.dynamic_slice_in_dim(targets, first_col, target_block, 1)

        def add_sources(block_index, running):
            sources = lax.dynamic_slice_in_dim(predicted, block_index * source_block, source_block, 1)
            return running + pair_terms(chosen, sources, softening)
        return lax.fori_loop(0, star_count // source_block, add_sources, jnp.zeros((6, target_block), jnp.float32))
    block_starts = (jnp.arange(active_count // target_block) * target_block).astype(jnp.int32)
    results = lax.map(per_block, block_starts)
    return jnp.transpose(results, (1, 0, 2)).reshape(6, active_count)

def reference(star_state, old_force, star_mass, elapsed, active_ids, neighbours, list_length):
    star_count = star_state.shape[1]
    listed_count = neighbours.shape[1]
    softening = 0.25 * math.sqrt(listed_count) / star_count
    predicted = predict(star_state, old_force, star_mass, elapsed)
    carried = jnp.concatenate([predicted[0:6], old_force, elapsed[None, :]], axis=0)
    own_rows = carried[:, active_ids]
    targets = own_rows[0:6]
    total_force = regular_sum(targets, predicted, softening)
    listed = predicted[:, neighbours]
    in_list = jnp.arange(listed_count)[None, :] < list_length[:, None]
    irregular = listed_sum(targets, listed, in_list, softening)
    return correct(own_rows, total_force, irregular)
```

```python
import functools
import math

import jax
import jax.numpy as jnp
from jax import lax
from jax.experimental import pallas as pl
from jax.experimental.pallas import tpu as pltpu
from jax.sharding import PartitionSpec as P

LANES = 128
F32 = jnp.float32
I32 = jnp.int32
BF16 = jnp.bfloat16
VMEM = pl.BlockSpec(memory_space=pltpu.VMEM)
SMEM = pl.BlockSpec(memory_space=pltpu.SMEM)
PARAMS = pltpu.CompilerParams(vmem_limit_bytes=32 * 1024 * 1024)


def iota(shape, axis):
    return lax.broadcasted_iota(I32, shape, axis)


def split3(value):
    high = value.astype(BF16)
    rest = value - high.astype(F32)
    middle = rest.astype(BF16)
    low = (rest - middle.astype(F32)).astype(BF16)
    return jnp.concatenate([high, middle, low], axis=1)


def pick(table_ref, low, high, rows):
    count = low.shape[1]
    hot = jnp.where(iota((LANES, count), 0) == low, 1.0, 0.0).astype(BF16)
    found = jnp.dot(table_ref[...], jnp.concatenate([hot] * 3, axis=0), preferred_element_type=F32)
    total = jnp.zeros((rows, count), F32)
    for block in range(table_ref.shape[0] // rows):
        total += jnp.where(high == block, found[block * rows : (block + 1) * rows], 0.0)
    return total


def request_kernel(stars_dev, cap, active_ref, length_ref, listed_ref, out_ref):
    devices = out_ref.shape[0]
    targets, slots = listed_ref.shape
    listed = listed_ref[...]
    owner = listed // stars_dev if stars_dev & (stars_dev - 1) else lax.shift_right_logical(listed, stars_dev.bit_length() - 1)
    local = listed - owner * stars_dev
    low = (local & (LANES - 1)).astype(F32)
    high = lax.shift_right_logical(local, 7).astype(F32)
    lane = iota((devices, LANES), 1)
    row = iota((devices, LANES), 0)
    before = jnp.where(iota((slots, 2 * LANES), 0) < iota((slots, 2 * LANES), 1), 1.0, 0.0).astype(BF16)
    mine = [
        jnp.where((owner[k : k + 1] == row) & (lane < length_ref[k]), 1.0, 0.0) for k in range(targets)
    ]
    counts = jnp.dot(jnp.concatenate(mine, axis=0).astype(BF16), before, preferred_element_type=F32)
    base = jnp.zeros((devices, LANES), F32)
    order = iota((LANES, slots), 0).astype(F32)
    lows, highs, hots, bases = [], [], [], [base]
    for k in range(targets):
        ahead = counts[k * devices : (k + 1) * devices]
        rank = jnp.sum(mine[k] * (ahead[:, :LANES] + base), axis=0, keepdims=True)
        hots.append(jnp.where(order == rank, 1.0, 0.0).astype(BF16))
        lows.append((mine[k] * low[k : k + 1]).astype(BF16))
        highs.append((mine[k] * high[k : k + 1]).astype(BF16))
        base = base + ahead[:, LANES:]
        bases.append(base)
    planes = jnp.concatenate([jnp.concatenate(lows, axis=1), jnp.concatenate(highs, axis=1)], axis=0)
    placed = lax.dot_general(
        planes, jnp.concatenate(hots, axis=1), (((1,), (1,)), ((), ())), preferred_element_type=F32
    )
    result = (placed[:devices] + LANES * placed[devices:]).astype(I32)
    for k in range(targets + 1):
        result = jnp.where(lane == cap + k, bases[k].astype(I32), result)
    for k in range(targets):
        result = jnp.where(lane == cap + targets + 1 + k, active_ref[k], result)
    out_ref[...] = result


def predict_kernel(state_ref, force_ref, mass_ref, elapsed_ref, predicted_ref, own_table_ref, star_table_ref):
    for block in range(mass_ref.shape[0]):
        cols = slice(block * LANES, (block + 1) * LANES)
        state, force = state_ref[:, cols], force_ref[:, cols]
        step = elapsed_ref[block : block + 1]
        accel, jerk = force[0:3], force[3:6]
        position = state[0:3] + step * (state[3:6] + step * (0.5 * accel + step * jerk / 6.0))
        velocity = state[3:6] + step * (accel + 0.5 * step * jerk)
        stars = jnp.concatenate([position, velocity, mass_ref[block : block + 1], step], axis=0)
        predicted_ref[:, cols] = stars
        rows = jnp.concatenate([stars, force, jnp.zeros((2, LANES), F32)], axis=0)
        own_table_ref[block * 16 : (block + 1) * 16] = split3(rows)
        star_table_ref[block * 8 : (block + 1) * 8] = split3(stars)


def own_kernel(stars_dev, cap, targets, request_ref, table_ref, own_ref, out_ref):
    devices = request_ref.shape[0]
    first = cap + targets + 1
    lane = iota((devices, LANES), 1)
    ids = pltpu.roll(request_ref[...].astype(F32), LANES - first, 1)
    ids = jnp.where(lane < targets, ids, 0.0)
    width = targets
    while width < LANES:
        ids = ids + pltpu.roll(ids, width, 1)
        width *= 2
    per_tile = LANES // targets
    lane, row = iota((per_tile, LANES), 1), iota((per_tile, LANES), 0)
    on_row = (lane >= row * targets) & (lane < (row + 1) * targets)
    tiles = devices // per_tile
    flat = [
        jnp.sum(jnp.where(on_row, ids[t * per_tile : (t + 1) * per_tile], 0.0), axis=0, keepdims=True)
        for t in range(tiles)
    ]
    local = jnp.concatenate(flat, axis=1).astype(I32) - lax.axis_index("stars") * stars_dev
    inside = (local >= 0) & (local < stars_dev)
    low = jnp.where(inside, local & (LANES - 1), -1)
    own = pick(table_ref, low, lax.shift_right_logical(local, 7), 16)
    own_ref[...] = own
    block = jnp.concatenate([own[0:6, t * LANES : (t + 1) * LANES] for t in range(tiles)], axis=0)
    height = math.lcm(block.shape[0], 8)
    block = jnp.concatenate([block] * (height // block.shape[0]), axis=0)
    for i in range(out_ref.shape[0] // height):
        out_ref[i * height : (i + 1) * height] = block


def listed_kernel(cap, targets, request_ref, table_ref, own_ref, listed_ref, slot_ref, back_ref):
    devices = request_ref.shape[0]
    request = request_ref[...]
    lane = iota((devices, LANES), 1)
    slot = jnp.zeros((devices, LANES), I32)
    for k in range(targets):
        slot += jnp.where(lane >= request[:, cap + k + 1 : cap + k + 2], 1, 0)
    per_row = LANES // cap
    rows = devices // per_row
    lane = iota((rows, LANES), 1)
    ids, slots = request[:rows], slot[:rows]
    for j in range(1, per_row):
        here = lane >= j * cap
        part = slice(j * rows, (j + 1) * rows)
        ids = jnp.where(here, pltpu.roll(request[part], j * cap, 1), ids)
        slots = jnp.where(here, pltpu.roll(slot[part], j * cap, 1), slots)
    slot_ref[...] = slots
    low, high = ids & (LANES - 1), lax.shift_right_logical(ids, 7)
    for pair in range(rows // 2):
        halves = [slice(2 * pair + i, 2 * pair + i + 1) for i in range(2)]
        found = pick(
            table_ref,
            jnp.concatenate([low[half] for half in halves], axis=1),
            jnp.concatenate([high[half] for half in halves], axis=1),
            8,
        )
        for i in range(2):
            listed_ref[(2 * pair + i) * 8 : (2 * pair + i + 1) * 8] = found[:, i * LANES : (i + 1) * LANES]
    own = own_ref[...]
    per_tile = LANES // targets
    lane, row = iota((per_tile, LANES), 1), iota((per_tile, LANES), 0)
    on_row = (lane >= row * targets) & (lane < (row + 1) * targets)
    same = jnp.where(iota((LANES, LANES), 0) % targets == iota((LANES, LANES), 1) % targets, 1.0, 0.0).astype(BF16)
    same = jnp.concatenate([same] * 3, axis=0)
    for t in range(devices // per_tile):
        tile = own[:, t * LANES : (t + 1) * LANES]
        spread = jnp.concatenate([jnp.where(on_row, tile[c : c + 1], 0.0) for c in range(16)], axis=0)
        folded = jnp.dot(split3(spread), same, preferred_element_type=F32)
        back = jnp.zeros((per_tile, LANES), F32)
        for c in range(LANES // targets):
            here = (lane >= c * targets) & (lane < (c + 1) * targets)
            back = jnp.where(here, folded[c * per_tile : (c + 1) * per_tile], back)
        back_ref[t * per_tile : (t + 1) * per_tile] = back


def pair_sums(target, source, mass, softening, sums):
    x, y, z = (source[c] - target[c] for c in range(3))
    u, v, w = (source[c] - target[c] for c in range(3, 6))
    inverse = lax.rsqrt(x * x + y * y + z * z + softening)
    square = inverse * inverse
    strength = mass * inverse * square
    radial = (x * u + y * v + z * w) * (strength * square)
    return (
        sums[0] + strength * x,
        sums[1] + strength * y,
        sums[2] + strength * z,
        sums[3] + strength * u,
        sums[4] + strength * v,
        sums[5] + strength * w,
        sums[6] + radial * x,
        sums[7] + radial * y,
        sums[8] + radial * z,
    )


def force_kernel(
    softening, cap, targets, group_step, source_step,
    sent_ref, predicted_ref, listed_ref, slot_ref, back_ref, out_ref, target_ref, source_ref,
):
    devices = back_ref.shape[0]
    rows = sent_ref.shape[0] // devices
    height = math.lcm(rows, 8)
    sent = sent_ref[0:height]
    for i in range(1, sent_ref.shape[0] // height):
        sent = sent + sent_ref[i * height : (i + 1) * height]
    block = sent[0:rows]
    for i in range(1, height // rows):
        block = block + sent[i * rows : (i + 1) * rows]
    for t in range(rows // 6):
        tile = jnp.concatenate([block[t * 6 : (t + 1) * 6], jnp.zeros((2, LANES), F32)], axis=0)
        target_ref[t * LANES : (t + 1) * LANES, 0:8] = tile.T
    blocks = predicted_ref.shape[1] // LANES
    for s in range(blocks):
        tile = predicted_ref[:, s * LANES : (s + 1) * LANES]
        for c in range(7):
            source_ref[s, c] = jnp.broadcast_to(tile[c : c + 1], (8, LANES))
    lane, row = iota((8, LANES), 1), iota((8, LANES), 0)
    zero = jnp.zeros((8, LANES), F32)

    def finish(sums):
        return [*sums[0:3], *(sums[3 + c] - 3.0 * sums[6 + c] for c in range(3))]

    def add_groups(step, _):
        groups = [step * group_step + i for i in range(group_step)]
        held = []
        for group in groups:
            tile = target_ref[pl.ds(pl.multiple_of(group * 8, 8), 8), 0:8]
            held.append([jnp.broadcast_to(tile[:, c : c + 1], (8, LANES)) for c in range(6)])

        def add_sources(block_step, sums):
            for i in range(source_step):
                source = [source_ref[block_step * source_step + i, c] for c in range(7)]
                sums = tuple(
                    pair_sums(held[n], source, source[6], softening, sums[n]) for n in range(group_step)
                )
            return sums

        sums = lax.fori_loop(0, blocks // source_step, add_sources, tuple((zero,) * 9 for _ in groups))
        for n, group in enumerate(groups):
            packed = lax.rem(group, slot_ref.shape[0])
            part = lax.div(group, slot_ref.shape[0])
            near = listed_ref[pl.ds(pl.multiple_of(packed * 8, 8), 8), :]
            slot = slot_ref[pl.ds(packed, 1), :]
            here = (slot == row) & (lane >= part * cap) & (lane < (part + 1) * cap)
            mass = jnp.where(here, near[6:7], 0.0)
            irregular = pair_sums(held[n], [near[c : c + 1] for c in range(6)], mass, softening, (zero,) * 9)
            result = zero
            for c, values in enumerate(finish(sums[n]) + finish(irregular)):
                result = jnp.where(lane == c * targets + row, jnp.sum(values, axis=1, keepdims=True), result)
            out_ref[pl.ds(2 * group, 1), :] = jnp.sum(result, axis=0, keepdims=True)
            out_ref[pl.ds(2 * group + 1, 1), :] = back_ref[pl.ds(group, 1), :]
        return 0

    lax.fori_loop(0, devices // group_step, add_groups, 0)


def correct_kernel(targets, sums_ref, state_ref, forces_ref, terms_ref):
    total = sums_ref[0:8]
    for i in range(1, sums_ref.shape[0] // 8):
        total = total + sums_ref[i * 8 : (i + 1) * 8]
    pair = total[0:2] + total[2:4] + total[4:6] + total[6:8]

    def rows(which, first, count):
        return jnp.concatenate(
            [pair[which : which + 1, c * targets : (c + 1) * targets] for c in range(first, first + count)], axis=0
        )

    accel, jerk, irregular = rows(0, 0, 3), rows(0, 3, 3), rows(0, 6, 6)
    position, velocity, step = rows(1, 0, 3), rows(1, 3, 3), rows(1, 7, 1)
    old_accel, old_jerk = rows(1, 8, 3), rows(1, 11, 3)
    change = accel - old_accel
    second = 3.0 * change - step * (2.0 * old_jerk + jerk)
    third = -2.0 * change + step * (old_jerk + jerk)
    state_ref[0:3] = position + step * step * (second / 12.0 + third / 20.0)
    state_ref[3:6] = velocity + step * (second / 3.0 + third / 4.0)
    forces_ref[0:6] = irregular
    forces_ref[6:9] = accel - irregular[0:3]
    forces_ref[9:12] = jerk - irregular[3:6]
    terms_ref[0:3] = second
    terms_ref[3:6] = third


def exchange(rows, devices):
    wide = rows.reshape(devices, 1, -1)
    return lax.all_to_all(wide, "stars", 0, 0, tiled=True).reshape(rows.shape)


def per_device(star_state, old_force, star_mass, elapsed, active_ids, neighbours, list_length):
    stars_dev = star_state.shape[1]
    devices = lax.axis_size("stars")
    targets, slots = neighbours.shape
    active = devices * targets
    cap = 2 * targets * slots // devices
    blocks = stars_dev // LANES
    packed = devices * cap // LANES
    softening = 0.25 * math.sqrt(slots) / (stars_dev * devices)

    def shape(*dims, dtype=F32):
        return jax.ShapeDtypeStruct(dims, dtype)

    def cost(flops):
        return pl.CostEstimate(flops=flops, bytes_accessed=1 << 20, transcendentals=0)

    request = pl.pallas_call(
        functools.partial(request_kernel, stars_dev, cap),
        out_shape=shape(devices, LANES, dtype=I32),
        in_specs=[SMEM, SMEM, VMEM],
        out_specs=VMEM,
        compiler_params=PARAMS,
    )(active_ids, list_length, neighbours)
    request = exchange(request, devices)
    predicted, own_table, star_table = pl.pallas_call(
        predict_kernel,
        out_shape=(
            shape(8, stars_dev),
            shape(blocks * 16, 3 * LANES, dtype=BF16),
            shape(blocks * 8, 3 * LANES, dtype=BF16),
        ),
        in_specs=[VMEM] * 4,
        out_specs=(VMEM,) * 3,
        compiler_params=PARAMS,
        cost_estimate=cost(1 << 20),
    )(star_state, old_force, star_mass.reshape(blocks, LANES), elapsed.reshape(blocks, LANES))
    own, sent = pl.pallas_call(
        functools.partial(own_kernel, stars_dev, cap, targets),
        out_shape=(shape(16, active), shape(devices * 6 * active // LANES, LANES)),
        in_specs=[VMEM] * 2,
        out_specs=(VMEM,) * 2,
        compiler_params=PARAMS,
    )(request, own_table)
    sent = exchange(sent, devices)
    listed, slot, back = pl.pallas_call(
        functools.partial(listed_kernel, cap, targets),
        out_shape=(shape(packed * 8, LANES), shape(packed, LANES, dtype=I32), shape(devices, LANES)),
        in_specs=[VMEM] * 3,
        out_specs=(VMEM,) * 3,
        compiler_params=PARAMS,
        cost_estimate=cost(1 << 24),
    )(request, star_table, own)
    sums = pl.pallas_call(
        functools.partial(force_kernel, softening, cap, targets, 2, 4),
        out_shape=shape(devices * 2, LANES),
        in_specs=[VMEM] * 5,
        out_specs=VMEM,
        scratch_shapes=[pltpu.VMEM((active, LANES), F32), pltpu.VMEM((blocks, 7, 8, LANES), F32)],
        compiler_params=PARAMS,
    )(sent, predicted, listed, slot, back)
    sums = exchange(sums, devices)
    return pl.pallas_call(
        functools.partial(correct_kernel, targets),
        out_shape=(shape(6, targets), shape(12, targets), shape(6, targets)),
        in_specs=[VMEM],
        out_specs=(VMEM,) * 3,
        compiler_params=PARAMS,
    )(sums)


def solution(mesh):
    placed = (
        P(None, "stars"),
        P(None, "stars"),
        P("stars"),
        P("stars"),
        P("stars"),
        P("stars", None),
        P("stars"),
    )
    return jax.shard_map(
        per_device,
        mesh=mesh,
        in_specs=placed,
        out_specs=(P(None, "stars"), P(None, "stars"), P(None, "stars")),
        check_vma=False,
    )
```

```python
import functools
import math

import jax
import jax.numpy as jnp
from jax import lax
from jax.experimental import pallas as pl
from jax.experimental.pallas import tpu as pltpu
from jax.sharding import PartitionSpec as P

LANES = 128
F32 = jnp.float32
I32 = jnp.int32
BF16 = jnp.bfloat16
VMEM = pl.BlockSpec(memory_space=pltpu.VMEM)
HBM = pl.BlockSpec(memory_space=pltpu.HBM)
PARAMS = pltpu.CompilerParams(vmem_limit_bytes=32 * 1024 * 1024)


def iota(shape, axis):
    return lax.broadcasted_iota(I32, shape, axis)


def split3(value):
    high = value.astype(BF16)
    rest = value - high.astype(F32)
    middle = rest.astype(BF16)
    low = (rest - middle.astype(F32)).astype(BF16)
    return jnp.concatenate([high, middle, low], axis=1)


def folding(targets):
    same = iota((LANES, LANES), 0) % targets == iota((LANES, LANES), 1) % targets
    return jnp.concatenate([jnp.where(same, 1.0, 0.0).astype(BF16)] * 3, axis=0)


def pick(table_ref, column):
    count = column.shape[1]
    low = jnp.where(column < 0, -1, column & (LANES - 1))
    high = lax.shift_right_logical(column, 7)
    hot = jnp.where(iota((LANES, count), 0) == low, 1.0, 0.0).astype(BF16)
    found = jnp.dot(table_ref[...], jnp.concatenate([hot] * 3, axis=0), preferred_element_type=F32)
    total = jnp.zeros((8, count), F32)
    for block in range(table_ref.shape[0] // 8):
        total += jnp.where(high == block, found[block * 8 : (block + 1) * 8], 0.0)
    return total


def request_kernel(
    stars_dev, cap, active_hbm, length_hbm, listed_hbm, out_ref, active_ref, length_ref, listed_ref, sems
):
    pairs = ((listed_hbm, listed_ref), (length_hbm, length_ref), (active_hbm, active_ref))
    copies = [pltpu.make_async_copy(*pair, sems.at[i]) for i, pair in enumerate(pairs)]
    for copy in copies:
        copy.start()
    for copy in copies:
        copy.wait()
    devices = out_ref.shape[0]
    targets, slots = listed_ref.shape
    listed = listed_ref[...]
    owner = listed // stars_dev if stars_dev & (stars_dev - 1) else lax.shift_right_logical(listed, stars_dev.bit_length() - 1)
    local = listed - owner * stars_dev
    low = (local & (LANES - 1)).astype(F32)
    high = lax.shift_right_logical(local, 7).astype(F32)
    lane = iota((devices, LANES), 1)
    row = iota((devices, LANES), 0)
    before = jnp.where(iota((slots, 2 * LANES), 0) < iota((slots, 2 * LANES), 1), 1.0, 0.0).astype(BF16)
    mine = [
        jnp.where((owner[k : k + 1] == row) & (lane < length_ref[k]), 1.0, 0.0) for k in range(targets)
    ]
    counts = jnp.dot(jnp.concatenate(mine, axis=0).astype(BF16), before, preferred_element_type=F32)
    base = jnp.zeros((devices, LANES), F32)
    order = iota((LANES, slots), 0).astype(F32)
    lows, highs, hots, bases = [], [], [], [base]
    for k in range(targets):
        ahead = counts[k * devices : (k + 1) * devices]
        rank = jnp.sum(mine[k] * (ahead[:, :LANES] + base), axis=0, keepdims=True)
        hots.append(jnp.where(order == rank, 1.0, 0.0).astype(BF16))
        lows.append((mine[k] * low[k : k + 1]).astype(BF16))
        highs.append((mine[k] * high[k : k + 1]).astype(BF16))
        base = base + ahead[:, LANES:]
        bases.append(base)
    planes = jnp.concatenate([jnp.concatenate(lows, axis=1), jnp.concatenate(highs, axis=1)], axis=0)
    placed = lax.dot_general(
        planes, jnp.concatenate(hots, axis=1), (((1,), (1,)), ((), ())), preferred_element_type=F32
    )
    result = (placed[:devices] + LANES * placed[devices:]).astype(I32)
    for k in range(targets + 1):
        result = jnp.where(lane == cap + k, bases[k].astype(I32), result)
    for k in range(targets):
        result = jnp.where(lane == cap + targets + 1 + k, active_ref[k], result)
    out_ref[...] = result


def predict_kernel(state_ref, force_ref, mass_ref, elapsed_ref, source_ref, star_table_ref, force_table_ref):
    for block in range(mass_ref.shape[0]):
        cols = slice(block * LANES, (block + 1) * LANES)
        state, force = state_ref[:, cols], force_ref[:, cols]
        step = elapsed_ref[block : block + 1]
        accel, jerk = force[0:3], force[3:6]
        position = state[0:3] + step * (state[3:6] + step * (0.5 * accel + step * jerk / 6.0))
        velocity = state[3:6] + step * (accel + 0.5 * step * jerk)
        stars = jnp.concatenate([position, velocity, mass_ref[block : block + 1], step], axis=0)
        for c in range(7):
            source_ref[block, c] = jnp.broadcast_to(stars[c : c + 1], (8, LANES))
        rows = slice(block * 8, (block + 1) * 8)
        star_table_ref[rows] = split3(stars)
        force_table_ref[rows] = split3(jnp.concatenate([force, jnp.zeros((2, LANES), F32)], axis=0))


def own_kernel(stars_dev, cap, targets, request_ref, table_ref, own_ref, local_ref, out_ref):
    devices = request_ref.shape[0]
    first = cap + targets + 1
    lane = iota((devices, LANES), 1)
    ids = pltpu.roll(request_ref[...].astype(F32), LANES - first, 1)
    ids = jnp.where(lane < targets, ids, 0.0)
    width = targets
    while width < LANES:
        ids = ids + pltpu.roll(ids, width, 1)
        width *= 2
    per_tile = LANES // targets
    lane, row = iota((per_tile, LANES), 1), iota((per_tile, LANES), 0)
    on_row = (lane >= row * targets) & (lane < (row + 1) * targets)
    tiles = devices // per_tile
    flat = [
        jnp.sum(jnp.where(on_row, ids[t * per_tile : (t + 1) * per_tile], 0.0), axis=0, keepdims=True)
        for t in range(tiles)
    ]
    local = jnp.concatenate(flat, axis=1).astype(I32) - lax.axis_index("stars") * stars_dev
    local = jnp.where((local >= 0) & (local < stars_dev), local, -1)
    local_ref[...] = jnp.broadcast_to(local, local_ref.shape)
    own = pick(table_ref, local)
    own_ref[...] = own
    block = jnp.concatenate([own[0:6, t * LANES : (t + 1) * LANES] for t in range(tiles)], axis=0)
    height = math.lcm(block.shape[0], 8)
    block = jnp.concatenate([block] * (height // block.shape[0]), axis=0)
    for i in range(out_ref.shape[0] // height):
        out_ref[i * height : (i + 1) * height] = block


def listed_kernel(
    cap, targets, request_ref, star_table_ref, force_table_ref, own_ref, local_ref, listed_ref, slot_ref, back_ref
):
    devices = request_ref.shape[0]
    request = request_ref[...]
    lane = iota((devices, LANES), 1)
    slot = jnp.zeros((devices, LANES), I32)
    for k in range(targets):
        slot += jnp.where(lane >= request[:, cap + k + 1 : cap + k + 2], 1, 0)
    per_row = LANES // cap
    rows = devices // per_row
    lane = iota((rows, LANES), 1)
    ids, slots = request[:rows], slot[:rows]
    for j in range(1, per_row):
        here = lane >= j * cap
        part = slice(j * rows, (j + 1) * rows)
        ids = jnp.where(here, pltpu.roll(request[part], j * cap, 1), ids)
        slots = jnp.where(here, pltpu.roll(slot[part], j * cap, 1), slots)
    slot_ref[...] = slots
    for pair in range(rows // 2):
        halves = [2 * pair, 2 * pair + 1]
        found = pick(star_table_ref, jnp.concatenate([ids[half : half + 1] for half in halves], axis=1))
        for i, half in enumerate(halves):
            listed_ref[half * 8 : (half + 1) * 8] = found[:, i * LANES : (i + 1) * LANES]
    own = jnp.concatenate([own_ref[...], pick(force_table_ref, local_ref[0:1])], axis=0)
    per_tile = LANES // targets
    lane, row = iota((per_tile, LANES), 1), iota((per_tile, LANES), 0)
    on_row = (lane >= row * targets) & (lane < (row + 1) * targets)
    fold = folding(targets)
    for t in range(devices // per_tile):
        tile = own[:, t * LANES : (t + 1) * LANES]
        spread = jnp.concatenate([jnp.where(on_row, tile[c : c + 1], 0.0) for c in range(16)], axis=0)
        folded = jnp.dot(split3(spread), fold, preferred_element_type=F32)
        back = jnp.zeros((per_tile, LANES), F32)
        for c in range(LANES // targets):
            here = (lane >= c * targets) & (lane < (c + 1) * targets)
            back = jnp.where(here, folded[c * per_tile : (c + 1) * per_tile], back)
        back_ref[t * per_tile : (t + 1) * per_tile] = back


def pair_sums(target, source, mass, softening, sums):
    x, y, z = (source[c] - target[c] for c in range(3))
    u, v, w = (source[c] - target[c] for c in range(3, 6))
    inverse = lax.rsqrt(x * x + y * y + z * z + softening)
    square = inverse * inverse
    strength = mass * inverse * square
    radial = (x * u + y * v + z * w) * (3.0 * square)
    return (
        sums[0] + strength * x,
        sums[1] + strength * y,
        sums[2] + strength * z,
        sums[3] + strength * (u - radial * x),
        sums[4] + strength * (v - radial * y),
        sums[5] + strength * (w - radial * z),
    )


def force_kernel(
    softening, cap, targets, group_step, source_step, sum_step,
    sent_ref, source_ref, listed_ref, slot_ref, back_ref, out_ref, target_ref, sums_ref,
):
    devices = back_ref.shape[0]
    rows = sent_ref.shape[0] // devices
    height = math.lcm(rows, 8)
    sent = sent_ref[0:height]
    for i in range(1, sent_ref.shape[0] // height):
        sent = sent + sent_ref[i * height : (i + 1) * height]
    block = sent[0:rows]
    for i in range(1, height // rows):
        block = block + sent[i * rows : (i + 1) * rows]
    for t in range(rows // 6):
        tile = jnp.concatenate([block[t * 6 : (t + 1) * 6], jnp.zeros((2, LANES), F32)], axis=0)
        target_ref[t * LANES : (t + 1) * LANES, 0:8] = tile.T
    blocks = source_ref.shape[0]
    lane, row = iota((8, LANES), 1), iota((8, LANES), 0)
    zeros = (jnp.zeros((8, LANES), F32),) * 6

    def add_groups(step, _):
        groups = [step * group_step + i for i in range(group_step)]
        held = []
        for group in groups:
            tile = target_ref[pl.ds(pl.multiple_of(group * 8, 8), 8), 0:8]
            held.append([jnp.broadcast_to(tile[:, c : c + 1], (8, LANES)) for c in range(6)])

        def add_sources(block_step, sums):
            for i in range(source_step):
                source = [source_ref[block_step * source_step + i, c] for c in range(7)]
                sums = tuple(
                    pair_sums(held[n], source, source[6], softening, sums[n]) for n in range(group_step)
                )
            return sums

        sums = lax.fori_loop(0, blocks // source_step, add_sources, (zeros,) * group_step)
        for n, group in enumerate(groups):
            packed = lax.rem(group, slot_ref.shape[0])
            part = lax.div(group, slot_ref.shape[0])
            near = listed_ref[pl.ds(pl.multiple_of(packed * 8, 8), 8), :]
            slot = slot_ref[pl.ds(packed, 1), :]
            here = (slot == row) & (lane >= part * cap) & (lane < (part + 1) * cap)
            mass = jnp.where(here, near[6:7], 0.0)
            irregular = pair_sums(held[n], [near[c : c + 1] for c in range(6)], mass, softening, zeros)
            for c, values in enumerate(sums[n] + irregular):
                sums_ref[group, c] = values
        return 0

    lax.fori_loop(0, devices // group_step, add_groups, 0)

    def add_lanes(step, _):
        for i in range(sum_step):
            group = step * sum_step + i
            result = zeros[0]
            for c in range(12):
                value = jnp.sum(sums_ref[group, c], axis=1, keepdims=True)
                result = jnp.where(lane == c * targets + row, value, result)
            out_ref[pl.ds(2 * group, 1), :] = jnp.sum(result, axis=0, keepdims=True)
            out_ref[pl.ds(2 * group + 1, 1), :] = back_ref[pl.ds(group, 1), :]
        return 0

    lax.fori_loop(0, devices // sum_step, add_lanes, 0)


def correct_kernel(targets, sums_ref, state_ref, forces_ref, terms_ref):
    total = sums_ref[0:8]
    for i in range(1, sums_ref.shape[0] // 8):
        total = total + sums_ref[i * 8 : (i + 1) * 8]
    pair = total[0:2] + total[2:4] + total[4:6] + total[6:8]
    lane, row = iota((16, LANES), 1), iota((16, LANES), 0)
    on_row = (lane >= row * targets) & (lane < (row + 1) * targets)
    spread = jnp.concatenate([jnp.where(on_row, pair[i : i + 1], 0.0) for i in range(2)], axis=0)
    rows = jnp.dot(split3(spread), folding(targets), preferred_element_type=F32)[:, 0:targets]
    accel, jerk, irregular = rows[0:3], rows[3:6], rows[6:12]
    position, velocity, step = rows[16:19], rows[19:22], rows[23:24]
    old_accel, old_jerk = rows[24:27], rows[27:30]
    change = accel - old_accel
    second = 3.0 * change - step * (2.0 * old_jerk + jerk)
    third = -2.0 * change + step * (old_jerk + jerk)
    state_ref[0:3] = position + step * step * (second / 12.0 + third / 20.0)
    state_ref[3:6] = velocity + step * (second / 3.0 + third / 4.0)
    forces = jnp.concatenate([irregular, rows[0:6] - irregular, jnp.zeros((4, targets), F32)], axis=0)
    forces_ref[...] = forces.T[:, 0:12]
    terms_ref[0:3] = second
    terms_ref[3:6] = third


def exchange(rows, devices):
    wide = rows.reshape(devices, 1, -1)
    return lax.all_to_all(wide, "stars", 0, 0, tiled=True).reshape(rows.shape)


def per_device(star_state, old_force, star_mass, elapsed, active_ids, neighbours, list_length):
    stars_dev = star_state.shape[1]
    devices = lax.axis_size("stars")
    targets, slots = neighbours.shape
    active = devices * targets
    cap = 2 * targets * slots // devices
    blocks = stars_dev // LANES
    packed = devices * cap // LANES
    softening = 0.25 * math.sqrt(slots) / (stars_dev * devices)

    def shape(*dims, dtype=F32):
        return jax.ShapeDtypeStruct(dims, dtype)

    def cost(flops):
        return pl.CostEstimate(flops=flops, bytes_accessed=1 << 20, transcendentals=0)

    request = pl.pallas_call(
        functools.partial(request_kernel, stars_dev, cap),
        out_shape=shape(devices, LANES, dtype=I32),
        in_specs=[HBM] * 3,
        out_specs=VMEM,
        scratch_shapes=[
            pltpu.SMEM((targets,), I32),
            pltpu.SMEM((targets,), I32),
            pltpu.VMEM((targets, slots), I32),
            pltpu.SemaphoreType.DMA((3,)),
        ],
        compiler_params=PARAMS,
    )(active_ids, list_length, neighbours)
    request = exchange(request, devices)
    source, star_table, force_table = pl.pallas_call(
        predict_kernel,
        out_shape=(
            shape(blocks, 7, 8, LANES),
            shape(blocks * 8, 3 * LANES, dtype=BF16),
            shape(blocks * 8, 3 * LANES, dtype=BF16),
        ),
        in_specs=[VMEM] * 4,
        out_specs=(VMEM,) * 3,
        compiler_params=PARAMS,
        cost_estimate=cost(1 << 20),
    )(star_state, old_force, star_mass.reshape(blocks, LANES), elapsed.reshape(blocks, LANES))
    own, local, sent = pl.pallas_call(
        functools.partial(own_kernel, stars_dev, cap, targets),
        out_shape=(shape(8, active), shape(8, active, dtype=I32), shape(devices * 6 * active // LANES, LANES)),
        in_specs=[VMEM] * 2,
        out_specs=(VMEM,) * 3,
        compiler_params=PARAMS,
    )(request, star_table)
    sent = exchange(sent, devices)
    listed, slot, back = pl.pallas_call(
        functools.partial(listed_kernel, cap, targets),
        out_shape=(shape(packed * 8, LANES), shape(packed, LANES, dtype=I32), shape(devices, LANES)),
        in_specs=[VMEM] * 5,
        out_specs=(VMEM,) * 3,
        compiler_params=PARAMS,
        cost_estimate=cost(1 << 24),
    )(request, star_table, force_table, own, local)
    sums = pl.pallas_call(
        functools.partial(force_kernel, softening, cap, targets, 4, 32, 16),
        out_shape=shape(devices * 2, LANES),
        in_specs=[VMEM] * 5,
        out_specs=VMEM,
        scratch_shapes=[pltpu.VMEM((active, LANES), F32), pltpu.VMEM((devices, 12, 8, LANES), F32)],
        compiler_params=PARAMS,
    )(sent, source, listed, slot, back)
    sums = exchange(sums, devices)
    state, forces, terms = pl.pallas_call(
        functools.partial(correct_kernel, targets),
        out_shape=(shape(6, targets), shape(targets, 12), shape(6, targets)),
        in_specs=[VMEM],
        out_specs=(VMEM,) * 3,
        compiler_params=PARAMS,
    )(sums)
    return state, forces.T, terms


def solution(mesh):
    placed = (
        P(None, "stars"),
        P(None, "stars"),
        P("stars"),
        P("stars"),
        P("stars"),
        P("stars", None),
        P("stars"),
    )
    return jax.shard_map(
        per_device,
        mesh=mesh,
        in_specs=placed,
        out_specs=(P(None, "stars"), P(None, "stars"), P(None, "stars")),
        check_vma=False,
    )
```

```python
import functools
import math

import jax
import jax.numpy as jnp
from jax import lax
from jax.experimental import pallas as pl
from jax.experimental.pallas import tpu as pltpu
from jax.sharding import PartitionSpec as P

LANES = 128
F32 = jnp.float32
I32 = jnp.int32
BF16 = jnp.bfloat16
VMEM = pl.BlockSpec(memory_space=pltpu.VMEM)
HBM = pl.BlockSpec(memory_space=pltpu.HBM)
PARAMS = pltpu.CompilerParams(vmem_limit_bytes=32 * 1024 * 1024)


def iota(shape, axis):
    return lax.broadcasted_iota(I32, shape, axis)


def split3(value):
    high = value.astype(BF16)
    rest = value - high.astype(F32)
    middle = rest.astype(BF16)
    low = (rest - middle.astype(F32)).astype(BF16)
    return jnp.concatenate([high, middle, low], axis=1)


def folding(targets):
    same = iota((LANES, LANES), 0) % targets == iota((LANES, LANES), 1) % targets
    return jnp.concatenate([jnp.where(same, 1.0, 0.0).astype(BF16)] * 3, axis=0)


def pick(table_ref, column):
    count = column.shape[1]
    low = jnp.where(column < 0, -1, column & (LANES - 1))
    high = lax.shift_right_logical(column, 7)
    hot = jnp.where(iota((LANES, count), 0) == low, 1.0, 0.0).astype(BF16)
    found = jnp.dot(table_ref[...], jnp.concatenate([hot] * 3, axis=0), preferred_element_type=F32)
    total = jnp.zeros((8, count), F32)
    for block in range(table_ref.shape[0] // 8):
        total += jnp.where(high == block, found[block * 8 : (block + 1) * 8], 0.0)
    return total


def request_kernel(
    stars_dev, cap, active_hbm, length_hbm, listed_hbm, out_ref, active_ref, length_ref, listed_ref, sems
):
    pairs = ((listed_hbm, listed_ref), (length_hbm, length_ref), (active_hbm, active_ref))
    copies = [pltpu.make_async_copy(*pair, sems.at[i]) for i, pair in enumerate(pairs)]
    for copy in copies:
        copy.start()
    for copy in copies:
        copy.wait()
    devices = out_ref.shape[0]
    targets, slots = listed_ref.shape
    listed = listed_ref[...]
    owner = listed // stars_dev if stars_dev & (stars_dev - 1) else lax.shift_right_logical(listed, stars_dev.bit_length() - 1)
    local = listed - owner * stars_dev
    low = (local & (LANES - 1)).astype(F32)
    high = lax.shift_right_logical(local, 7).astype(F32)
    lane = iota((devices, LANES), 1)
    row = iota((devices, LANES), 0)
    before = jnp.where(iota((slots, 2 * LANES), 0) < iota((slots, 2 * LANES), 1), 1.0, 0.0).astype(BF16)
    mine = [
        jnp.where((owner[k : k + 1] == row) & (lane < length_ref[k]), 1.0, 0.0) for k in range(targets)
    ]
    counts = jnp.dot(jnp.concatenate(mine, axis=0).astype(BF16), before, preferred_element_type=F32)
    base = jnp.zeros((devices, LANES), F32)
    order = iota((LANES, slots), 0).astype(F32)
    lows, highs, hots, bases = [], [], [], [base]
    for k in range(targets):
        ahead = counts[k * devices : (k + 1) * devices]
        rank = jnp.sum(mine[k] * (ahead[:, :LANES] + base), axis=0, keepdims=True)
        hots.append(jnp.where(order == rank, 1.0, 0.0).astype(BF16))
        lows.append((mine[k] * low[k : k + 1]).astype(BF16))
        highs.append((mine[k] * high[k : k + 1]).astype(BF16))
        base = base + ahead[:, LANES:]
        bases.append(base)
    planes = jnp.concatenate([jnp.concatenate(lows, axis=1), jnp.concatenate(highs, axis=1)], axis=0)
    placed = lax.dot_general(
        planes, jnp.concatenate(hots, axis=1), (((1,), (1,)), ((), ())), preferred_element_type=F32
    )
    result = (placed[:devices] + LANES * placed[devices:]).astype(I32)
    for k in range(targets + 1):
        result = jnp.where(lane == cap + k, bases[k].astype(I32), result)
    for k in range(targets):
        result = jnp.where(lane == cap + targets + 1 + k, active_ref[k], result)
    out_ref[...] = result


def predict_kernel(state_ref, force_ref, mass_ref, elapsed_ref, source_ref, star_table_ref, force_table_ref):
    for block in range(mass_ref.shape[0]):
        cols = slice(block * LANES, (block + 1) * LANES)
        state, force = state_ref[:, cols], force_ref[:, cols]
        step = elapsed_ref[block : block + 1]
        accel, jerk = force[0:3], force[3:6]
        position = state[0:3] + step * (state[3:6] + step * (0.5 * accel + step * jerk / 6.0))
        velocity = state[3:6] + step * (accel + 0.5 * step * jerk)
        stars = jnp.concatenate([position, velocity, mass_ref[block : block + 1], step], axis=0)
        for c in range(7):
            source_ref[block, c] = jnp.broadcast_to(stars[c : c + 1], (8, LANES))
        rows = slice(block * 8, (block + 1) * 8)
        star_table_ref[rows] = split3(stars)
        force_table_ref[rows] = split3(jnp.concatenate([force, jnp.zeros((2, LANES), F32)], axis=0))


def own_kernel(stars_dev, cap, targets, request_ref, table_ref, own_ref, local_ref, out_ref):
    devices = request_ref.shape[0]
    first = cap + targets + 1
    lane = iota((devices, LANES), 1)
    ids = pltpu.roll(request_ref[...].astype(F32), LANES - first, 1)
    ids = jnp.where(lane < targets, ids, 0.0)
    width = targets
    while width < LANES:
        ids = ids + pltpu.roll(ids, width, 1)
        width *= 2
    per_tile = LANES // targets
    lane, row = iota((per_tile, LANES), 1), iota((per_tile, LANES), 0)
    on_row = (lane >= row * targets) & (lane < (row + 1) * targets)
    tiles = devices // per_tile
    flat = [
        jnp.sum(jnp.where(on_row, ids[t * per_tile : (t + 1) * per_tile], 0.0), axis=0, keepdims=True)
        for t in range(tiles)
    ]
    local = jnp.concatenate(flat, axis=1).astype(I32) - lax.axis_index("stars") * stars_dev
    local = jnp.where((local >= 0) & (local < stars_dev), local, -1)
    local_ref[...] = jnp.broadcast_to(local, local_ref.shape)
    own = pick(table_ref, local)
    own_ref[...] = own
    block = jnp.concatenate([own[0:6, t * LANES : (t + 1) * LANES] for t in range(tiles)], axis=0)
    height = math.lcm(block.shape[0], 8)
    block = jnp.concatenate([block] * (height // block.shape[0]), axis=0)
    for i in range(out_ref.shape[0] // height):
        out_ref[i * height : (i + 1) * height] = block


def listed_kernel(
    cap, targets, request_ref, star_table_ref, force_table_ref, own_ref, local_ref, listed_ref, slot_ref, back_ref
):
    devices = request_ref.shape[0]
    request = request_ref[...]
    lane = iota((devices, LANES), 1)
    slot = jnp.zeros((devices, LANES), I32)
    for k in range(targets):
        slot += jnp.where(lane >= request[:, cap + k + 1 : cap + k + 2], 1, 0)
    per_row = LANES // cap
    rows = devices // per_row
    lane = iota((rows, LANES), 1)
    ids, slots = request[:rows], slot[:rows]
    for j in range(1, per_row):
        here = lane >= j * cap
        part = slice(j * rows, (j + 1) * rows)
        ids = jnp.where(here, pltpu.roll(request[part], j * cap, 1), ids)
        slots = jnp.where(here, pltpu.roll(slot[part], j * cap, 1), slots)
    slot_ref[...] = slots
    for pair in range(rows // 2):
        halves = [2 * pair, 2 * pair + 1]
        found = pick(star_table_ref, jnp.concatenate([ids[half : half + 1] for half in halves], axis=1))
        for i, half in enumerate(halves):
            listed_ref[half * 8 : (half + 1) * 8] = found[:, i * LANES : (i + 1) * LANES]
    own = jnp.concatenate([own_ref[...], pick(force_table_ref, local_ref[0:1])], axis=0)
    per_tile = LANES // targets
    lane, row = iota((per_tile, LANES), 1), iota((per_tile, LANES), 0)
    on_row = (lane >= row * targets) & (lane < (row + 1) * targets)
    fold = folding(targets)
    for t in range(devices // per_tile):
        tile = own[:, t * LANES : (t + 1) * LANES]
        spread = jnp.concatenate([jnp.where(on_row, tile[c : c + 1], 0.0) for c in range(16)], axis=0)
        folded = jnp.dot(split3(spread), fold, preferred_element_type=F32)
        back = jnp.zeros((per_tile, LANES), F32)
        for c in range(LANES // targets):
            here = (lane >= c * targets) & (lane < (c + 1) * targets)
            back = jnp.where(here, folded[c * per_tile : (c + 1) * per_tile], back)
        back_ref[t * per_tile : (t + 1) * per_tile] = back


def pair_sums(target, source, mass, softening, sums):
    x, y, z = (source[c] - target[c] for c in range(3))
    u, v, w = (source[c] - target[c] for c in range(3, 6))
    inverse = lax.rsqrt(x * x + y * y + z * z + softening)
    square = inverse * inverse
    strength = mass * inverse * square
    radial = (x * u + y * v + z * w) * (3.0 * square)
    return (
        sums[0] + strength * x,
        sums[1] + strength * y,
        sums[2] + strength * z,
        sums[3] + strength * (u - radial * x),
        sums[4] + strength * (v - radial * y),
        sums[5] + strength * (w - radial * z),
    )


def force_kernel(
    softening, cap, targets, group_step, source_step, sum_step,
    sent_ref, source_ref, listed_ref, slot_ref, back_ref, out_ref, target_ref, sums_ref,
):
    devices = back_ref.shape[0]
    rows = sent_ref.shape[0] // devices
    height = math.lcm(rows, 8)
    sent = sent_ref[0:height]
    for i in range(1, sent_ref.shape[0] // height):
        sent = sent + sent_ref[i * height : (i + 1) * height]
    block = sent[0:rows]
    for i in range(1, height // rows):
        block = block + sent[i * rows : (i + 1) * rows]
    for t in range(rows // 6):
        tile = jnp.concatenate([block[t * 6 : (t + 1) * 6], jnp.zeros((2, LANES), F32)], axis=0)
        target_ref[t * LANES : (t + 1) * LANES, 0:8] = tile.T
    blocks = source_ref.shape[0]
    lane, row = iota((8, LANES), 1), iota((8, LANES), 0)
    zeros = (jnp.zeros((8, LANES), F32),) * 6

    def add_groups(step, _):
        groups = [step * group_step + i for i in range(group_step)]
        held = []
        for group in groups:
            tile = target_ref[pl.ds(pl.multiple_of(group * 8, 8), 8), 0:8]
            held.append([jnp.broadcast_to(tile[:, c : c + 1], (8, LANES)) for c in range(6)])

        def add_sources(block_step, sums):
            for i in range(source_step):
                source = [source_ref[block_step * source_step + i, c] for c in range(7)]
                sums = tuple(
                    pair_sums(held[n], source, source[6], softening, sums[n]) for n in range(group_step)
                )
            return sums

        sums = lax.fori_loop(0, blocks // source_step, add_sources, (zeros,) * group_step)
        for n, group in enumerate(groups):
            packed = lax.rem(group, slot_ref.shape[0])
            part = lax.div(group, slot_ref.shape[0])
            near = listed_ref[pl.ds(pl.multiple_of(packed * 8, 8), 8), :]
            slot = slot_ref[pl.ds(packed, 1), :]
            here = (slot == row) & (lane >= part * cap) & (lane < (part + 1) * cap)
            mass = jnp.where(here, near[6:7], 0.0)
            irregular = pair_sums(held[n], [near[c : c + 1] for c in range(6)], mass, softening, zeros)
            for c, values in enumerate(sums[n] + irregular):
                sums_ref[group, c] = values
        return 0

    lax.fori_loop(0, devices // group_step, add_groups, 0)

    def add_lanes(step, _):
        for i in range(sum_step):
            group = step * sum_step + i
            result = zeros[0]
            for c in range(12):
                value = jnp.sum(sums_ref[group, c], axis=1, keepdims=True)
                result = jnp.where(lane == c * targets + row, value, result)
            out_ref[pl.ds(2 * group, 1), :] = jnp.sum(result, axis=0, keepdims=True)
            out_ref[pl.ds(2 * group + 1, 1), :] = back_ref[pl.ds(group, 1), :]
        return 0

    lax.fori_loop(0, devices // sum_step, add_lanes, 0)


def correct_kernel(targets, sums_ref, state_ref, forces_ref, terms_ref):
    total = sums_ref[0:8]
    for i in range(1, sums_ref.shape[0] // 8):
        total = total + sums_ref[i * 8 : (i + 1) * 8]
    pair = total[0:2] + total[2:4] + total[4:6] + total[6:8]
    lane, row = iota((16, LANES), 1), iota((16, LANES), 0)
    on_row = (lane >= row * targets) & (lane < (row + 1) * targets)
    spread = jnp.concatenate([jnp.where(on_row, pair[i : i + 1], 0.0) for i in range(2)], axis=0)
    rows = jnp.dot(split3(spread), folding(targets), preferred_element_type=F32)[:, 0:targets]
    accel, jerk, irregular = rows[0:3], rows[3:6], rows[6:12]
    position, velocity, step = rows[16:19], rows[19:22], rows[23:24]
    old_accel, old_jerk = rows[24:27], rows[27:30]
    change = accel - old_accel
    second = 3.0 * change - step * (2.0 * old_jerk + jerk)
    third = -2.0 * change + step * (old_jerk + jerk)
    state_ref[0:3] = position + step * step * (second / 12.0 + third / 20.0)
    state_ref[3:6] = velocity + step * (second / 3.0 + third / 4.0)
    forces = jnp.concatenate([irregular, rows[0:6] - irregular, jnp.zeros((4, targets), F32)], axis=0)
    forces_ref[...] = forces.T[:, 0:12]
    terms_ref[0:3] = second
    terms_ref[3:6] = third


def exchange(rows, devices):
    wide = rows.reshape(devices, 1, -1)
    return lax.all_to_all(wide, "stars", 0, 0, tiled=True).reshape(rows.shape)


def per_device(star_state, old_force, star_mass, elapsed, active_ids, neighbours, list_length):
    stars_dev = star_state.shape[1]
    devices = lax.axis_size("stars")
    targets, slots = neighbours.shape
    active = devices * targets
    cap = 2 * targets * slots // devices
    blocks = stars_dev // LANES
    packed = devices * cap // LANES
    softening = 0.25 * math.sqrt(slots) / (stars_dev * devices)

    def shape(*dims, dtype=F32):
        return jax.ShapeDtypeStruct(dims, dtype)

    def cost(flops):
        return pl.CostEstimate(flops=flops, bytes_accessed=1 << 20, transcendentals=0)

    request = pl.pallas_call(
        functools.partial(request_kernel, stars_dev, cap),
        out_shape=shape(devices, LANES, dtype=I32),
        in_specs=[HBM] * 3,
        out_specs=VMEM,
        scratch_shapes=[
            pltpu.SMEM((targets,), I32),
            pltpu.SMEM((targets,), I32),
            pltpu.VMEM((targets, slots), I32),
            pltpu.SemaphoreType.DMA((3,)),
        ],

    )(active_ids, list_length, neighbours)
    request = exchange(request, devices)
    source, star_table, force_table = pl.pallas_call(
        predict_kernel,
        out_shape=(
            shape(blocks, 7, 8, LANES),
            shape(blocks * 8, 3 * LANES, dtype=BF16),
            shape(blocks * 8, 3 * LANES, dtype=BF16),
        ),
        in_specs=[VMEM] * 4,
        out_specs=(VMEM,) * 3,
        compiler_params=PARAMS,
        cost_estimate=cost(1 << 20),
    )(star_state, old_force, star_mass.reshape(blocks, LANES), elapsed.reshape(blocks, LANES))
    own, local, sent = pl.pallas_call(
        functools.partial(own_kernel, stars_dev, cap, targets),
        out_shape=(shape(8, active), shape(8, active, dtype=I32), shape(devices * 6 * active // LANES, LANES)),
        in_specs=[VMEM] * 2,
        out_specs=(VMEM,) * 3,
        compiler_params=PARAMS,
    )(request, star_table)
    sent = exchange(sent, devices)
    listed, slot, back = pl.pallas_call(
        functools.partial(listed_kernel, cap, targets),
        out_shape=(shape(packed * 8, LANES), shape(packed, LANES, dtype=I32), shape(devices, LANES)),
        in_specs=[VMEM] * 5,
        out_specs=(VMEM,) * 3,
        compiler_params=PARAMS,
        cost_estimate=cost(1 << 24),
    )(request, star_table, force_table, own, local)
    sums = pl.pallas_call(
        functools.partial(force_kernel, softening, cap, targets, 4, 32, 16),
        out_shape=shape(devices * 2, LANES),
        in_specs=[VMEM] * 5,
        out_specs=VMEM,
        scratch_shapes=[pltpu.VMEM((active, LANES), F32), pltpu.VMEM((devices, 12, 8, LANES), F32)],
        compiler_params=PARAMS,
    )(sent, source, listed, slot, back)
    sums = exchange(sums, devices)
    state, forces, terms = pl.pallas_call(
        functools.partial(correct_kernel, targets),
        out_shape=(shape(6, targets), shape(targets, 12), shape(6, targets)),
        in_specs=[VMEM],
        out_specs=(VMEM,) * 3,
        compiler_params=PARAMS,
    )(sums)
    return state, forces.T, terms


def solution(mesh):
    placed = (
        P(None, "stars"),
        P(None, "stars"),
        P("stars"),
        P("stars"),
        P("stars"),
        P("stars", None),
        P("stars"),
    )
    return jax.shard_map(
        per_device,
        mesh=mesh,
        in_specs=placed,
        out_specs=(P(None, "stars"), P(None, "stars"), P(None, "stars")),
        check_vma=False,
    )
```

```python
import functools
import math

import jax
import jax.numpy as jnp
from jax import lax
from jax.experimental import pallas as pl
from jax.experimental.pallas import tpu as pltpu
from jax.sharding import PartitionSpec as P

LANES = 128
PARTS = 4
F32 = jnp.float32
I32 = jnp.int32
BF16 = jnp.bfloat16
VMEM = pl.BlockSpec(memory_space=pltpu.VMEM)
HBM = pl.BlockSpec(memory_space=pltpu.HBM)
PARAMS = pltpu.CompilerParams(vmem_limit_bytes=32 * 1024 * 1024)


def iota(shape, axis):
    return lax.broadcasted_iota(I32, shape, axis)


def part_of(device):
    return (device >> 1) & (PARTS - 1)


def line_of(device):
    return (device >> 3) * 2 + (device & 1)


def device_at(line, part):
    return (line >> 1) * 2 * PARTS + part * 2 + (line & 1)


def turn(value, lanes):
    lanes %= LANES
    return pltpu.roll(value, lanes, 1) if lanes else value


def split3(value):
    high = value.astype(BF16)
    rest = value - high.astype(F32)
    middle = rest.astype(BF16)
    low = (rest - middle.astype(F32)).astype(BF16)
    return jnp.concatenate([high, middle, low], axis=1)


def folding(targets):
    same = iota((LANES, LANES), 0) % targets == iota((LANES, LANES), 1) % targets
    return jnp.concatenate([jnp.where(same, 1.0, 0.0).astype(BF16)] * 3, axis=0)


def pick(table, column):
    count = column.shape[1]
    low = jnp.where(column < 0, -1, column & (LANES - 1))
    high = lax.shift_right_logical(column, 7)
    hot = jnp.where(iota((LANES, count), 0) == low, 1.0, 0.0).astype(BF16)
    found = jnp.dot(table, jnp.concatenate([hot] * 3, axis=0), preferred_element_type=F32)
    total = jnp.zeros((8, count), F32)
    for block in range(table.shape[0] // 8):
        total += jnp.where(high == block, found[block * 8 : (block + 1) * 8], 0.0)
    return total


def request_kernel(
    stars_dev, cap, active_hbm, length_hbm, listed_hbm, out_ref, active_ref, length_ref, listed_ref, sems
):
    pairs = ((listed_hbm, listed_ref), (length_hbm, length_ref), (active_hbm, active_ref))
    copies = [pltpu.make_async_copy(*pair, sems.at[i]) for i, pair in enumerate(pairs)]
    for copy in copies:
        copy.start()
    for copy in copies:
        copy.wait()
    targets, slots = listed_ref.shape
    devices = lax.axis_size("stars")
    listed = listed_ref[...]
    owner = listed // stars_dev if stars_dev & (stars_dev - 1) else lax.shift_right_logical(listed, stars_dev.bit_length() - 1)
    local = listed - owner * stars_dev
    low = (local & (LANES - 1)).astype(F32)
    high = lax.shift_right_logical(local, 7).astype(F32)
    lane = iota((devices, LANES), 1)
    row = iota((devices, LANES), 0)
    before = jnp.where(iota((slots, 2 * LANES), 0) < iota((slots, 2 * LANES), 1), 1.0, 0.0).astype(BF16)
    mine = [
        jnp.where((owner[k : k + 1] == row) & (lane < length_ref[k]), 1.0, 0.0) for k in range(targets)
    ]
    counts = jnp.dot(jnp.concatenate(mine, axis=0).astype(BF16), before, preferred_element_type=F32)
    base = jnp.zeros((devices, LANES), F32)
    order = iota((LANES, slots), 0).astype(F32)
    lows, highs, hots = [], [], []
    place = lane - part_of(row)
    begins = jnp.zeros((devices, LANES), F32)
    for k in range(targets):
        ahead = counts[k * devices : (k + 1) * devices]
        rank = jnp.sum(mine[k] * (ahead[:, :LANES] + base), axis=0, keepdims=True)
        hots.append(jnp.where(order == rank, 1.0, 0.0).astype(BF16))
        lows.append((mine[k] * low[k : k + 1]).astype(BF16))
        highs.append((mine[k] * high[k : k + 1]).astype(BF16))
        base = base + ahead[:, LANES:]
        begins = jnp.where(place == (k + 1) * PARTS, base, begins)
    planes = jnp.concatenate([jnp.concatenate(lows, axis=1), jnp.concatenate(highs, axis=1)], axis=0)
    placed = lax.dot_general(
        planes, jnp.concatenate(hots, axis=1), (((1,), (1,)), ((), ())), preferred_element_type=F32
    )
    packed = (placed[:devices] + LANES * placed[devices:]).astype(I32)
    per_row = min(LANES // cap, PARTS)
    alone = packed
    for i in range(1, per_row):
        packed = jnp.where(lane >= i * cap, turn(pltpu.roll(alone, devices - 2 * i, 0), i * cap), packed)
    lane1 = iota((1, LANES), 1)
    actives = jnp.zeros((1, LANES), I32)
    for k in range(targets):
        actives = jnp.where(lane1 == (targets + 1) * PARTS + k, active_ref[k], actives)
    size = 2 * PARTS
    height = size * (PARTS // per_row + 1)
    for first in range(0, devices, size):
        blocks = []
        for core in range(2):
            begin = jnp.where((row[:size] & 1) == core, begins[first : first + size], 0.0)
            begin = jnp.sum(begin, axis=0, keepdims=True).astype(I32)
            rows = [packed[first + at + core : first + at + core + 1] for at in range(0, size, 2 * per_row)]
            blocks += [*rows, begin + actives]
        at = first // size * height
        out_ref[at : at + height] = jnp.concatenate(blocks * PARTS, axis=0)


def predict_kernel(given_ref, star_ref, star_table_ref, force_table_ref):
    tables = []
    for block in range(given_ref.shape[1] // LANES):
        cols = slice(block * LANES, (block + 1) * LANES)
        state, force, mass, step = (given_ref[first:last, cols] for first, last in ((0, 6), (6, 12), (12, 13), (13, 14)))
        accel, jerk = force[0:3], force[3:6]
        position = state[0:3] + step * (state[3:6] + step * (0.5 * accel + step * jerk / 6.0))
        velocity = state[3:6] + step * (accel + 0.5 * step * jerk)
        stars = jnp.concatenate([position, velocity, mass, step], axis=0)
        star_ref[:, cols] = stars
        tables.append((stars, jnp.concatenate([force, jnp.zeros((2, LANES), F32)], axis=0)))
        if block % 2:
            rows = slice((block - 1) * 8, (block + 1) * 8)
            for table_ref, pair in zip((star_table_ref, force_table_ref), zip(*tables)):
                table_ref[rows] = split3(jnp.concatenate(pair, axis=0))
            tables = []


def own_kernel(stars_dev, targets, request_ref, star_table_ref, force_table_ref, out_ref):
    devices = out_ref.shape[0] // sent_rows(out_ref)
    lines = devices // PARTS
    width = request_ref.shape[0] // devices
    first = (targets + 1) * PARTS
    lane, row = iota((devices, LANES), 1), iota((devices, LANES), 0)
    ids = request_ref[pl.ds(width - 1, devices, stride=width), :]
    ids = jnp.where(lane < targets, turn(ids.astype(F32), -first), 0.0)
    span = targets
    while span < LANES:
        ids = ids + turn(ids, span)
        span *= 2
    per_tile = LANES // targets
    tiles = devices // per_tile
    start = (part_of(row) * lines + line_of(row)) * targets
    flat = []
    for t in range(tiles):
        offset = lane + t * LANES - start
        here = (offset >= 0) & (offset < targets)
        flat.append(jnp.sum(jnp.where(here, ids, 0.0), axis=0, keepdims=True))
    local = jnp.concatenate(flat, axis=1).astype(I32) - lax.axis_index("stars") * stars_dev
    local = jnp.where((local >= 0) & (local < stars_dev), local, -1)
    own = pick(star_table_ref[...], local)
    old = pick(force_table_ref[...], local)
    words = jnp.concatenate([own[7:8], old[0:7]], axis=0)
    span = lines * targets
    last = 6 * span
    fold = folding(targets)
    lane, row = iota((per_tile, LANES), 1), iota((per_tile, LANES), 0)
    on_row = (lane >= row * targets) & (lane < (row + 1) * targets)
    lane1 = iota((1, LANES), 1)
    rows = sent_rows(out_ref)
    backs = []
    for t in range(tiles):
        tile = words[:, t * LANES : (t + 1) * LANES]
        spread = jnp.concatenate([jnp.where(on_row, tile[c : c + 1], 0.0) for c in range(7)], axis=0)
        folded = jnp.dot(split3(spread), fold, preferred_element_type=F32)
        back = jnp.zeros((per_tile, LANES), F32)
        for c in range(7):
            begin = last % LANES + c * targets
            here = (lane >= begin) & (lane < begin + targets)
            back = jnp.where(here, folded[c * per_tile : (c + 1) * per_tile], back)
        backs.append(back)
    piece = min(span, LANES)
    turned = {}
    for part in range(PARTS):
        group = [jnp.zeros((1, LANES), F32) for _ in range(rows)]
        for at in range(0, span, piece):
            tile, source = divmod(part * span + at, LANES)
            for c in range(6):
                to, begin = divmod(c * span + at, LANES)
                shift = (begin - source) % LANES
                if (tile, shift) not in turned:
                    turned[tile, shift] = turn(own[:, tile * LANES : (tile + 1) * LANES], shift)
                here = (lane1 >= begin) & (lane1 < begin + piece)
                group[to] = jnp.where(here, turned[tile, shift][c : c + 1], group[to])
        for line in range(lines):
            at = device_at(line, part) * rows
            for r in range(rows - 1):
                out_ref[at + r : at + r + 1] = group[r]
            tile, source = divmod(part * span + line * targets, LANES)
            block = source // targets
            out_ref[at + rows - 1 : at + rows] = group[rows - 1] + backs[tile][block : block + 1]


def sent_rows(ref):
    return ref.shape[0] // lax.axis_size("stars")


def listed_kernel(cap, targets, request_ref, *refs):
    star_refs, (all_ref, listed_ref, slot_ref, table_ref) = refs[:PARTS], refs[PARTS:]
    blocks = star_refs[0].shape[1] // LANES
    mine = part_of(lax.axis_index("stars"))
    for mask, star_ref in enumerate(star_refs):
        stars = star_ref[...]
        all_ref[mask * 8 : (mask + 1) * 8] = stars
        first = (mine ^ mask) * (blocks * 8)
        for pair in range(blocks // 2):
            tiles = [stars[:, (2 * pair + i) * LANES : (2 * pair + i + 1) * LANES] for i in range(2)]
            start = pl.multiple_of(first + pair * 16, 16)
            table_ref[pl.ds(start, 16), :] = split3(jnp.concatenate(tiles, axis=0))
    devices = lax.axis_size("stars")
    lines = devices // PARTS
    width = request_ref.shape[0] // devices
    rows = width - 1
    per_row = PARTS // rows
    at = [device_at(line, mine) * width for line in range(lines)]
    begins = jnp.concatenate([request_ref[pl.ds(first + rows, 1), :] for first in at], axis=0)
    lane = iota((lines, LANES), 1)
    for j in range(rows):
        slot = jnp.zeros((lines, LANES), I32)
        for k in range(1, targets + 1):
            for i in range(per_row):
                column = k * PARTS + j * per_row + i
                begin = begins[:, column : column + 1]
                here = (lane >= begin + i * cap) & (lane >= i * cap) & (lane < (i + 1) * cap)
                slot += jnp.where(here, 1, 0)
        slot_ref[j * lines : (j + 1) * lines] = slot
    lane = iota((1, LANES), 1)
    lane8 = iota((8, LANES), 1)
    for j in range(rows):
        asked = [request_ref[pl.ds(first + j, 1), :] for first in at]
        found = []
        for i in range(per_row):
            columns = []
            for chunk in range(lines // per_row):
                column = asked[chunk * per_row]
                column = turn(column, -i * cap)
                for b in range(1, per_row):
                    column = jnp.where(lane >= b * cap, turn(asked[chunk * per_row + b], (b - i) * cap), column)
                columns.append(column)
            size = blocks * 8
            table = table_ref[(j * per_row + i) * size : (j * per_row + i + 1) * size]
            found.append(pick(table, jnp.concatenate(columns, axis=1)))
        for line in range(lines):
            chunk, b = divmod(line, per_row)
            cols = slice(chunk * LANES, (chunk + 1) * LANES)
            near = turn(found[0][:, cols], -b * cap)
            for i in range(1, per_row):
                near = jnp.where(lane8 >= i * cap, turn(found[i][:, cols], (i - b) * cap), near)
            listed_ref[(j * lines + line) * 8 : (j * lines + line + 1) * 8] = near


def pair_sums(target, source, mass, softening, sums):
    x, y, z = (source[c] - target[c] for c in range(3))
    u, v, w = (source[c] - target[c] for c in range(3, 6))
    inverse = lax.rsqrt(x * x + y * y + z * z + softening)
    square = inverse * inverse
    strength = mass * inverse * square
    radial = (x * u + y * v + z * w) * (3.0 * square)
    return (
        sums[0] + strength * x,
        sums[1] + strength * y,
        sums[2] + strength * z,
        sums[3] + strength * (u - radial * x),
        sums[4] + strength * (v - radial * y),
        sums[5] + strength * (w - radial * z),
    )


def force_kernel(softening, targets, group_step, core, sent_ref, all_ref, listed_ref, slot_ref, out_ref, kept_ref, target_ref):
    devices = lax.axis_size("stars")
    lines = devices // PARTS
    span = lines * targets
    rows = sent_ref.shape[0] // devices
    height = math.lcm(rows, 8)
    sent = sent_ref[0:height]
    for i in range(1, sent_ref.shape[0] // height):
        sent = sent + sent_ref[i * height : (i + 1) * height]
    block = sent[0:rows]
    for i in range(1, height // rows):
        block = block + sent[i * rows : (i + 1) * rows]
    if kept_ref.shape[0] > rows:
        block = jnp.concatenate([block, jnp.zeros((kept_ref.shape[0] - rows, LANES), F32)], axis=0)
    kept_ref[...] = block
    piece = min(span, LANES)
    for at in range(0, span, piece):
        places = [divmod(c * span + at, LANES) for c in range(6)]
        tile = [turn(block[r : r + 1], -begin) for r, begin in places]
        tile = jnp.concatenate([*tile, jnp.zeros((2, LANES), F32)], axis=0).T
        target_ref[at : at + piece, 0:8] = tile[0:piece]
    side = (lax.axis_index("stars") + core) & 1
    lane, row = iota((8, LANES), 1), iota((8, LANES), 0)
    zeros = (jnp.zeros((8, LANES), F32),) * 6
    count = lines // 2
    for first in range(0, count, group_step):
        groups = [2 * n + side for n in range(first, min(first + group_step, count))]
        held = []
        for group in groups:
            tile = target_ref[pl.ds(pl.multiple_of(group * targets, 8), 8), 0:8]
            held.append([jnp.broadcast_to(tile[:, c : c + 1], (8, LANES)) for c in range(6)])

        def add_stars(part, sums, held=held):
            for s in range(all_ref.shape[1] // LANES):
                tile = all_ref[pl.ds(pl.multiple_of(part * 8, 8), 8), s * LANES : (s + 1) * LANES]
                source = [jnp.broadcast_to(tile[c : c + 1], (8, LANES)) for c in range(7)]
                sums = tuple(pair_sums(held[n], source, source[6], softening, sums[n]) for n in range(len(held)))
            return sums

        sums = lax.fori_loop(0, PARTS, add_stars, (zeros,) * len(held))
        for n, group in enumerate(groups):
            irregular = zeros
            for j in range(slot_ref.shape[0] // lines):
                at = j * lines + group
                near = listed_ref[pl.ds(pl.multiple_of(at * 8, 8), 8), :]
                mass = jnp.where(slot_ref[pl.ds(at, 1), :] == row, near[6:7], 0.0)
                irregular = pair_sums(held[n], [near[c : c + 1] for c in range(6)], mass, softening, irregular)
            result = zeros[0]
            for c, values in enumerate(sums[n] + irregular):
                value = jnp.sum(values, axis=1, keepdims=True)
                result = jnp.where(lane == c * targets + row, value, result)
            out_ref[first + n : first + n + 1] = jnp.sum(result, axis=0, keepdims=True)


def share_kernel(mine_ref, partner_ref, *out_refs):
    total = mine_ref[...] + partner_ref[...]
    place = lax.axis_index("stars") // (2 * PARTS)
    for mask, out_ref in enumerate(out_refs):
        chosen = place ^ mask
        result = total[0:1]
        for n in range(1, len(out_refs)):
            result = jnp.where(chosen == n, total[n : n + 1], result)
        out_ref[...] = result


def correct_kernel(targets, kept_ref, *refs):
    sums_refs, (state_ref, forces_ref, terms_ref) = refs[:-3], refs[-3:]
    lines = 2 * len(sums_refs)
    span = lines * targets
    total = sums_refs[0][...]
    for sums_ref in sums_refs[1:]:
        total = total + sums_ref[...]
    kept = kept_ref[...]
    piece = min(span, LANES)
    at = line_of(lax.axis_index("stars")) * targets
    moved = pltpu.roll(kept, (LANES - at % piece) % LANES, 1)
    lane, row = iota((16, LANES), 1), iota((16, LANES), 0)
    on_row = (lane >= row * targets) & (lane < (row + 1) * targets)
    lane1 = iota((1, LANES), 1)
    spread = [jnp.where(on_row, total, 0.0)]
    for c in range(6):
        r, begin = divmod(c * span, LANES)
        value = moved[r : r + 1]
        for q in range(1, span // piece):
            value = jnp.where(at // piece == q, moved[r + q : r + q + 1], value)
        spread.append(jnp.where((lane1 >= begin) & (lane1 < begin + targets), value, 0.0))
    for c in range(7):
        r, begin = divmod(6 * span + c * targets, LANES)
        spread.append(jnp.where((lane1 >= begin) & (lane1 < begin + targets), kept[r : r + 1], 0.0))
    spread.append(jnp.zeros((3, LANES), F32))
    rows = jnp.dot(split3(jnp.concatenate(spread, axis=0)), folding(targets), preferred_element_type=F32)[:, 0:targets]
    accel, jerk, irregular = rows[0:3], rows[3:6], rows[6:12]
    position, velocity, step = rows[16:19], rows[19:22], rows[22:23]
    old_accel, old_jerk = rows[23:26], rows[26:29]
    change = accel - old_accel
    second = 3.0 * change - step * (2.0 * old_jerk + jerk)
    third = -2.0 * change + step * (old_jerk + jerk)
    state_ref[0:3] = position + step * step * (second / 12.0 + third / 20.0)
    state_ref[3:6] = velocity + step * (second / 3.0 + third / 4.0)
    forces = jnp.concatenate([irregular, rows[0:6] - irregular, jnp.zeros((4, targets), F32)], axis=0)
    forces_ref[...] = forces.T[:, 0:12]
    terms_ref[0:3] = second
    terms_ref[3:6] = third


def exchange(rows, devices):
    wide = rows.reshape(devices, 1, -1)
    return lax.all_to_all(wide, "stars", 0, 0, tiled=True).reshape(rows.shape)


def per_device(star_state, old_force, star_mass, elapsed, active_ids, neighbours, list_length):
    stars_dev = star_state.shape[1]
    devices = lax.axis_size("stars")
    lines = devices // PARTS
    targets, slots = neighbours.shape
    cap = 2 * targets * slots // devices
    blocks = stars_dev // LANES
    request_rows = max(1, PARTS * cap // LANES)
    back_rows = -(-(6 * lines + 7) * targets // LANES)
    softening = 0.25 * math.sqrt(slots) / (stars_dev * devices)

    def shape(*dims, dtype=F32):
        return jax.ShapeDtypeStruct(dims, dtype)

    def cost(flops):
        return pl.CostEstimate(flops=flops, bytes_accessed=1 << 20, transcendentals=0)

    def swap(value, mask):
        return lax.ppermute(value, "stars", [(i, i ^ mask) for i in range(devices)])

    request = pl.pallas_call(
        functools.partial(request_kernel, stars_dev, cap),
        out_shape=shape(devices * (request_rows + 1), LANES, dtype=I32),
        in_specs=[HBM] * 3,
        out_specs=VMEM,
        scratch_shapes=[
            pltpu.SMEM((targets,), I32),
            pltpu.SMEM((targets,), I32),
            pltpu.VMEM((targets, slots), I32),
            pltpu.SemaphoreType.DMA((3,)),
        ],
        cost_estimate=pl.CostEstimate(flops=1 << 20, bytes_accessed=1 << 26, transcendentals=0),
    )(active_ids, list_length, neighbours)
    asked = exchange(request, devices)
    stars, star_table, force_table = pl.pallas_call(
        predict_kernel,
        out_shape=(
            shape(8, stars_dev),
            shape(blocks * 8, 3 * LANES, dtype=BF16),
            shape(blocks * 8, 3 * LANES, dtype=BF16),
        ),
        in_specs=[VMEM],
        out_specs=(VMEM,) * 3,
        compiler_params=PARAMS,
        cost_estimate=cost(1 << 20),
    )(jnp.concatenate([star_state, old_force, star_mass[None], elapsed[None]], axis=0))
    shared = [stars, *(swap(stars, 2 * mask) for mask in range(1, PARTS))]
    sent = pl.pallas_call(
        functools.partial(own_kernel, stars_dev, targets),
        out_shape=shape(devices * back_rows, LANES),
        in_specs=[VMEM] * 3,
        out_specs=VMEM,
        compiler_params=PARAMS,
    )(asked, star_table, force_table)
    sent = exchange(sent, devices)
    every, listed, slot = pl.pallas_call(
        functools.partial(listed_kernel, cap, targets),
        out_shape=(
            shape(PARTS * 8, stars_dev),
            shape(lines * request_rows * 8, LANES),
            shape(lines * request_rows, LANES, dtype=I32),
        ),
        in_specs=[VMEM] * (1 + PARTS),
        out_specs=(VMEM,) * 3,
        scratch_shapes=[pltpu.VMEM((PARTS * blocks * 8, 3 * LANES), BF16)],
        compiler_params=PARAMS,
        cost_estimate=cost(1 << 24),
    )(asked, *shared)
    kept_rows = -(-back_rows // 8) * 8

    def forces_of(core):
        return pl.pallas_call(
            functools.partial(force_kernel, softening, targets, 4, core),
            out_shape=(shape(max(8, lines // 2), LANES), shape(kept_rows, LANES)),
            in_specs=[VMEM] * 4,
            out_specs=(VMEM,) * 2,
            scratch_shapes=[pltpu.VMEM((lines * targets, LANES), F32)],
            compiler_params=PARAMS,
        )(sent, every, listed, slot)

    theirs, _ = forces_of(1)
    mine, kept = forces_of(0)
    sums = pl.pallas_call(
        share_kernel,
        out_shape=(shape(1, LANES),) * (lines // 2),
        in_specs=[VMEM] * 2,
        out_specs=(VMEM,) * (lines // 2),
        compiler_params=PARAMS,
    )(mine, swap(theirs, 1))
    sums = [sums[0], *(swap(sums[mask], mask * 2 * PARTS) for mask in range(lines // 2 - 1, 0, -1))]
    state, forces, terms = pl.pallas_call(
        functools.partial(correct_kernel, targets),
        out_shape=(shape(6, targets), shape(targets, 12), shape(6, targets)),
        in_specs=[VMEM] * (1 + lines // 2),
        out_specs=(VMEM,) * 3,
        compiler_params=PARAMS,
    )(kept, *sums)
    return state, forces.T, terms


def solution(mesh):
    placed = (
        P(None, "stars"),
        P(None, "stars"),
        P("stars"),
        P("stars"),
        P("stars"),
        P("stars", None),
        P("stars"),
    )
    return jax.shard_map(
        per_device,
        mesh=mesh,
        in_specs=placed,
        out_specs=(P(None, "stars"), P(None, "stars"), P(None, "stars")),
        check_vma=False,
    )
```

```python
import functools
import math

import jax
import jax.numpy as jnp
from jax import lax
from jax.experimental import pallas as pl
from jax.experimental.pallas import tpu as pltpu
from jax.sharding import PartitionSpec as P

LANES = 128
PARTS = 4
F32 = jnp.float32
I32 = jnp.int32
BF16 = jnp.bfloat16
VMEM = pl.BlockSpec(memory_space=pltpu.VMEM)
HBM = pl.BlockSpec(memory_space=pltpu.HBM)
PARAMS = pltpu.CompilerParams(vmem_limit_bytes=32 * 1024 * 1024)


def iota(shape, axis):
    return lax.broadcasted_iota(I32, shape, axis)


def part_of(device):
    return (device >> 1) & (PARTS - 1)


def line_of(device):
    return (device >> 3) * 2 + (device & 1)


def device_at(line, part):
    return (line >> 1) * 2 * PARTS + part * 2 + (line & 1)


def turn(value, lanes):
    lanes %= LANES
    return pltpu.roll(value, lanes, 1) if lanes else value


def split3(value):
    high = value.astype(BF16)
    rest = value - high.astype(F32)
    middle = rest.astype(BF16)
    low = (rest - middle.astype(F32)).astype(BF16)
    return jnp.concatenate([high, middle, low], axis=1)


def folding(targets):
    same = iota((LANES, LANES), 0) % targets == iota((LANES, LANES), 1) % targets
    return jnp.concatenate([jnp.where(same, 1.0, 0.0).astype(BF16)] * 3, axis=0)


def pick(table, column, rows=8):
    count = column.shape[1]
    low = jnp.where(column < 0, -1, column & (LANES - 1))
    high = lax.shift_right_logical(column, 7)
    hot = jnp.where(iota((LANES, count), 0) == low, 1.0, 0.0).astype(BF16)
    found = jnp.dot(table, jnp.concatenate([hot] * 3, axis=0), preferred_element_type=F32)
    total = jnp.zeros((rows, count), F32)
    for block in range(table.shape[0] // rows):
        total += jnp.where(high == block, found[block * rows : (block + 1) * rows], 0.0)
    return total


def request_kernel(
    stars_dev, cap, active_hbm, length_hbm, listed_hbm, out_ref, active_ref, length_ref, listed_ref, sems
):
    pairs = ((listed_hbm, listed_ref), (length_hbm, length_ref), (active_hbm, active_ref))
    copies = [pltpu.make_async_copy(*pair, sems.at[i]) for i, pair in enumerate(pairs)]
    for copy in copies:
        copy.start()
    for copy in copies:
        copy.wait()
    targets, slots = listed_ref.shape
    devices = lax.axis_size("stars")
    listed = listed_ref[...]
    owner = listed // stars_dev if stars_dev & (stars_dev - 1) else lax.shift_right_logical(listed, stars_dev.bit_length() - 1)
    local = listed - owner * stars_dev
    low = (local & (LANES - 1)).astype(F32)
    high = lax.shift_right_logical(local, 7).astype(F32)
    lane = iota((devices, LANES), 1)
    row = iota((devices, LANES), 0)
    before = jnp.where(iota((slots, 2 * LANES), 0) < iota((slots, 2 * LANES), 1), 1.0, 0.0).astype(BF16)
    mine = [
        jnp.where((owner[k : k + 1] == row) & (lane < length_ref[k]), 1.0, 0.0) for k in range(targets)
    ]
    counts = jnp.dot(jnp.concatenate(mine, axis=0).astype(BF16), before, preferred_element_type=F32)
    base = jnp.zeros((devices, LANES), F32)
    order = iota((LANES, slots), 0).astype(F32)
    lows, highs, hots = [], [], []
    place = lane - part_of(row)
    begins = jnp.zeros((devices, LANES), F32)
    for k in range(targets):
        ahead = counts[k * devices : (k + 1) * devices]
        rank = jnp.sum(mine[k] * (ahead[:, :LANES] + base), axis=0, keepdims=True)
        hots.append(jnp.where(order == rank, 1.0, 0.0).astype(BF16))
        lows.append((mine[k] * low[k : k + 1]).astype(BF16))
        highs.append((mine[k] * high[k : k + 1]).astype(BF16))
        base = base + ahead[:, LANES:]
        begins = jnp.where(place == LANES // 2 + k * PARTS, base, begins)
    planes = jnp.concatenate([jnp.concatenate(lows, axis=1), jnp.concatenate(highs, axis=1)], axis=0)
    placed = lax.dot_general(
        planes, jnp.concatenate(hots, axis=1), (((1,), (1,)), ((), ())), preferred_element_type=F32
    )
    packed = (placed[:devices] + LANES * placed[devices:]).astype(I32)
    per_row = min(LANES // cap, PARTS)
    alone = packed
    for i in range(1, per_row):
        packed = jnp.where(lane >= i * cap, turn(pltpu.roll(alone, devices - 2 * i, 0), i * cap), packed)
    lane1 = iota((1, LANES), 1)
    actives = jnp.zeros((1, LANES), I32)
    for k in range(targets):
        actives = jnp.where((lane1 < LANES // 2) & (lane1 % targets == k), active_ref[k], actives)
    size = 2 * PARTS
    height = size * (PARTS // per_row + 1)
    for first in range(0, devices, size):
        blocks = []
        for core in range(2):
            begin = jnp.where((row[:size] & 1) == core, begins[first : first + size], 0.0)
            begin = jnp.sum(begin, axis=0, keepdims=True).astype(I32)
            rows = [packed[first + at + core : first + at + core + 1] for at in range(0, size, 2 * per_row)]
            blocks += [*rows, begin + actives]
        at = first // size * height
        out_ref[at : at + height] = jnp.concatenate(blocks * PARTS, axis=0)


def predict_kernel(given_ref, star_ref, table_ref):
    for block in range(given_ref.shape[1] // LANES):
        cols = slice(block * LANES, (block + 1) * LANES)
        state, force, mass, step = (given_ref[first:last, cols] for first, last in ((0, 6), (6, 12), (12, 13), (13, 14)))
        accel, jerk = force[0:3], force[3:6]
        position = state[0:3] + step * (state[3:6] + step * (0.5 * accel + step * jerk / 6.0))
        velocity = state[3:6] + step * (accel + 0.5 * step * jerk)
        stars = jnp.concatenate([position, velocity, mass, step], axis=0)
        star_ref[:, cols] = stars
        rows = jnp.concatenate([stars, force, jnp.zeros((2, LANES), F32)], axis=0)
        table_ref[block * 16 : (block + 1) * 16] = split3(rows)


def own_kernel(stars_dev, targets, request_ref, table_ref, out_ref):
    devices = out_ref.shape[0] // sent_rows(out_ref)
    lines = devices // PARTS
    width = request_ref.shape[0] // devices
    lane, row = iota((devices, LANES), 1), iota((devices, LANES), 0)
    ids = request_ref[pl.ds(width - 1, devices, stride=width), :]
    ids = ids.astype(F32)
    ids = jnp.where(lane < LANES // 2, ids, turn(ids, LANES // 2))
    per_tile = LANES // targets
    tiles = devices // per_tile
    start = (part_of(row) * lines + line_of(row)) * targets
    flat = []
    for t in range(tiles):
        offset = lane + t * LANES - start
        here = (offset >= 0) & (offset < targets)
        flat.append(jnp.sum(jnp.where(here, ids, 0.0), axis=0, keepdims=True))
    local = jnp.concatenate(flat, axis=1).astype(I32) - lax.axis_index("stars") * stars_dev
    local = jnp.where((local >= 0) & (local < stars_dev), local, -1)
    own = pick(table_ref[...], local, 16)
    words = own[7:14]
    own = own[0:8]
    span = lines * targets
    last = 6 * span
    fold = folding(targets)
    lane, row = iota((per_tile, LANES), 1), iota((per_tile, LANES), 0)
    on_row = (lane >= row * targets) & (lane < (row + 1) * targets)
    lane1 = iota((1, LANES), 1)
    rows = sent_rows(out_ref)
    backs = []
    for t in range(tiles):
        tile = words[:, t * LANES : (t + 1) * LANES]
        spread = jnp.concatenate([jnp.where(on_row, tile[c : c + 1], 0.0) for c in range(7)], axis=0)
        folded = jnp.dot(split3(spread), fold, preferred_element_type=F32)
        back = jnp.zeros((per_tile, LANES), F32)
        for c in range(7):
            begin = last % LANES + c * targets
            here = (lane >= begin) & (lane < begin + targets)
            back = jnp.where(here, folded[c * per_tile : (c + 1) * per_tile], back)
        backs.append(back)
    piece = min(span, LANES)
    turned = {}
    for part in range(PARTS):
        group = [jnp.zeros((1, LANES), F32) for _ in range(rows)]
        for at in range(0, span, piece):
            tile, source = divmod(part * span + at, LANES)
            for c in range(6):
                to, begin = divmod(c * span + at, LANES)
                shift = (begin - source) % LANES
                if (tile, shift) not in turned:
                    turned[tile, shift] = turn(own[:, tile * LANES : (tile + 1) * LANES], shift)
                here = (lane1 >= begin) & (lane1 < begin + piece)
                group[to] = jnp.where(here, turned[tile, shift][c : c + 1], group[to])
        for line in range(lines):
            at = device_at(line, part) * rows
            for r in range(rows - 1):
                out_ref[at + r : at + r + 1] = group[r]
            tile, source = divmod(part * span + line * targets, LANES)
            block = source // targets
            out_ref[at + rows - 1 : at + rows] = group[rows - 1] + backs[tile][block : block + 1]


def sent_rows(ref):
    return ref.shape[0] // lax.axis_size("stars")


def listed_kernel(cap, targets, request_ref, *refs):
    star_refs, (all_ref, listed_ref, slot_ref, table_ref) = refs[:PARTS], refs[PARTS:]
    blocks = star_refs[0].shape[1] // LANES
    mine = part_of(lax.axis_index("stars"))
    for mask, star_ref in enumerate(star_refs):
        stars = star_ref[...]
        all_ref[mask * 8 : (mask + 1) * 8] = stars
        first = (mine ^ mask) * (blocks * 8)
        for pair in range(blocks // 2):
            tiles = [stars[:, (2 * pair + i) * LANES : (2 * pair + i + 1) * LANES] for i in range(2)]
            start = pl.multiple_of(first + pair * 16, 16)
            table_ref[pl.ds(start, 16), :] = split3(jnp.concatenate(tiles, axis=0))
    devices = lax.axis_size("stars")
    lines = devices // PARTS
    width = request_ref.shape[0] // devices
    rows = width - 1
    per_row = PARTS // rows
    at = [device_at(line, mine) * width for line in range(lines)]
    begins = jnp.concatenate([request_ref[pl.ds(first + rows, 1), :] for first in at], axis=0)
    lane = iota((lines, LANES), 1)
    for j in range(rows):
        slot = jnp.zeros((lines, LANES), I32)
        for k in range(1, targets + 1):
            for i in range(per_row):
                column = LANES // 2 + (k - 1) * PARTS + j * per_row + i
                begin = begins[:, column : column + 1]
                here = (lane >= begin + i * cap) & (lane >= i * cap) & (lane < (i + 1) * cap)
                slot += jnp.where(here, 1, 0)
        slot_ref[j * lines : (j + 1) * lines] = slot
    lane = iota((1, LANES), 1)
    lane8 = iota((8, LANES), 1)
    for j in range(rows):
        asked = [request_ref[pl.ds(first + j, 1), :] for first in at]
        found = []
        for i in range(per_row):
            columns = []
            for chunk in range(lines // per_row):
                column = asked[chunk * per_row]
                column = turn(column, -i * cap)
                for b in range(1, per_row):
                    column = jnp.where(lane >= b * cap, turn(asked[chunk * per_row + b], (b - i) * cap), column)
                columns.append(column)
            size = blocks * 8
            table = table_ref[(j * per_row + i) * size : (j * per_row + i + 1) * size]
            found.append(pick(table, jnp.concatenate(columns, axis=1)))
        for line in range(lines):
            chunk, b = divmod(line, per_row)
            cols = slice(chunk * LANES, (chunk + 1) * LANES)
            near = turn(found[0][:, cols], -b * cap)
            for i in range(1, per_row):
                near = jnp.where(lane8 >= i * cap, turn(found[i][:, cols], (i - b) * cap), near)
            listed_ref[(j * lines + line) * 8 : (j * lines + line + 1) * 8] = near


def pair_sums(target, source, mass, softening, sums):
    x, y, z = (source[c] - target[c] for c in range(3))
    u, v, w = (source[c] - target[c] for c in range(3, 6))
    inverse = lax.rsqrt(x * x + y * y + z * z + softening)
    square = inverse * inverse
    strength = mass * inverse * square
    radial = (x * u + y * v + z * w) * (3.0 * square)
    return (
        sums[0] + strength * x,
        sums[1] + strength * y,
        sums[2] + strength * z,
        sums[3] + strength * (u - radial * x),
        sums[4] + strength * (v - radial * y),
        sums[5] + strength * (w - radial * z),
    )


def force_kernel(
    softening, targets, group_step, core, masks, sent_ref, all_ref, listed_ref, slot_ref, out_ref, *kept_refs
):
    devices = lax.axis_size("stars")
    lines = devices // PARTS
    span = lines * targets
    rows = sent_ref.shape[0] // devices
    height = math.lcm(rows, 8)
    sent = sent_ref[0:height]
    for i in range(1, sent_ref.shape[0] // height):
        sent = sent + sent_ref[i * height : (i + 1) * height]
    block = sent[0:rows]
    for i in range(1, height // rows):
        block = block + sent[i * rows : (i + 1) * rows]
    target_ref = kept_refs[-1]
    for kept_ref in kept_refs[:-1]:
        kept_ref[0:rows] = block
        kept_ref[rows:] = jnp.zeros((kept_ref.shape[0] - rows, LANES), F32)
    piece = min(span, LANES)
    for at in range(0, span, piece):
        places = [divmod(c * span + at, LANES) for c in range(6)]
        tile = [turn(block[r : r + 1], -begin) for r, begin in places]
        tile = jnp.concatenate([*tile, jnp.zeros((2, LANES), F32)], axis=0).T
        target_ref[at : at + piece, 0:8] = tile[0:piece]
    me = lax.axis_index("stars")
    side, place = (me + core) & 1, me // (2 * PARTS)
    lane, row = iota((8, LANES), 1), iota((8, LANES), 0)
    zeros = (jnp.zeros((8, LANES), F32),) * 6
    for first in range(0, len(masks), group_step):
        groups = [2 * (place ^ mask) + side for mask in masks[first : first + group_step]]
        held = []
        for group in groups:
            tile = target_ref[pl.ds(pl.multiple_of(group * targets, 8), 8), 0:8]
            held.append([jnp.broadcast_to(tile[:, c : c + 1], (8, LANES)) for c in range(6)])

        def add_stars(part, sums, held=held):
            for s in range(all_ref.shape[1] // LANES):
                tile = all_ref[pl.ds(pl.multiple_of(part * 8, 8), 8), s * LANES : (s + 1) * LANES]
                source = [jnp.broadcast_to(tile[c : c + 1], (8, LANES)) for c in range(7)]
                sums = tuple(pair_sums(held[n], source, source[6], softening, sums[n]) for n in range(len(held)))
            return sums

        sums = lax.fori_loop(0, PARTS, add_stars, (zeros,) * len(held))
        for n, group in enumerate(groups):
            irregular = zeros
            for j in range(slot_ref.shape[0] // lines):
                at = j * lines + group
                near = listed_ref[pl.ds(pl.multiple_of(at * 8, 8), 8), :]
                mass = jnp.where(slot_ref[pl.ds(at, 1), :] == row, near[6:7], 0.0)
                irregular = pair_sums(held[n], [near[c : c + 1] for c in range(6)], mass, softening, irregular)
            result = zeros[0]
            for c, values in enumerate(sums[n] + irregular):
                value = jnp.sum(values, axis=1, keepdims=True)
                result = jnp.where(lane == c * targets + row, value, result)
            out_ref[first + n : first + n + 1] = jnp.sum(result, axis=0, keepdims=True)


def share_kernel(mine_ref, partner_ref, *out_refs):
    for n, out_ref in enumerate(out_refs):
        out_ref[...] = mine_ref[n : n + 1] + partner_ref[n + 1 : n + 2]


def correct_kernel(targets, kept_ref, mine_ref, partner_ref, *refs):
    sums_refs, (state_ref, forces_ref, terms_ref) = refs[:-3], refs[-3:]
    lines = 2 * (len(sums_refs) + 1)
    span = lines * targets
    total = mine_ref[0:1] + partner_ref[0:1]
    for sums_ref in sums_refs:
        total = total + sums_ref[...]
    kept = kept_ref[...]
    piece = min(span, LANES)
    at = line_of(lax.axis_index("stars")) * targets
    moved = pltpu.roll(kept, (LANES - at % piece) % LANES, 1)
    lane, row = iota((16, LANES), 1), iota((16, LANES), 0)
    on_row = (lane >= row * targets) & (lane < (row + 1) * targets)
    lane1 = iota((1, LANES), 1)
    spread = [jnp.where(on_row, total, 0.0)]
    for c in range(6):
        r, begin = divmod(c * span, LANES)
        value = moved[r : r + 1]
        for q in range(1, span // piece):
            value = jnp.where(at // piece == q, moved[r + q : r + q + 1], value)
        spread.append(jnp.where((lane1 >= begin) & (lane1 < begin + targets), value, 0.0))
    for c in range(7):
        r, begin = divmod(6 * span + c * targets, LANES)
        spread.append(jnp.where((lane1 >= begin) & (lane1 < begin + targets), kept[r : r + 1], 0.0))
    spread.append(jnp.zeros((3, LANES), F32))
    rows = jnp.dot(split3(jnp.concatenate(spread, axis=0)), folding(targets), preferred_element_type=F32)[:, 0:targets]
    accel, jerk, irregular = rows[0:3], rows[3:6], rows[6:12]
    position, velocity, step = rows[16:19], rows[19:22], rows[22:23]
    old_accel, old_jerk = rows[23:26], rows[26:29]
    change = accel - old_accel
    second = 3.0 * change - step * (2.0 * old_jerk + jerk)
    third = -2.0 * change + step * (old_jerk + jerk)
    state_ref[0:3] = position + step * step * (second / 12.0 + third / 20.0)
    state_ref[3:6] = velocity + step * (second / 3.0 + third / 4.0)
    forces = jnp.concatenate([irregular, rows[0:6] - irregular, jnp.zeros((4, targets), F32)], axis=0)
    forces_ref[...] = forces.T[:, 0:12]
    terms_ref[0:3] = second
    terms_ref[3:6] = third


def exchange(rows, devices):
    wide = rows.reshape(devices, 1, -1)
    return lax.all_to_all(wide, "stars", 0, 0, tiled=True).reshape(rows.shape)


def per_device(star_state, old_force, star_mass, elapsed, active_ids, neighbours, list_length):
    stars_dev = star_state.shape[1]
    devices = lax.axis_size("stars")
    lines = devices // PARTS
    targets, slots = neighbours.shape
    cap = 2 * targets * slots // devices
    blocks = stars_dev // LANES
    request_rows = max(1, PARTS * cap // LANES)
    back_rows = -(-(6 * lines + 7) * targets // LANES)
    softening = 0.25 * math.sqrt(slots) / (stars_dev * devices)

    def shape(*dims, dtype=F32):
        return jax.ShapeDtypeStruct(dims, dtype)

    def cost(flops):
        return pl.CostEstimate(flops=flops, bytes_accessed=1 << 20, transcendentals=0)

    def swap(value, mask):
        return lax.ppermute(value, "stars", [(i, i ^ mask) for i in range(devices)])

    request = pl.pallas_call(
        functools.partial(request_kernel, stars_dev, cap),
        out_shape=shape(devices * (request_rows + 1), LANES, dtype=I32),
        in_specs=[HBM] * 3,
        out_specs=VMEM,
        scratch_shapes=[
            pltpu.SMEM((targets,), I32),
            pltpu.SMEM((targets,), I32),
            pltpu.VMEM((targets, slots), I32),
            pltpu.SemaphoreType.DMA((3,)),
        ],
        cost_estimate=pl.CostEstimate(flops=1 << 20, bytes_accessed=1 << 26, transcendentals=0),
    )(active_ids, list_length, neighbours)
    asked = exchange(request, devices)
    stars, table = pl.pallas_call(
        predict_kernel,
        out_shape=(shape(8, stars_dev), shape(blocks * 16, 3 * LANES, dtype=BF16)),
        in_specs=[VMEM],
        out_specs=(VMEM,) * 2,
        compiler_params=PARAMS,
        cost_estimate=cost(1 << 20),
    )(jnp.concatenate([star_state, old_force, star_mass[None], elapsed[None]], axis=0))
    shared = [stars, *(swap(stars, 2 * mask) for mask in range(1, PARTS))]
    sent = pl.pallas_call(
        functools.partial(own_kernel, stars_dev, targets),
        out_shape=shape(devices * back_rows, LANES),
        in_specs=[VMEM] * 2,
        out_specs=VMEM,
        compiler_params=PARAMS,
    )(asked, table)
    sent = exchange(sent, devices)
    every, listed, slot = pl.pallas_call(
        functools.partial(listed_kernel, cap, targets),
        out_shape=(
            shape(PARTS * 8, stars_dev),
            shape(lines * request_rows * 8, LANES),
            shape(lines * request_rows, LANES, dtype=I32),
        ),
        in_specs=[VMEM] * (1 + PARTS),
        out_specs=(VMEM,) * 3,
        scratch_shapes=[pltpu.VMEM((PARTS * blocks * 8, 3 * LANES), BF16)],
        compiler_params=PARAMS,
        cost_estimate=cost(1 << 24),
    )(asked, *shared)
    kept_rows = -(-back_rows // 8) * 8

    places = lines // 2

    def forces_of(core, masks, *kept):
        return pl.pallas_call(
            functools.partial(force_kernel, softening, targets, 4, core, masks),
            out_shape=(shape(-(-len(masks) // 8) * 8, LANES), *kept),
            in_specs=[VMEM] * 4,
            out_specs=(VMEM,) * (1 + len(kept)),
            scratch_shapes=[pltpu.VMEM((lines * targets, LANES), F32)],
            compiler_params=PARAMS,
        )(sent, every, listed, slot)

    (theirs,) = forces_of(1, range(places))
    (others,) = forces_of(0, range(1, places))
    theirs = swap(theirs, 1)
    sums = pl.pallas_call(
        share_kernel,
        out_shape=(shape(1, LANES),) * (places - 1),
        in_specs=[VMEM] * 2,
        out_specs=(VMEM,) * (places - 1),
        compiler_params=PARAMS,
    )(others, theirs)
    sums = [swap(sums[mask - 1], mask * 2 * PARTS) for mask in range(places - 1, 0, -1)]
    mine, kept = forces_of(0, range(1), shape(kept_rows, LANES))
    state, forces, terms = pl.pallas_call(
        functools.partial(correct_kernel, targets),
        out_shape=(shape(6, targets), shape(targets, 12), shape(6, targets)),
        in_specs=[VMEM] * (2 + places),
        out_specs=(VMEM,) * 3,
        compiler_params=PARAMS,
    )(kept, mine, theirs, *sums)
    return state, forces.T, terms


def solution(mesh):
    placed = (
        P(None, "stars"),
        P(None, "stars"),
        P("stars"),
        P("stars"),
        P("stars"),
        P("stars", None),
        P("stars"),
    )
    return jax.shard_map(
        per_device,
        mesh=mesh,
        in_specs=placed,
        out_specs=(P(None, "stars"), P(None, "stars"), P(None, "stars")),
        check_vma=False,
    )
```

```python
import functools
import math

import jax
import jax.numpy as jnp
from jax import lax
from jax.experimental import pallas as pl
from jax.experimental.pallas import tpu as pltpu
from jax.sharding import PartitionSpec as P

LANES = 128
PARTS = 4
F32 = jnp.float32
I32 = jnp.int32
BF16 = jnp.bfloat16
VMEM = pl.BlockSpec(memory_space=pltpu.VMEM)
HBM = pl.BlockSpec(memory_space=pltpu.HBM)
PARAMS = pltpu.CompilerParams(vmem_limit_bytes=32 * 1024 * 1024)


def iota(shape, axis):
    return lax.broadcasted_iota(I32, shape, axis)


def part_of(device):
    return (device >> 1) & (PARTS - 1)


def line_of(device):
    return (device >> 3) * 2 + (device & 1)


def device_at(line, part):
    return (line >> 1) * 2 * PARTS + part * 2 + (line & 1)


def turn(value, lanes):
    lanes %= LANES
    return pltpu.roll(value, lanes, 1) if lanes else value


def split3(value):
    high = value.astype(BF16)
    rest = value - high.astype(F32)
    middle = rest.astype(BF16)
    low = (rest - middle.astype(F32)).astype(BF16)
    return jnp.concatenate([high, middle, low], axis=1)


def folding(targets):
    same = iota((LANES, LANES), 0) % targets == iota((LANES, LANES), 1) % targets
    return jnp.concatenate([jnp.where(same, 1.0, 0.0).astype(BF16)] * 3, axis=0)


def pick(table, column, rows=8):
    count = column.shape[1]
    low = jnp.where(column < 0, -1, column & (LANES - 1))
    high = lax.shift_right_logical(column, 7)
    hot = jnp.where(iota((LANES, count), 0) == low, 1.0, 0.0).astype(BF16)
    found = jnp.dot(table, jnp.concatenate([hot] * 3, axis=0), preferred_element_type=F32)
    total = jnp.zeros((rows, count), F32)
    for block in range(table.shape[0] // rows):
        total += jnp.where(high == block, found[block * rows : (block + 1) * rows], 0.0)
    return total


def first_kernel(stars_dev, cap, *refs):
    sources, (request_ref, star_ref, table_ref), targets, sems = refs[:7], refs[7:10], refs[10:17], refs[17]
    copies = [pltpu.make_async_copy(*pair, sems.at[i]) for i, pair in enumerate(zip(sources, targets))]
    for copy in copies:
        copy.start()
    for copy in copies[:3]:
        copy.wait()
    sort_requests(stars_dev, cap, *targets[:3], request_ref)
    for copy in copies[3:]:
        copy.wait()
    predict(*targets[3:], star_ref, table_ref)


def sort_requests(stars_dev, cap, active_ref, length_ref, listed_ref, out_ref):
    targets, slots = listed_ref.shape
    devices = lax.axis_size("stars")
    listed = listed_ref[...]
    owner = listed // stars_dev if stars_dev & (stars_dev - 1) else lax.shift_right_logical(listed, stars_dev.bit_length() - 1)
    local = listed - owner * stars_dev
    low = (local & (LANES - 1)).astype(F32)
    high = lax.shift_right_logical(local, 7).astype(F32)
    lane = iota((devices, LANES), 1)
    row = iota((devices, LANES), 0)
    before = jnp.where(iota((slots, 2 * LANES), 0) < iota((slots, 2 * LANES), 1), 1.0, 0.0).astype(BF16)
    mine = [
        jnp.where((owner[k : k + 1] == row) & (lane < length_ref[k]), 1.0, 0.0) for k in range(targets)
    ]
    counts = jnp.dot(jnp.concatenate(mine, axis=0).astype(BF16), before, preferred_element_type=F32)
    base = jnp.zeros((devices, LANES), F32)
    order = iota((LANES, slots), 0).astype(F32)
    lows, highs, hots = [], [], []
    place = lane - part_of(row)
    begins = jnp.zeros((devices, LANES), F32)
    for k in range(targets):
        ahead = counts[k * devices : (k + 1) * devices]
        rank = jnp.sum(mine[k] * (ahead[:, :LANES] + base), axis=0, keepdims=True)
        hots.append(jnp.where(order == rank, 1.0, 0.0).astype(BF16))
        lows.append((mine[k] * low[k : k + 1]).astype(BF16))
        highs.append((mine[k] * high[k : k + 1]).astype(BF16))
        base = base + ahead[:, LANES:]
        begins = jnp.where(place == LANES // 2 + k * PARTS, base, begins)
    planes = jnp.concatenate([jnp.concatenate(lows, axis=1), jnp.concatenate(highs, axis=1)], axis=0)
    placed = lax.dot_general(
        planes, jnp.concatenate(hots, axis=1), (((1,), (1,)), ((), ())), preferred_element_type=F32
    )
    packed = (placed[:devices] + LANES * placed[devices:]).astype(I32)
    per_row = min(LANES // cap, PARTS)
    alone = packed
    for i in range(1, per_row):
        packed = jnp.where(lane >= i * cap, turn(pltpu.roll(alone, devices - 2 * i, 0), i * cap), packed)
    lane1 = iota((1, LANES), 1)
    actives = jnp.zeros((1, LANES), I32)
    for k in range(targets):
        actives = jnp.where((lane1 < LANES // 2) & (lane1 % targets == k), active_ref[k], actives)
    size = 2 * PARTS
    height = size * (PARTS // per_row + 1)
    for first in range(0, devices, size):
        blocks = []
        for core in range(2):
            begin = jnp.where((row[:size] & 1) == core, begins[first : first + size], 0.0)
            begin = jnp.sum(begin, axis=0, keepdims=True).astype(I32)
            rows = [packed[first + at + core : first + at + core + 1] for at in range(0, size, 2 * per_row)]
            blocks += [*rows, begin + actives]
        at = first // size * height
        out_ref[at : at + height] = jnp.concatenate(blocks * PARTS, axis=0)


def predict(state_ref, force_ref, mass_ref, elapsed_ref, star_ref, table_ref):
    for block in range(mass_ref.shape[0]):
        cols = slice(block * LANES, (block + 1) * LANES)
        state, force = state_ref[:, cols], force_ref[:, cols]
        mass, step = mass_ref[block : block + 1], elapsed_ref[block : block + 1]
        accel, jerk = force[0:3], force[3:6]
        position = state[0:3] + step * (state[3:6] + step * (0.5 * accel + step * jerk / 6.0))
        velocity = state[3:6] + step * (accel + 0.5 * step * jerk)
        stars = jnp.concatenate([position, velocity, mass, step], axis=0)
        star_ref[:, cols] = stars
        rows = jnp.concatenate([stars, force, jnp.zeros((2, LANES), F32)], axis=0)
        table_ref[block * 16 : (block + 1) * 16] = split3(rows)


def own_kernel(stars_dev, targets, request_ref, table_ref, out_ref):
    devices = out_ref.shape[0] // sent_rows(out_ref)
    lines = devices // PARTS
    width = request_ref.shape[0] // devices
    lane, row = iota((devices, LANES), 1), iota((devices, LANES), 0)
    ids = request_ref[pl.ds(width - 1, devices, stride=width), :]
    ids = ids.astype(F32)
    ids = jnp.where(lane < LANES // 2, ids, turn(ids, LANES // 2))
    per_tile = LANES // targets
    tiles = devices // per_tile
    start = (part_of(row) * lines + line_of(row)) * targets
    flat = []
    for t in range(tiles):
        offset = lane + t * LANES - start
        here = (offset >= 0) & (offset < targets)
        flat.append(jnp.sum(jnp.where(here, ids, 0.0), axis=0, keepdims=True))
    local = jnp.concatenate(flat, axis=1).astype(I32) - lax.axis_index("stars") * stars_dev
    local = jnp.where((local >= 0) & (local < stars_dev), local, -1)
    own = pick(table_ref[...], local, 16)
    words = own[7:14]
    own = own[0:8]
    span = lines * targets
    last = 6 * span
    fold = folding(targets)
    lane, row = iota((per_tile, LANES), 1), iota((per_tile, LANES), 0)
    on_row = (lane >= row * targets) & (lane < (row + 1) * targets)
    lane1 = iota((1, LANES), 1)
    rows = sent_rows(out_ref)
    backs = []
    for t in range(tiles):
        tile = words[:, t * LANES : (t + 1) * LANES]
        spread = jnp.concatenate([jnp.where(on_row, tile[c : c + 1], 0.0) for c in range(7)], axis=0)
        folded = jnp.dot(split3(spread), fold, preferred_element_type=F32)
        back = jnp.zeros((per_tile, LANES), F32)
        for c in range(7):
            begin = last % LANES + c * targets
            here = (lane >= begin) & (lane < begin + targets)
            back = jnp.where(here, folded[c * per_tile : (c + 1) * per_tile], back)
        backs.append(back)
    piece = min(span, LANES)
    turned = {}
    for part in range(PARTS):
        group = [jnp.zeros((1, LANES), F32) for _ in range(rows)]
        for at in range(0, span, piece):
            tile, source = divmod(part * span + at, LANES)
            for c in range(6):
                to, begin = divmod(c * span + at, LANES)
                shift = (begin - source) % LANES
                if (tile, shift) not in turned:
                    turned[tile, shift] = turn(own[:, tile * LANES : (tile + 1) * LANES], shift)
                here = (lane1 >= begin) & (lane1 < begin + piece)
                group[to] = jnp.where(here, turned[tile, shift][c : c + 1], group[to])
        for line in range(lines):
            at = device_at(line, part) * rows
            for r in range(rows - 1):
                out_ref[at + r : at + r + 1] = group[r]
            tile, source = divmod(part * span + line * targets, LANES)
            block = source // targets
            out_ref[at + rows - 1 : at + rows] = group[rows - 1] + backs[tile][block : block + 1]


def sent_rows(ref):
    return ref.shape[0] // lax.axis_size("stars")


def listed_kernel(cap, targets, request_ref, *refs):
    star_refs, (all_ref, listed_ref, slot_ref, table_ref) = refs[:PARTS], refs[PARTS:]
    blocks = star_refs[0].shape[1] // LANES
    mine = part_of(lax.axis_index("stars"))
    for mask, star_ref in zip((0, *(3, 2, 1)), star_refs):
        stars = star_ref[...]
        all_ref[mask * 8 : (mask + 1) * 8] = stars
        first = (mine ^ mask) * (blocks * 8)
        for pair in range(blocks // 2):
            tiles = [stars[:, (2 * pair + i) * LANES : (2 * pair + i + 1) * LANES] for i in range(2)]
            start = pl.multiple_of(first + pair * 16, 16)
            table_ref[pl.ds(start, 16), :] = split3(jnp.concatenate(tiles, axis=0))
    devices = lax.axis_size("stars")
    lines = devices // PARTS
    width = request_ref.shape[0] // devices
    rows = width - 1
    per_row = PARTS // rows
    at = [device_at(line, mine) * width for line in range(lines)]
    begins = jnp.concatenate([request_ref[pl.ds(first + rows, 1), :] for first in at], axis=0)
    lane = iota((lines, LANES), 1)
    for j in range(rows):
        slot = jnp.zeros((lines, LANES), I32)
        for k in range(1, targets + 1):
            for i in range(per_row):
                column = LANES // 2 + (k - 1) * PARTS + j * per_row + i
                begin = begins[:, column : column + 1]
                here = (lane >= begin + i * cap) & (lane >= i * cap) & (lane < (i + 1) * cap)
                slot += jnp.where(here, 1, 0)
        slot_ref[j * lines : (j + 1) * lines] = slot
    lane = iota((1, LANES), 1)
    lane8 = iota((8, LANES), 1)
    for j in range(rows):
        asked = [request_ref[pl.ds(first + j, 1), :] for first in at]
        found = []
        for i in range(per_row):
            columns = []
            for chunk in range(lines // per_row):
                column = asked[chunk * per_row]
                column = turn(column, -i * cap)
                for b in range(1, per_row):
                    column = jnp.where(lane >= b * cap, turn(asked[chunk * per_row + b], (b - i) * cap), column)
                columns.append(column)
            size = blocks * 8
            table = table_ref[(j * per_row + i) * size : (j * per_row + i + 1) * size]
            found.append(pick(table, jnp.concatenate(columns, axis=1)))
        for line in range(lines):
            chunk, b = divmod(line, per_row)
            cols = slice(chunk * LANES, (chunk + 1) * LANES)
            near = turn(found[0][:, cols], -b * cap)
            for i in range(1, per_row):
                near = jnp.where(lane8 >= i * cap, turn(found[i][:, cols], (i - b) * cap), near)
            listed_ref[(j * lines + line) * 8 : (j * lines + line + 1) * 8] = near


def pair_sums(target, source, mass, softening, sums):
    x, y, z = (source[c] - target[c] for c in range(3))
    u, v, w = (source[c] - target[c] for c in range(3, 6))
    inverse = lax.rsqrt(x * x + y * y + z * z + softening)
    square = inverse * inverse
    strength = mass * inverse * square
    radial = (x * u + y * v + z * w) * (3.0 * square)
    return (
        sums[0] + strength * x,
        sums[1] + strength * y,
        sums[2] + strength * z,
        sums[3] + strength * (u - radial * x),
        sums[4] + strength * (v - radial * y),
        sums[5] + strength * (w - radial * z),
    )


def force_kernel(
    softening, targets, group_step, core, masks, sent_ref, all_ref, listed_ref, slot_ref, out_ref, *kept_refs
):
    devices = lax.axis_size("stars")
    lines = devices // PARTS
    span = lines * targets
    rows = sent_ref.shape[0] // devices
    height = math.lcm(rows, 8)
    sent = sent_ref[0:height]
    for i in range(1, sent_ref.shape[0] // height):
        sent = sent + sent_ref[i * height : (i + 1) * height]
    block = sent[0:rows]
    for i in range(1, height // rows):
        block = block + sent[i * rows : (i + 1) * rows]
    target_ref = kept_refs[-1]
    for kept_ref in kept_refs[:-1]:
        kept_ref[0:rows] = block
        kept_ref[rows:] = jnp.zeros((kept_ref.shape[0] - rows, LANES), F32)
    piece = min(span, LANES)
    for at in range(0, span, piece):
        places = [divmod(c * span + at, LANES) for c in range(6)]
        tile = [turn(block[r : r + 1], -begin) for r, begin in places]
        tile = jnp.concatenate([*tile, jnp.zeros((2, LANES), F32)], axis=0).T
        target_ref[at : at + piece, 0:8] = tile[0:piece]
    me = lax.axis_index("stars")
    side, place = (me + core) & 1, me // (2 * PARTS)
    lane, row = iota((8, LANES), 1), iota((8, LANES), 0)
    zeros = (jnp.zeros((8, LANES), F32),) * 6
    for first in range(0, len(masks), group_step):
        groups = [2 * (place ^ mask) + side for mask in masks[first : first + group_step]]
        held = []
        for group in groups:
            tile = target_ref[pl.ds(pl.multiple_of(group * targets, 8), 8), 0:8]
            held.append([jnp.broadcast_to(tile[:, c : c + 1], (8, LANES)) for c in range(6)])

        def add_stars(part, sums, held=held):
            for s in range(all_ref.shape[1] // LANES):
                tile = all_ref[pl.ds(pl.multiple_of(part * 8, 8), 8), s * LANES : (s + 1) * LANES]
                source = [jnp.broadcast_to(tile[c : c + 1], (8, LANES)) for c in range(7)]
                sums = tuple(pair_sums(held[n], source, source[6], softening, sums[n]) for n in range(len(held)))
            return sums

        sums = lax.fori_loop(0, PARTS, add_stars, (zeros,) * len(held))
        for n, group in enumerate(groups):
            irregular = zeros
            for j in range(slot_ref.shape[0] // lines):
                at = j * lines + group
                near = listed_ref[pl.ds(pl.multiple_of(at * 8, 8), 8), :]
                mass = jnp.where(slot_ref[pl.ds(at, 1), :] == row, near[6:7], 0.0)
                irregular = pair_sums(held[n], [near[c : c + 1] for c in range(6)], mass, softening, irregular)
            result = zeros[0]
            for c, values in enumerate(sums[n] + irregular):
                value = jnp.sum(values, axis=1, keepdims=True)
                result = jnp.where(lane == c * targets + row, value, result)
            out_ref[first + n : first + n + 1] = jnp.sum(result, axis=0, keepdims=True)


def share_kernel(mine_ref, partner_ref, *out_refs):
    for n, out_ref in enumerate(out_refs):
        out_ref[...] = mine_ref[n : n + 1] + partner_ref[n + 1 : n + 2]


def correct_kernel(targets, kept_ref, mine_ref, partner_ref, *refs):
    sums_refs, (state_ref, forces_ref, terms_ref) = refs[:-3], refs[-3:]
    lines = 2 * (len(sums_refs) + 1)
    span = lines * targets
    total = mine_ref[0:1] + partner_ref[0:1]
    for sums_ref in sums_refs:
        total = total + sums_ref[...]
    kept = kept_ref[...]
    piece = min(span, LANES)
    at = line_of(lax.axis_index("stars")) * targets
    moved = pltpu.roll(kept, (LANES - at % piece) % LANES, 1)
    lane, row = iota((16, LANES), 1), iota((16, LANES), 0)
    on_row = (lane >= row * targets) & (lane < (row + 1) * targets)
    lane1 = iota((1, LANES), 1)
    spread = [jnp.where(on_row, total, 0.0)]
    for c in range(6):
        r, begin = divmod(c * span, LANES)
        value = moved[r : r + 1]
        for q in range(1, span // piece):
            value = jnp.where(at // piece == q, moved[r + q : r + q + 1], value)
        spread.append(jnp.where((lane1 >= begin) & (lane1 < begin + targets), value, 0.0))
    for c in range(7):
        r, begin = divmod(6 * span + c * targets, LANES)
        spread.append(jnp.where((lane1 >= begin) & (lane1 < begin + targets), kept[r : r + 1], 0.0))
    spread.append(jnp.zeros((3, LANES), F32))
    rows = jnp.dot(split3(jnp.concatenate(spread, axis=0)), folding(targets), preferred_element_type=F32)[:, 0:targets]
    accel, jerk, irregular = rows[0:3], rows[3:6], rows[6:12]
    position, velocity, step = rows[16:19], rows[19:22], rows[22:23]
    old_accel, old_jerk = rows[23:26], rows[26:29]
    change = accel - old_accel
    second = 3.0 * change - step * (2.0 * old_jerk + jerk)
    third = -2.0 * change + step * (old_jerk + jerk)
    state_ref[0:3] = position + step * step * (second / 12.0 + third / 20.0)
    state_ref[3:6] = velocity + step * (second / 3.0 + third / 4.0)
    forces = jnp.concatenate([irregular, rows[0:6] - irregular, jnp.zeros((4, targets), F32)], axis=0)
    forces_ref[...] = forces.T[:, 0:12]
    terms_ref[0:3] = second
    terms_ref[3:6] = third


def exchange(rows, devices):
    wide = rows.reshape(devices, 1, -1)
    return lax.all_to_all(wide, "stars", 0, 0, tiled=True).reshape(rows.shape)


def per_device(star_state, old_force, star_mass, elapsed, active_ids, neighbours, list_length):
    stars_dev = star_state.shape[1]
    devices = lax.axis_size("stars")
    lines = devices // PARTS
    targets, slots = neighbours.shape
    cap = 2 * targets * slots // devices
    blocks = stars_dev // LANES
    request_rows = max(1, PARTS * cap // LANES)
    back_rows = -(-(6 * lines + 7) * targets // LANES)
    softening = 0.25 * math.sqrt(slots) / (stars_dev * devices)

    def shape(*dims, dtype=F32):
        return jax.ShapeDtypeStruct(dims, dtype)

    def cost(flops):
        return pl.CostEstimate(flops=flops, bytes_accessed=1 << 20, transcendentals=0)

    def swap(value, mask):
        return lax.ppermute(value, "stars", [(i, i ^ mask) for i in range(devices)])

    given = (
        active_ids,
        list_length,
        neighbours,
        star_state,
        old_force,
        star_mass.reshape(blocks, LANES),
        elapsed.reshape(blocks, LANES),
    )
    request, stars, table = pl.pallas_call(
        functools.partial(first_kernel, stars_dev, cap),
        out_shape=(
            shape(devices * (request_rows + 1), LANES, dtype=I32),
            pltpu.VMEM((8, stars_dev), F32),
            pltpu.VMEM((blocks * 16, 3 * LANES), BF16),
        ),
        in_specs=[HBM] * 7,
        out_specs=(VMEM,) * 3,
        scratch_shapes=[
            pltpu.SMEM((targets,), I32),
            pltpu.SMEM((targets,), I32),
            *(pltpu.VMEM(value.shape, value.dtype) for value in given[2:]),
            pltpu.SemaphoreType.DMA((7,)),
        ],
        compiler_params=PARAMS,
    )(*(pltpu.with_memory_space_constraint(value, pltpu.HBM) for value in given))
    asked = exchange(request, devices)
    shared = [stars, *(swap(stars, 2 * mask) for mask in (3, 2, 1))]
    sent = pl.pallas_call(
        functools.partial(own_kernel, stars_dev, targets),
        out_shape=shape(devices * back_rows, LANES),
        in_specs=[VMEM] * 2,
        out_specs=VMEM,
        compiler_params=PARAMS,
    )(asked, table)
    sent = exchange(sent, devices)
    every, listed, slot = pl.pallas_call(
        functools.partial(listed_kernel, cap, targets),
        out_shape=(
            shape(PARTS * 8, stars_dev),
            shape(lines * request_rows * 8, LANES),
            shape(lines * request_rows, LANES, dtype=I32),
        ),
        in_specs=[VMEM] * (1 + PARTS),
        out_specs=(VMEM,) * 3,
        scratch_shapes=[pltpu.VMEM((PARTS * blocks * 8, 3 * LANES), BF16)],
        compiler_params=PARAMS,
        cost_estimate=cost(1 << 24),
    )(asked, *shared)
    kept_rows = -(-back_rows // 8) * 8

    places = lines // 2

    def forces_of(core, masks, *kept):
        return pl.pallas_call(
            functools.partial(force_kernel, softening, targets, 4, core, masks),
            out_shape=(shape(-(-len(masks) // 8) * 8, LANES), *kept),
            in_specs=[VMEM] * 4,
            out_specs=(VMEM,) * (1 + len(kept)),
            scratch_shapes=[pltpu.VMEM((lines * targets, LANES), F32)],
            compiler_params=PARAMS,
        )(sent, every, listed, slot)

    (theirs,) = forces_of(1, range(places))
    (others,) = forces_of(0, range(1, places))
    theirs = swap(theirs, 1)
    sums = pl.pallas_call(
        share_kernel,
        out_shape=(shape(1, LANES),) * (places - 1),
        in_specs=[VMEM] * 2,
        out_specs=(VMEM,) * (places - 1),
        compiler_params=PARAMS,
    )(others, theirs)
    sums = [swap(sums[mask - 1], mask * 2 * PARTS) for mask in range(places - 1, 0, -1)]
    mine, kept = forces_of(0, range(1), shape(kept_rows, LANES))
    state, forces, terms = pl.pallas_call(
        functools.partial(correct_kernel, targets),
        out_shape=(shape(6, targets), shape(targets, 12), shape(6, targets)),
        in_specs=[VMEM] * (2 + places),
        out_specs=(VMEM,) * 3,
        compiler_params=PARAMS,
    )(kept, mine, theirs, *sums)
    return state, forces.T, terms


def solution(mesh):
    placed = (
        P(None, "stars"),
        P(None, "stars"),
        P("stars"),
        P("stars"),
        P("stars"),
        P("stars", None),
        P("stars"),
    )
    return jax.shard_map(
        per_device,
        mesh=mesh,
        in_specs=placed,
        out_specs=(P(None, "stars"), P(None, "stars"), P(None, "stars")),
        check_vma=False,
    )
```

```python
import functools
import math

import jax
import jax.numpy as jnp
from jax import lax
from jax.experimental import pallas as pl
from jax.experimental.pallas import tpu as pltpu
from jax.sharding import PartitionSpec as P

LANES = 128
PARTS = 4
F32 = jnp.float32
I32 = jnp.int32
BF16 = jnp.bfloat16
VMEM = pl.BlockSpec(memory_space=pltpu.VMEM)
HBM = pl.BlockSpec(memory_space=pltpu.HBM)
PARAMS = pltpu.CompilerParams(vmem_limit_bytes=32 * 1024 * 1024)


def iota(shape, axis):
    return lax.broadcasted_iota(I32, shape, axis)


def part_of(device):
    return (device >> 1) & (PARTS - 1)


def line_of(device):
    return (device >> 3) * 2 + (device & 1)


def device_at(line, part):
    return (line >> 1) * 2 * PARTS + part * 2 + (line & 1)


def turn(value, lanes):
    lanes %= LANES
    return pltpu.roll(value, lanes, 1) if lanes else value


def split3(value):
    high = value.astype(BF16)
    rest = value - high.astype(F32)
    middle = rest.astype(BF16)
    low = (rest - middle.astype(F32)).astype(BF16)
    return jnp.concatenate([high, middle, low], axis=1)


def pick(table, column, rows=8):
    count = column.shape[1]
    low = jnp.where(column < 0, -1, column & (LANES - 1))
    high = lax.shift_right_logical(column, 7)
    hot = jnp.where(iota((LANES, count), 0) == low, 1.0, 0.0).astype(BF16)
    found = jnp.dot(table, jnp.concatenate([hot] * 3, axis=0), preferred_element_type=F32)
    level = [found[first : first + rows] for first in range(0, table.shape[0], rows)]
    bit = 1
    while len(level) > 1:
        odd = (high & bit) != 0
        level = [
            jnp.where(odd, level[i + 1], level[i]) if i + 1 < len(level) else level[i] for i in range(0, len(level), 2)
        ]
        bit *= 2
    return level[0]


def first_kernel(stars_dev, cap, *refs):
    sources, (request_ref, star_ref, table_ref), targets, sems = refs[:7], refs[7:10], refs[10:17], refs[17]
    copies = [pltpu.make_async_copy(*pair, sems.at[i]) for i, pair in enumerate(zip(sources, targets))]
    for copy in copies:
        copy.start()
    for copy in copies[:3]:
        copy.wait()
    sort_requests(stars_dev, cap, *targets[:3], request_ref)
    for copy in copies[3:]:
        copy.wait()
    predict(*targets[3:], star_ref, table_ref)


def sort_requests(stars_dev, cap, active_ref, length_ref, listed_ref, out_ref):
    targets, slots = listed_ref.shape
    devices = lax.axis_size("stars")
    listed = listed_ref[...]
    owner = listed // stars_dev if stars_dev & (stars_dev - 1) else lax.shift_right_logical(listed, stars_dev.bit_length() - 1)
    local = listed - owner * stars_dev
    low = (local & (LANES - 1)).astype(F32)
    high = lax.shift_right_logical(local, 7).astype(F32)
    lane = iota((devices, LANES), 1)
    row = iota((devices, LANES), 0)
    before = jnp.where(iota((slots, 2 * LANES), 0) < iota((slots, 2 * LANES), 1), 1.0, 0.0).astype(BF16)
    mine = [
        jnp.where((owner[k : k + 1] == row) & (lane < length_ref[k]), 1.0, 0.0) for k in range(targets)
    ]
    counts = jnp.dot(jnp.concatenate(mine, axis=0).astype(BF16), before, preferred_element_type=F32)
    base = jnp.zeros((devices, LANES), F32)
    order = iota((LANES, slots), 0).astype(F32)
    lows, highs, hots = [], [], []
    place = lane - part_of(row)
    begins = jnp.zeros((devices, LANES), F32)
    for k in range(targets):
        ahead = counts[k * devices : (k + 1) * devices]
        rank = jnp.sum(mine[k] * (ahead[:, :LANES] + base), axis=0, keepdims=True)
        hots.append(jnp.where(order == rank, 1.0, 0.0).astype(BF16))
        lows.append((mine[k] * low[k : k + 1]).astype(BF16))
        highs.append((mine[k] * high[k : k + 1]).astype(BF16))
        base = base + ahead[:, LANES:]
        begins = jnp.where(place == LANES // 2 + k * PARTS, base, begins)
    planes = jnp.concatenate([jnp.concatenate(lows, axis=1), jnp.concatenate(highs, axis=1)], axis=0)
    placed = lax.dot_general(
        planes, jnp.concatenate(hots, axis=1), (((1,), (1,)), ((), ())), preferred_element_type=F32
    )
    packed = (placed[:devices] + LANES * placed[devices:]).astype(I32)
    per_row = min(LANES // cap, PARTS)
    alone = packed
    for i in range(1, per_row):
        packed = jnp.where(lane >= i * cap, turn(pltpu.roll(alone, devices - 2 * i, 0), i * cap), packed)
    lane1 = iota((1, LANES), 1)
    actives = jnp.zeros((1, LANES), I32)
    for k in range(targets):
        actives = jnp.where((lane1 < LANES // 2) & (lane1 % targets == k), active_ref[k], actives)
    size = 2 * PARTS
    height = size * (PARTS // per_row + 1)
    for first in range(0, devices, size):
        blocks = []
        for core in range(2):
            begin = jnp.where((row[:size] & 1) == core, begins[first : first + size], 0.0)
            begin = jnp.sum(begin, axis=0, keepdims=True).astype(I32)
            rows = [packed[first + at + core : first + at + core + 1] for at in range(0, size, 2 * per_row)]
            blocks += [*rows, begin + actives]
        at = first // size * height
        out_ref[at : at + height] = jnp.concatenate(blocks * PARTS, axis=0)


def predict(state_ref, force_ref, mass_ref, elapsed_ref, star_ref, table_ref):
    for block in range(mass_ref.shape[0]):
        cols = slice(block * LANES, (block + 1) * LANES)
        state, force = state_ref[:, cols], force_ref[:, cols]
        mass, step = mass_ref[block : block + 1], elapsed_ref[block : block + 1]
        accel, jerk = force[0:3], force[3:6]
        position = state[0:3] + step * (state[3:6] + step * (0.5 * accel + step * jerk / 6.0))
        velocity = state[3:6] + step * (accel + 0.5 * step * jerk)
        stars = jnp.concatenate([position, velocity, mass, step], axis=0)
        star_ref[:, cols] = stars
        rows = jnp.concatenate([stars, force, jnp.zeros((2, LANES), F32)], axis=0)
        table_ref[block * 16 : (block + 1) * 16] = split3(rows)


def own_kernel(stars_dev, targets, request_ref, table_ref, out_ref):
    devices = out_ref.shape[0] // sent_rows(out_ref)
    lines = devices // PARTS
    width = request_ref.shape[0] // devices
    lane, row = iota((devices, LANES), 1), iota((devices, LANES), 0)
    ids = request_ref[pl.ds(width - 1, devices, stride=width), :]
    ids = ids.astype(F32)
    ids = jnp.where(lane < LANES // 2, ids, turn(ids, LANES // 2))
    per_tile = LANES // targets
    tiles = devices // per_tile
    start = (part_of(row) * lines + line_of(row)) * targets
    flat = []
    for t in range(tiles):
        offset = lane + t * LANES - start
        here = (offset >= 0) & (offset < targets)
        flat.append(jnp.sum(jnp.where(here, ids, 0.0), axis=0, keepdims=True))
    local = jnp.concatenate(flat, axis=1).astype(I32) - lax.axis_index("stars") * stars_dev
    local = jnp.where((local >= 0) & (local < stars_dev), local, -1)
    own = pick(table_ref[...], local, 16)
    words = own[7:15]
    own = own[0:8]
    span = lines * targets
    last = 6 * span
    lane = iota((per_tile, LANES), 1)
    lane1 = iota((1, LANES), 1)
    rows = sent_rows(out_ref)
    backs = []
    for t in range(tiles):
        back = jnp.zeros((per_tile, LANES), F32)
        tile = pltpu.roll(words[:, t * LANES : (t + 1) * LANES], targets, 1, stride=targets, stride_axis=0)
        tile = turn(tile, last)
        for c in range(7):
            begin = last % LANES + c * targets
            here = (lane >= begin) & (lane < begin + targets)
            spread = jnp.broadcast_to(tile[c : c + 1], (per_tile, LANES))
            back = jnp.where(here, pltpu.roll(spread, 0, 1, stride=targets, stride_axis=0), back)
        backs.append(back)
    piece = min(span, LANES)
    turned = {}
    for part in range(PARTS):
        group = [jnp.zeros((1, LANES), F32) for _ in range(rows)]
        for at in range(0, span, piece):
            tile, source = divmod(part * span + at, LANES)
            for c in range(6):
                to, begin = divmod(c * span + at, LANES)
                shift = (begin - source) % LANES
                if (tile, shift) not in turned:
                    turned[tile, shift] = turn(own[:, tile * LANES : (tile + 1) * LANES], shift)
                here = (lane1 >= begin) & (lane1 < begin + piece)
                group[to] = jnp.where(here, turned[tile, shift][c : c + 1], group[to])
        for line in range(lines):
            at = device_at(line, part) * rows
            for r in range(rows - 1):
                out_ref[at + r : at + r + 1] = group[r]
            tile, source = divmod(part * span + line * targets, LANES)
            block = per_tile - 1 - source // targets
            out_ref[at + rows - 1 : at + rows] = group[rows - 1] + backs[tile][block : block + 1]


def sent_rows(ref):
    return ref.shape[0] // lax.axis_size("stars")


def listed_kernel(cap, targets, request_ref, *refs):
    star_refs, (all_ref, listed_ref, slot_ref, table_ref) = refs[:PARTS], refs[PARTS:]
    blocks = star_refs[0].shape[1] // LANES
    mine = part_of(lax.axis_index("stars"))
    for mask, star_ref in zip((0, *(3, 2, 1)), star_refs):
        stars = star_ref[...]
        all_ref[mask * 8 : (mask + 1) * 8] = stars
        first = (mine ^ mask) * (blocks * 8)
        for pair in range(blocks // 2):
            tiles = [stars[:, (2 * pair + i) * LANES : (2 * pair + i + 1) * LANES] for i in range(2)]
            start = pl.multiple_of(first + pair * 16, 16)
            table_ref[pl.ds(start, 16), :] = split3(jnp.concatenate(tiles, axis=0))
    devices = lax.axis_size("stars")
    lines = devices // PARTS
    width = request_ref.shape[0] // devices
    rows = width - 1
    per_row = PARTS // rows
    at = [device_at(line, mine) * width for line in range(lines)]
    begins = jnp.concatenate([request_ref[pl.ds(first + rows, 1), :] for first in at], axis=0)
    lane = iota((lines, LANES), 1)
    for j in range(rows):
        slot = jnp.zeros((lines, LANES), I32)
        for k in range(1, targets + 1):
            for i in range(per_row):
                column = LANES // 2 + (k - 1) * PARTS + j * per_row + i
                begin = begins[:, column : column + 1]
                here = (lane >= begin + i * cap) & (lane >= i * cap) & (lane < (i + 1) * cap)
                slot += jnp.where(here, 1, 0)
        slot_ref[j * lines : (j + 1) * lines] = slot
    lane = iota((1, LANES), 1)
    lane8 = iota((8, LANES), 1)
    for j in range(rows):
        asked = [request_ref[pl.ds(first + j, 1), :] for first in at]
        found = []
        for i in range(per_row):
            columns = []
            for chunk in range(lines // per_row):
                column = asked[chunk * per_row]
                column = turn(column, -i * cap)
                for b in range(1, per_row):
                    column = jnp.where(lane >= b * cap, turn(asked[chunk * per_row + b], (b - i) * cap), column)
                columns.append(column)
            size = blocks * 8
            table = table_ref[(j * per_row + i) * size : (j * per_row + i + 1) * size]
            found.append(pick(table, jnp.concatenate(columns, axis=1)))
        for line in range(lines):
            chunk, b = divmod(line, per_row)
            cols = slice(chunk * LANES, (chunk + 1) * LANES)
            near = turn(found[0][:, cols], -b * cap)
            for i in range(1, per_row):
                near = jnp.where(lane8 >= i * cap, turn(found[i][:, cols], (i - b) * cap), near)
            listed_ref[(j * lines + line) * 8 : (j * lines + line + 1) * 8] = near


def pair_sums(target, source, mass, softening, sums):
    x, y, z = (source[c] - target[c] for c in range(3))
    u, v, w = (source[c] - target[c] for c in range(3, 6))
    inverse = lax.rsqrt(x * x + y * y + z * z + softening)
    square = inverse * inverse
    strength = mass * inverse * square
    radial = (x * u + y * v + z * w) * (3.0 * square)
    return (
        sums[0] + strength * x,
        sums[1] + strength * y,
        sums[2] + strength * z,
        sums[3] + strength * (u - radial * x),
        sums[4] + strength * (v - radial * y),
        sums[5] + strength * (w - radial * z),
    )


def add_sent(sent_ref, kept_ref, target_ref):
    devices = lax.axis_size("stars")
    span = target_ref.shape[0]
    rows = sent_ref.shape[0] // devices
    height = math.lcm(rows, 8)
    sent = sent_ref[0:height]
    for i in range(1, sent_ref.shape[0] // height):
        sent = sent + sent_ref[i * height : (i + 1) * height]
    block = sent[0:rows]
    for i in range(1, height // rows):
        block = block + sent[i * rows : (i + 1) * rows]
    kept_ref[...] = jnp.zeros(kept_ref.shape, F32)
    kept_ref[0:rows] = block
    piece = min(span, LANES)
    for at in range(0, span, piece):
        places = [divmod(c * span + at, LANES) for c in range(6)]
        tile = [turn(block[r : r + 1], -begin) for r, begin in places]
        tile = jnp.concatenate([*tile, jnp.zeros((2, LANES), F32)], axis=0).T
        target_ref[at : at + piece, 0:8] = tile[0:piece]


def first_force_kernel(softening, targets, group_step, core, masks, sent_ref, all_ref, listed_ref, slot_ref, out_ref, kept_ref, target_ref):
    add_sent(sent_ref, kept_ref, target_ref)
    force_kernel(softening, targets, group_step, core, masks, target_ref, all_ref, listed_ref, slot_ref, out_ref)


def force_kernel(softening, targets, group_step, core, masks, target_ref, all_ref, listed_ref, slot_ref, out_ref):
    lines = lax.axis_size("stars") // PARTS
    me = lax.axis_index("stars")
    side, place = (me + core) & 1, me // (2 * PARTS)
    lane, row = iota((8, LANES), 1), iota((8, LANES), 0)
    zeros = (jnp.zeros((8, LANES), F32),) * 6
    for first in range(0, len(masks), group_step):
        groups = [2 * (place ^ mask) + side for mask in masks[first : first + group_step]]
        held = []
        for group in groups:
            tile = target_ref[pl.ds(pl.multiple_of(group * targets, 8), 8), 0:8]
            held.append([jnp.broadcast_to(tile[:, c : c + 1], (8, LANES)) for c in range(6)])

        def add_stars(part, sums, held=held):
            for s in range(all_ref.shape[1] // LANES):
                tile = all_ref[pl.ds(pl.multiple_of(part * 8, 8), 8), s * LANES : (s + 1) * LANES]
                source = [jnp.broadcast_to(tile[c : c + 1], (8, LANES)) for c in range(7)]
                sums = tuple(pair_sums(held[n], source, source[6], softening, sums[n]) for n in range(len(held)))
            return sums

        sums = lax.fori_loop(0, PARTS, add_stars, (zeros,) * len(held))
        for n, group in enumerate(groups):
            irregular = zeros
            for j in range(slot_ref.shape[0] // lines):
                at = j * lines + group
                near = listed_ref[pl.ds(pl.multiple_of(at * 8, 8), 8), :]
                mass = jnp.where(slot_ref[pl.ds(at, 1), :] == row, near[6:7], 0.0)
                irregular = pair_sums(held[n], [near[c : c + 1] for c in range(6)], mass, softening, irregular)
            result = zeros[0]
            for c, values in enumerate(sums[n] + irregular):
                value = jnp.sum(values, axis=1, keepdims=True)
                result = jnp.where(lane == -c * targets % LANES + row, value, result)
            out_ref[first + n : first + n + 1] = jnp.sum(result, axis=0, keepdims=True)


def share_kernel(mine_ref, partner_ref, *out_refs):
    for n, out_ref in enumerate(out_refs):
        out_ref[...] = mine_ref[n : n + 1] + partner_ref[n + 1 : n + 2]


def unfold(row, targets):
    wide = jnp.broadcast_to(row, (LANES // targets, LANES))
    return pltpu.roll(wide, 0, 1, stride=targets, stride_axis=0)[:, 0:targets]


def correct_kernel(targets, kept_ref, mine_ref, partner_ref, *refs):
    sums_refs, (state_ref, forces_ref, terms_ref) = refs[:-3], refs[-3:]
    lines = 2 * (len(sums_refs) + 1)
    span = lines * targets
    total = mine_ref[0:1] + partner_ref[0:1]
    for sums_ref in sums_refs:
        total = total + sums_ref[...]
    kept = kept_ref[...]
    piece = min(span, LANES)
    at = line_of(lax.axis_index("stars")) * targets
    moved = pltpu.roll(kept, (LANES - at % piece) % LANES, 1)
    turned = {}
    rows = []
    for c in range(6):
        r, begin = divmod(c * span, LANES)
        if begin not in turned:
            turned[begin] = turn(moved, -begin)
        value = turned[begin][r : r + 1]
        for q in range(1, span // piece):
            value = jnp.where(at // piece == q, turned[begin][r + q : r + q + 1], value)
        rows.append(value[:, 0:targets])
    position, velocity = jnp.concatenate(rows[0:3], axis=0), jnp.concatenate(rows[3:6], axis=0)
    r, begin = divmod(6 * span, LANES)
    words = unfold(turn(kept[r : r + 1], -begin), targets)
    step = words[0:1]
    old_accel = jnp.concatenate([words[-c : LANES // targets + 1 - c] for c in (1, 2, 3)], axis=0)
    old_jerk = jnp.concatenate([words[-c : LANES // targets + 1 - c] for c in (4, 5, 6)], axis=0)
    rows = unfold(total, targets)
    accel, jerk, irregular = rows[0:3], rows[3:6], rows[6:12]
    change = accel - old_accel
    second = 3.0 * change - step * (2.0 * old_jerk + jerk)
    third = -2.0 * change + step * (old_jerk + jerk)
    state_ref[0:3] = position + step * step * (second / 12.0 + third / 20.0)
    state_ref[3:6] = velocity + step * (second / 3.0 + third / 4.0)
    forces = jnp.concatenate([irregular, rows[0:6] - irregular, jnp.zeros((4, targets), F32)], axis=0)
    forces_ref[...] = forces.T[:, 0:12]
    terms_ref[0:3] = second
    terms_ref[3:6] = third


def exchange(rows, devices):
    wide = rows.reshape(devices, 1, -1)
    return lax.all_to_all(wide, "stars", 0, 0, tiled=True).reshape(rows.shape)


def per_device(star_state, old_force, star_mass, elapsed, active_ids, neighbours, list_length):
    stars_dev = star_state.shape[1]
    devices = lax.axis_size("stars")
    lines = devices // PARTS
    targets, slots = neighbours.shape
    cap = 2 * targets * slots // devices
    blocks = stars_dev // LANES
    request_rows = max(1, PARTS * cap // LANES)
    back_rows = -(-(6 * lines + 7) * targets // LANES)
    softening = 0.25 * math.sqrt(slots) / (stars_dev * devices)

    def shape(*dims, dtype=F32):
        return jax.ShapeDtypeStruct(dims, dtype)

    def cost(flops):
        return pl.CostEstimate(flops=flops, bytes_accessed=1 << 20, transcendentals=0)

    def swap(value, mask):
        return lax.ppermute(value, "stars", [(i, i ^ mask) for i in range(devices)])

    given = (
        active_ids,
        list_length,
        neighbours,
        star_state,
        old_force,
        star_mass.reshape(blocks, LANES),
        elapsed.reshape(blocks, LANES),
    )
    request, stars, table = pl.pallas_call(
        functools.partial(first_kernel, stars_dev, cap),
        out_shape=(
            shape(devices * (request_rows + 1), LANES, dtype=I32),
            pltpu.VMEM((8, stars_dev), F32),
            pltpu.VMEM((blocks * 16, 3 * LANES), BF16),
        ),
        in_specs=[HBM] * 7,
        out_specs=(VMEM,) * 3,
        scratch_shapes=[
            pltpu.SMEM((targets,), I32),
            pltpu.SMEM((targets,), I32),
            *(pltpu.VMEM(value.shape, value.dtype) for value in given[2:]),
            pltpu.SemaphoreType.DMA((7,)),
        ],
        compiler_params=PARAMS,
    )(*(pltpu.with_memory_space_constraint(value, pltpu.HBM) for value in given))
    asked = exchange(request, devices)
    shared = [stars, *(swap(stars, 2 * mask) for mask in (3, 2, 1))]
    sent = pl.pallas_call(
        functools.partial(own_kernel, stars_dev, targets),
        out_shape=shape(devices * back_rows, LANES),
        in_specs=[VMEM] * 2,
        out_specs=VMEM,
        compiler_params=PARAMS,
    )(asked, table)
    sent = exchange(sent, devices)
    every, listed, slot = pl.pallas_call(
        functools.partial(listed_kernel, cap, targets),
        out_shape=(
            shape(PARTS * 8, stars_dev),
            shape(lines * request_rows * 8, LANES),
            shape(lines * request_rows, LANES, dtype=I32),
        ),
        in_specs=[VMEM] * (1 + PARTS),
        out_specs=(VMEM,) * 3,
        scratch_shapes=[pltpu.VMEM((PARTS * blocks * 8, 3 * LANES), BF16)],
        compiler_params=PARAMS,
        cost_estimate=cost(1 << 24),
    )(asked, *shared)
    kept_rows = -(-back_rows // 8) * 8

    places = lines // 2

    def forces_of(kernel, core, masks, given, *kept):
        return pl.pallas_call(
            functools.partial(kernel, softening, targets, 4, core, masks),
            out_shape=(shape(-(-len(masks) // 8) * 8, LANES), *kept),
            in_specs=[VMEM] * 4,
            out_specs=(VMEM,) * (1 + len(kept)),
            compiler_params=PARAMS,
        )(given, every, listed, slot)

    theirs, kept, upright = forces_of(
        first_force_kernel, 1, range(places), sent, shape(kept_rows, LANES), shape(lines * targets, LANES)
    )
    (others,) = forces_of(force_kernel, 0, range(1, places), upright)
    theirs = swap(theirs, 1)
    sums = pl.pallas_call(
        share_kernel,
        out_shape=(shape(1, LANES),) * (places - 1),
        in_specs=[VMEM] * 2,
        out_specs=(VMEM,) * (places - 1),
        compiler_params=PARAMS,
    )(others, theirs)
    sums = [swap(sums[mask - 1], mask * 2 * PARTS) for mask in range(places - 1, 0, -1)]
    (mine,) = forces_of(force_kernel, 0, range(1), upright)
    state, forces, terms = pl.pallas_call(
        functools.partial(correct_kernel, targets),
        out_shape=(shape(6, targets), shape(targets, 12), shape(6, targets)),
        in_specs=[VMEM] * (2 + places),
        out_specs=(VMEM,) * 3,
        compiler_params=PARAMS,
    )(kept, mine, theirs, *sums)
    return state, forces.T, terms


def solution(mesh):
    placed = (
        P(None, "stars"),
        P(None, "stars"),
        P("stars"),
        P("stars"),
        P("stars"),
        P("stars", None),
        P("stars"),
    )
    return jax.shard_map(
        per_device,
        mesh=mesh,
        in_specs=placed,
        out_specs=(P(None, "stars"), P(None, "stars"), P(None, "stars")),
        check_vma=False,
    )
```

```python
import functools
import math

import jax
import jax.numpy as jnp
from jax import lax
from jax.experimental import pallas as pl
from jax.experimental.pallas import tpu as pltpu
from jax.sharding import PartitionSpec as P

LANES = 128
PARTS = 4
SPACING = 11
F32 = jnp.float32
I32 = jnp.int32
BF16 = jnp.bfloat16
VMEM = pl.BlockSpec(memory_space=pltpu.VMEM)
HBM = pl.BlockSpec(memory_space=pltpu.HBM)
PARAMS = pltpu.CompilerParams(vmem_limit_bytes=32 * 1024 * 1024)


def iota(shape, axis):
    return lax.broadcasted_iota(I32, shape, axis)


def part_of(device):
    return (device >> 1) & (PARTS - 1)


def line_of(device):
    return (device >> 3) * 2 + (device & 1)


def device_at(line, part):
    return (line >> 1) * 2 * PARTS + part * 2 + (line & 1)


def spaced(device, devices):
    return device * SPACING & (devices - 1)


def place_of(device, devices):
    return device * pow(SPACING, -1, devices) & (devices - 1)


def turn(value, lanes):
    lanes %= LANES
    return pltpu.roll(value, lanes, 1) if lanes else value


def split3(value):
    high = value.astype(BF16)
    rest = value - high.astype(F32)
    middle = rest.astype(BF16)
    low = (rest - middle.astype(F32)).astype(BF16)
    return jnp.concatenate([high, middle, low], axis=1)


def pick(table, column, rows=8):
    count = column.shape[1]
    low = jnp.where(column < 0, -1, column & (LANES - 1))
    high = lax.shift_right_logical(column, 7)
    hot = jnp.where(iota((LANES, count), 0) == low, 1.0, 0.0).astype(BF16)
    found = jnp.dot(table, jnp.concatenate([hot] * 3, axis=0), preferred_element_type=F32)
    level = [found[first : first + rows] for first in range(0, table.shape[0], rows)]
    bit = 1
    while len(level) > 1:
        odd = (high & bit) != 0
        level = [
            jnp.where(odd, level[i + 1], level[i]) if i + 1 < len(level) else level[i] for i in range(0, len(level), 2)
        ]
        bit *= 2
    return level[0]


def first_kernel(stars_dev, cap, *refs):
    sources, (request_ref, star_ref, table_ref), targets, sems = refs[:7], refs[7:10], refs[10:17], refs[17]
    copies = [pltpu.make_async_copy(*pair, sems.at[i]) for i, pair in enumerate(zip(sources, targets))]
    for copy in copies:
        copy.start()
    for copy in copies[:3]:
        copy.wait()
    sort_requests(stars_dev, cap, *targets[:3], request_ref)
    for copy in copies[3:]:
        copy.wait()
    predict(*targets[3:], star_ref, table_ref)


def sort_requests(stars_dev, cap, active_ref, length_ref, listed_ref, out_ref):
    targets, slots = listed_ref.shape
    devices = lax.axis_size("stars")
    listed = listed_ref[...]
    owner = listed // stars_dev if stars_dev & (stars_dev - 1) else lax.shift_right_logical(listed, stars_dev.bit_length() - 1)
    local = listed - owner * stars_dev
    low = (local & (LANES - 1)).astype(F32)
    high = lax.shift_right_logical(local, 7).astype(F32)
    lane = iota((devices, LANES), 1)
    row = iota((devices, LANES), 0)
    before = jnp.where(iota((slots, 2 * LANES), 0) < iota((slots, 2 * LANES), 1), 1.0, 0.0).astype(BF16)
    mine = [
        jnp.where((owner[k : k + 1] == row) & (lane < length_ref[k]), 1.0, 0.0) for k in range(targets)
    ]
    counts = jnp.dot(jnp.concatenate(mine, axis=0).astype(BF16), before, preferred_element_type=F32)
    base = jnp.zeros((devices, LANES), F32)
    order = iota((LANES, slots), 0).astype(F32)
    lows, highs, hots = [], [], []
    place = lane - part_of(row)
    begins = jnp.zeros((devices, LANES), F32)
    for k in range(targets):
        ahead = counts[k * devices : (k + 1) * devices]
        rank = jnp.sum(mine[k] * (ahead[:, :LANES] + base), axis=0, keepdims=True)
        hots.append(jnp.where(order == rank, 1.0, 0.0).astype(BF16))
        lows.append((mine[k] * low[k : k + 1]).astype(BF16))
        highs.append((mine[k] * high[k : k + 1]).astype(BF16))
        base = base + ahead[:, LANES:]
        begins = jnp.where(place == LANES // 2 + k * PARTS, base, begins)
    planes = jnp.concatenate([jnp.concatenate(lows, axis=1), jnp.concatenate(highs, axis=1)], axis=0)
    placed = lax.dot_general(
        planes, jnp.concatenate(hots, axis=1), (((1,), (1,)), ((), ())), preferred_element_type=F32
    )
    packed = (placed[:devices] + LANES * placed[devices:]).astype(I32)
    per_row = min(LANES // cap, PARTS)
    alone = packed
    for i in range(1, per_row):
        packed = jnp.where(lane >= i * cap, turn(pltpu.roll(alone, devices - 2 * i, 0), i * cap), packed)
    lane1 = iota((1, LANES), 1)
    actives = jnp.zeros((1, LANES), I32)
    for k in range(targets):
        actives = jnp.where((lane1 < LANES // 2) & (lane1 % targets == k), active_ref[k], actives)
    size = 2 * PARTS
    width = PARTS // per_row + 1
    for first in range(0, devices, size):
        blocks = []
        for core in range(2):
            begin = jnp.where((row[:size] & 1) == core, begins[first : first + size], 0.0)
            begin = jnp.sum(begin, axis=0, keepdims=True).astype(I32)
            rows = [packed[first + at + core : first + at + core + 1] for at in range(0, size, 2 * per_row)]
            blocks += [*rows, begin + actives]
        for core in range(2):
            block = jnp.concatenate(blocks[core * width : (core + 1) * width], axis=0)
            for device in range(first + core, first + size, 2):
                at = place_of(device, devices) * width
                out_ref[at : at + width] = block


def predict(state_ref, force_ref, mass_ref, elapsed_ref, star_ref, table_ref):
    for block in range(mass_ref.shape[0]):
        cols = slice(block * LANES, (block + 1) * LANES)
        state, force = state_ref[:, cols], force_ref[:, cols]
        mass, step = mass_ref[block : block + 1], elapsed_ref[block : block + 1]
        accel, jerk = force[0:3], force[3:6]
        position = state[0:3] + step * (state[3:6] + step * (0.5 * accel + step * jerk / 6.0))
        velocity = state[3:6] + step * (accel + 0.5 * step * jerk)
        stars = jnp.concatenate([position, velocity, mass, step], axis=0)
        star_ref[:, cols] = stars
        rows = jnp.concatenate([stars, force, jnp.zeros((2, LANES), F32)], axis=0)
        table_ref[block * 16 : (block + 1) * 16] = split3(rows)


def own_kernel(stars_dev, targets, request_ref, table_ref, out_ref):
    devices = out_ref.shape[0] // sent_rows(out_ref)
    lines = devices // PARTS
    width = request_ref.shape[0] // devices
    lane, row = iota((devices, LANES), 1), iota((devices, LANES), 0)
    ids = request_ref[pl.ds(width - 1, devices, stride=width), :]
    ids = ids.astype(F32)
    ids = jnp.where(lane < LANES // 2, ids, turn(ids, LANES // 2))
    per_tile = LANES // targets
    tiles = devices // per_tile
    sender = spaced(row, devices)
    start = (part_of(sender) * lines + line_of(sender)) * targets
    flat = []
    for t in range(tiles):
        offset = lane + t * LANES - start
        here = (offset >= 0) & (offset < targets)
        flat.append(jnp.sum(jnp.where(here, ids, 0.0), axis=0, keepdims=True))
    local = jnp.concatenate(flat, axis=1).astype(I32) - lax.axis_index("stars") * stars_dev
    local = jnp.where((local >= 0) & (local < stars_dev), local, -1)
    own = pick(table_ref[...], local, 16)
    words = own[7:15]
    own = own[0:8]
    span = lines * targets
    last = 6 * span
    lane = iota((per_tile, LANES), 1)
    lane1 = iota((1, LANES), 1)
    rows = sent_rows(out_ref)
    backs = []
    for t in range(tiles):
        back = jnp.zeros((per_tile, LANES), F32)
        tile = pltpu.roll(words[:, t * LANES : (t + 1) * LANES], targets, 1, stride=targets, stride_axis=0)
        tile = turn(tile, last)
        for c in range(7):
            begin = last % LANES + c * targets
            here = (lane >= begin) & (lane < begin + targets)
            spread = jnp.broadcast_to(tile[c : c + 1], (per_tile, LANES))
            back = jnp.where(here, pltpu.roll(spread, 0, 1, stride=targets, stride_axis=0), back)
        backs.append(back)
    piece = min(span, LANES)
    turned = {}
    for part in range(PARTS):
        group = [jnp.zeros((1, LANES), F32) for _ in range(rows)]
        for at in range(0, span, piece):
            tile, source = divmod(part * span + at, LANES)
            for c in range(6):
                to, begin = divmod(c * span + at, LANES)
                shift = (begin - source) % LANES
                if (tile, shift) not in turned:
                    turned[tile, shift] = turn(own[:, tile * LANES : (tile + 1) * LANES], shift)
                here = (lane1 >= begin) & (lane1 < begin + piece)
                group[to] = jnp.where(here, turned[tile, shift][c : c + 1], group[to])
        for line in range(lines):
            at = place_of(device_at(line, part), devices) * rows
            for r in range(rows - 1):
                out_ref[at + r : at + r + 1] = group[r]
            tile, source = divmod(part * span + line * targets, LANES)
            block = per_tile - 1 - source // targets
            out_ref[at + rows - 1 : at + rows] = group[rows - 1] + backs[tile][block : block + 1]


def sent_rows(ref):
    return ref.shape[0] // lax.axis_size("stars")


def listed_kernel(cap, targets, request_ref, *refs):
    star_refs, (all_ref, listed_ref, slot_ref, table_ref) = refs[:PARTS], refs[PARTS:]
    blocks = star_refs[0].shape[1] // LANES
    mine = part_of(lax.axis_index("stars"))
    for mask, star_ref in zip((0, *(3, 2, 1)), star_refs):
        stars = star_ref[...]
        all_ref[mask * 8 : (mask + 1) * 8] = stars
        first = (mine ^ mask) * (blocks * 8)
        for pair in range(blocks // 2):
            tiles = [stars[:, (2 * pair + i) * LANES : (2 * pair + i + 1) * LANES] for i in range(2)]
            start = pl.multiple_of(first + pair * 16, 16)
            table_ref[pl.ds(start, 16), :] = split3(jnp.concatenate(tiles, axis=0))
    devices = lax.axis_size("stars")
    lines = devices // PARTS
    width = request_ref.shape[0] // devices
    rows = width - 1
    per_row = PARTS // rows
    at = [place_of(device_at(line, mine), devices) * width for line in range(lines)]
    begins = jnp.concatenate([request_ref[pl.ds(first + rows, 1), :] for first in at], axis=0)
    lane = iota((lines, LANES), 1)
    for j in range(rows):
        slot = jnp.zeros((lines, LANES), I32)
        for k in range(1, targets + 1):
            for i in range(per_row):
                column = LANES // 2 + (k - 1) * PARTS + j * per_row + i
                begin = begins[:, column : column + 1]
                here = (lane >= begin + i * cap) & (lane >= i * cap) & (lane < (i + 1) * cap)
                slot += jnp.where(here, 1, 0)
        slot_ref[j * lines : (j + 1) * lines] = slot
    lane = iota((1, LANES), 1)
    lane8 = iota((8, LANES), 1)
    for j in range(rows):
        asked = [request_ref[pl.ds(first + j, 1), :] for first in at]
        found = []
        for i in range(per_row):
            columns = []
            for chunk in range(lines // per_row):
                column = asked[chunk * per_row]
                column = turn(column, -i * cap)
                for b in range(1, per_row):
                    column = jnp.where(lane >= b * cap, turn(asked[chunk * per_row + b], (b - i) * cap), column)
                columns.append(column)
            size = blocks * 8
            table = table_ref[(j * per_row + i) * size : (j * per_row + i + 1) * size]
            found.append(pick(table, jnp.concatenate(columns, axis=1)))
        for line in range(lines):
            chunk, b = divmod(line, per_row)
            cols = slice(chunk * LANES, (chunk + 1) * LANES)
            near = turn(found[0][:, cols], -b * cap)
            for i in range(1, per_row):
                near = jnp.where(lane8 >= i * cap, turn(found[i][:, cols], (i - b) * cap), near)
            listed_ref[(j * lines + line) * 8 : (j * lines + line + 1) * 8] = near


def pair_sums(target, source, mass, softening, sums):
    x, y, z = (source[c] - target[c] for c in range(3))
    u, v, w = (source[c] - target[c] for c in range(3, 6))
    inverse = lax.rsqrt(x * x + y * y + z * z + softening)
    square = inverse * inverse
    strength = mass * inverse * square
    radial = (x * u + y * v + z * w) * (3.0 * square)
    return (
        sums[0] + strength * x,
        sums[1] + strength * y,
        sums[2] + strength * z,
        sums[3] + strength * (u - radial * x),
        sums[4] + strength * (v - radial * y),
        sums[5] + strength * (w - radial * z),
    )


def add_sent(sent_ref, kept_ref, target_ref):
    devices = lax.axis_size("stars")
    span = target_ref.shape[0]
    rows = sent_ref.shape[0] // devices
    height = math.lcm(rows, 8)
    sent = sent_ref[0:height]
    for i in range(1, sent_ref.shape[0] // height):
        sent = sent + sent_ref[i * height : (i + 1) * height]
    block = sent[0:rows]
    for i in range(1, height // rows):
        block = block + sent[i * rows : (i + 1) * rows]
    kept_ref[...] = jnp.zeros(kept_ref.shape, F32)
    kept_ref[0:rows] = block
    piece = min(span, LANES)
    for at in range(0, span, piece):
        places = [divmod(c * span + at, LANES) for c in range(6)]
        tile = [turn(block[r : r + 1], -begin) for r, begin in places]
        tile = jnp.concatenate([*tile, jnp.zeros((2, LANES), F32)], axis=0).T
        target_ref[at : at + piece, 0:8] = tile[0:piece]


def first_force_kernel(softening, targets, group_step, core, masks, sent_ref, all_ref, listed_ref, slot_ref, out_ref, kept_ref, target_ref):
    add_sent(sent_ref, kept_ref, target_ref)
    force_kernel(softening, targets, group_step, core, masks, target_ref, all_ref, listed_ref, slot_ref, out_ref)


def force_kernel(softening, targets, group_step, core, masks, target_ref, all_ref, listed_ref, slot_ref, out_ref):
    lines = lax.axis_size("stars") // PARTS
    me = lax.axis_index("stars")
    side, place = (me + core) & 1, me // (2 * PARTS)
    lane, row = iota((8, LANES), 1), iota((8, LANES), 0)
    zeros = (jnp.zeros((8, LANES), F32),) * 6
    for first in range(0, len(masks), group_step):
        groups = [2 * (place ^ mask) + side for mask in masks[first : first + group_step]]
        held = []
        for group in groups:
            tile = target_ref[pl.ds(pl.multiple_of(group * targets, 8), 8), 0:8]
            held.append([jnp.broadcast_to(tile[:, c : c + 1], (8, LANES)) for c in range(6)])

        def add_stars(part, sums, held=held):
            for s in range(all_ref.shape[1] // LANES):
                tile = all_ref[pl.ds(pl.multiple_of(part * 8, 8), 8), s * LANES : (s + 1) * LANES]
                source = [jnp.broadcast_to(tile[c : c + 1], (8, LANES)) for c in range(7)]
                sums = tuple(pair_sums(held[n], source, source[6], softening, sums[n]) for n in range(len(held)))
            return sums

        sums = lax.fori_loop(0, PARTS, add_stars, (zeros,) * len(held))
        for n, group in enumerate(groups):
            irregular = zeros
            for j in range(slot_ref.shape[0] // lines):
                at = j * lines + group
                near = listed_ref[pl.ds(pl.multiple_of(at * 8, 8), 8), :]
                mass = jnp.where(slot_ref[pl.ds(at, 1), :] == row, near[6:7], 0.0)
                irregular = pair_sums(held[n], [near[c : c + 1] for c in range(6)], mass, softening, irregular)
            result = zeros[0]
            for c, values in enumerate(sums[n] + irregular):
                value = jnp.sum(values, axis=1, keepdims=True)
                result = jnp.where(lane == -c * targets % LANES + row, value, result)
            out_ref[first + n : first + n + 1] = jnp.sum(result, axis=0, keepdims=True)


def share_kernel(mine_ref, partner_ref, *out_refs):
    for n, out_ref in enumerate(out_refs):
        out_ref[...] = mine_ref[n : n + 1] + partner_ref[n + 1 : n + 2]


def unfold(row, targets):
    wide = jnp.broadcast_to(row, (LANES // targets, LANES))
    return pltpu.roll(wide, 0, 1, stride=targets, stride_axis=0)[:, 0:targets]


def correct_kernel(targets, kept_ref, mine_ref, partner_ref, *refs):
    sums_refs, (state_ref, forces_ref, terms_ref) = refs[:-3], refs[-3:]
    lines = 2 * (len(sums_refs) + 1)
    span = lines * targets
    total = mine_ref[0:1] + partner_ref[0:1]
    for sums_ref in sums_refs:
        total = total + sums_ref[...]
    kept = kept_ref[...]
    piece = min(span, LANES)
    at = line_of(lax.axis_index("stars")) * targets
    moved = pltpu.roll(kept, (LANES - at % piece) % LANES, 1)
    turned = {}
    rows = []
    for c in range(6):
        r, begin = divmod(c * span, LANES)
        if begin not in turned:
            turned[begin] = turn(moved, -begin)
        value = turned[begin][r : r + 1]
        for q in range(1, span // piece):
            value = jnp.where(at // piece == q, turned[begin][r + q : r + q + 1], value)
        rows.append(value[:, 0:targets])
    position, velocity = jnp.concatenate(rows[0:3], axis=0), jnp.concatenate(rows[3:6], axis=0)
    r, begin = divmod(6 * span, LANES)
    words = unfold(turn(kept[r : r + 1], -begin), targets)
    step = words[0:1]
    old_accel = jnp.concatenate([words[-c : LANES // targets + 1 - c] for c in (1, 2, 3)], axis=0)
    old_jerk = jnp.concatenate([words[-c : LANES // targets + 1 - c] for c in (4, 5, 6)], axis=0)
    rows = unfold(total, targets)
    accel, jerk, irregular = rows[0:3], rows[3:6], rows[6:12]
    change = accel - old_accel
    second = 3.0 * change - step * (2.0 * old_jerk + jerk)
    third = -2.0 * change + step * (old_jerk + jerk)
    state_ref[0:3] = position + step * step * (second / 12.0 + third / 20.0)
    state_ref[3:6] = velocity + step * (second / 3.0 + third / 4.0)
    forces = jnp.concatenate([irregular, rows[0:6] - irregular, jnp.zeros((4, targets), F32)], axis=0)
    forces_ref[...] = forces.T[:, 0:12]
    terms_ref[0:3] = second
    terms_ref[3:6] = third


def exchange(rows, devices):
    wide = rows.reshape(devices, 1, -1)
    order = [[spaced(place, devices) for place in range(devices)]]
    return lax.all_to_all(wide, "stars", 0, 0, axis_index_groups=order, tiled=True).reshape(rows.shape)


def per_device(star_state, old_force, star_mass, elapsed, active_ids, neighbours, list_length):
    stars_dev = star_state.shape[1]
    devices = lax.axis_size("stars")
    lines = devices // PARTS
    targets, slots = neighbours.shape
    cap = 2 * targets * slots // devices
    blocks = stars_dev // LANES
    request_rows = max(1, PARTS * cap // LANES)
    back_rows = -(-(6 * lines + 7) * targets // LANES)
    softening = 0.25 * math.sqrt(slots) / (stars_dev * devices)

    def shape(*dims, dtype=F32):
        return jax.ShapeDtypeStruct(dims, dtype)

    def cost(flops):
        return pl.CostEstimate(flops=flops, bytes_accessed=1 << 20, transcendentals=0)

    def swap(value, mask):
        return lax.ppermute(value, "stars", [(i, i ^ mask) for i in range(devices)])

    given = (
        active_ids,
        list_length,
        neighbours,
        star_state,
        old_force,
        star_mass.reshape(blocks, LANES),
        elapsed.reshape(blocks, LANES),
    )
    request, stars, table = pl.pallas_call(
        functools.partial(first_kernel, stars_dev, cap),
        out_shape=(
            shape(devices * (request_rows + 1), LANES, dtype=I32),
            pltpu.VMEM((8, stars_dev), F32),
            pltpu.VMEM((blocks * 16, 3 * LANES), BF16),
        ),
        in_specs=[HBM] * 7,
        out_specs=(VMEM,) * 3,
        scratch_shapes=[
            pltpu.SMEM((targets,), I32),
            pltpu.SMEM((targets,), I32),
            *(pltpu.VMEM(value.shape, value.dtype) for value in given[2:]),
            pltpu.SemaphoreType.DMA((7,)),
        ],
        compiler_params=PARAMS,
    )(*(pltpu.with_memory_space_constraint(value, pltpu.HBM) for value in given))
    asked = exchange(request, devices)
    shared = [stars, *(swap(stars, 2 * mask) for mask in (3, 2, 1))]
    sent = pl.pallas_call(
        functools.partial(own_kernel, stars_dev, targets),
        out_shape=shape(devices * back_rows, LANES),
        in_specs=[VMEM] * 2,
        out_specs=VMEM,
        compiler_params=PARAMS,
    )(asked, table)
    sent = exchange(sent, devices)
    every, listed, slot = pl.pallas_call(
        functools.partial(listed_kernel, cap, targets),
        out_shape=(
            shape(PARTS * 8, stars_dev),
            shape(lines * request_rows * 8, LANES),
            shape(lines * request_rows, LANES, dtype=I32),
        ),
        in_specs=[VMEM] * (1 + PARTS),
        out_specs=(VMEM,) * 3,
        scratch_shapes=[pltpu.VMEM((PARTS * blocks * 8, 3 * LANES), BF16)],
        compiler_params=PARAMS,
        cost_estimate=cost(1 << 24),
    )(asked, *shared)
    kept_rows = -(-back_rows // 8) * 8

    places = lines // 2

    def forces_of(kernel, core, masks, given, *kept):
        return pl.pallas_call(
            functools.partial(kernel, softening, targets, 4, core, masks),
            out_shape=(shape(-(-len(masks) // 8) * 8, LANES), *kept),
            in_specs=[VMEM] * 4,
            out_specs=(VMEM,) * (1 + len(kept)),
            compiler_params=PARAMS,
        )(given, every, listed, slot)

    theirs, kept, upright = forces_of(
        first_force_kernel, 1, range(places), sent, shape(kept_rows, LANES), shape(lines * targets, LANES)
    )
    (others,) = forces_of(force_kernel, 0, range(1, places), upright)
    theirs = swap(theirs, 1)
    sums = pl.pallas_call(
        share_kernel,
        out_shape=(shape(1, LANES),) * (places - 1),
        in_specs=[VMEM] * 2,
        out_specs=(VMEM,) * (places - 1),
        compiler_params=PARAMS,
    )(others, theirs)
    sums = [swap(sums[mask - 1], mask * 2 * PARTS) for mask in range(places - 1, 0, -1)]
    (mine,) = forces_of(force_kernel, 0, range(1), upright)
    state, forces, terms = pl.pallas_call(
        functools.partial(correct_kernel, targets),
        out_shape=(shape(6, targets), shape(targets, 12), shape(6, targets)),
        in_specs=[VMEM] * (2 + places),
        out_specs=(VMEM,) * 3,
        compiler_params=PARAMS,
    )(kept, mine, theirs, *sums)
    return state, forces.T, terms


def solution(mesh):
    placed = (
        P(None, "stars"),
        P(None, "stars"),
        P("stars"),
        P("stars"),
        P("stars"),
        P("stars", None),
        P("stars"),
    )
    return jax.shard_map(
        per_device,
        mesh=mesh,
        in_specs=placed,
        out_specs=(P(None, "stars"), P(None, "stars"), P(None, "stars")),
        check_vma=False,
    )
```

```python
import functools
import math

import jax
import jax.numpy as jnp
from jax import lax
from jax.experimental import pallas as pl
from jax.experimental.pallas import tpu as pltpu
from jax.sharding import PartitionSpec as P

LANES = 128
PARTS = 4
SPACING = 11
F32 = jnp.float32
I32 = jnp.int32
BF16 = jnp.bfloat16
VMEM = pl.BlockSpec(memory_space=pltpu.VMEM)
HBM = pl.BlockSpec(memory_space=pltpu.HBM)
PARAMS = pltpu.CompilerParams(vmem_limit_bytes=32 * 1024 * 1024)


def iota(shape, axis):
    return lax.broadcasted_iota(I32, shape, axis)


def part_of(device):
    return (device >> 1) & (PARTS - 1)


def line_of(device):
    return (device >> 3) * 2 + (device & 1)


def device_at(line, part):
    return (line >> 1) * 2 * PARTS + part * 2 + (line & 1)


def spaced(device, devices):
    return device * SPACING & (devices - 1)


def place_of(device, devices):
    return device * pow(SPACING, -1, devices) & (devices - 1)


def turn(value, lanes):
    lanes %= LANES
    return pltpu.roll(value, lanes, 1) if lanes else value


def split3(value):
    high = value.astype(BF16)
    rest = value - high.astype(F32)
    middle = rest.astype(BF16)
    low = (rest - middle.astype(F32)).astype(BF16)
    return jnp.concatenate([high, middle, low], axis=1)


def pick(table, column, rows=8):
    count = column.shape[1]
    low = jnp.where(column < 0, -1, column & (LANES - 1))
    high = lax.shift_right_logical(column, 7)
    hot = jnp.where(iota((LANES, count), 0) == low, 1.0, 0.0).astype(BF16)
    found = jnp.dot(table, jnp.concatenate([hot] * 3, axis=0), preferred_element_type=F32)
    level = [found[first : first + rows] for first in range(0, table.shape[0], rows)]
    bit = 1
    while len(level) > 1:
        odd = (high & bit) != 0
        level = [
            jnp.where(odd, level[i + 1], level[i]) if i + 1 < len(level) else level[i] for i in range(0, len(level), 2)
        ]
        bit *= 2
    return level[0]


def first_kernel(stars_dev, cap, *refs):
    sources, (request_ref, star_ref, table_ref), targets, sems = refs[:7], refs[7:10], refs[10:17], refs[17]
    copies = [pltpu.make_async_copy(*pair, sems.at[i]) for i, pair in enumerate(zip(sources, targets))]
    for copy in copies:
        copy.start()
    for copy in copies[:3]:
        copy.wait()
    sort_requests(stars_dev, cap, *targets[:3], request_ref)
    for copy in copies[3:]:
        copy.wait()
    predict(*targets[3:], star_ref, table_ref)


def sort_requests(stars_dev, cap, active_ref, length_ref, listed_ref, out_ref):
    targets, slots = listed_ref.shape
    devices = lax.axis_size("stars")
    listed = listed_ref[...]
    owner = listed // stars_dev if stars_dev & (stars_dev - 1) else lax.shift_right_logical(listed, stars_dev.bit_length() - 1)
    local = listed - owner * stars_dev
    low = (local & (LANES - 1)).astype(F32)
    high = lax.shift_right_logical(local, 7).astype(F32)
    lane = iota((devices, LANES), 1)
    row = iota((devices, LANES), 0)
    before = jnp.where(iota((slots, 2 * LANES), 0) < iota((slots, 2 * LANES), 1), 1.0, 0.0).astype(BF16)
    mine = [
        jnp.where((owner[k : k + 1] == row) & (lane < length_ref[k]), 1.0, 0.0) for k in range(targets)
    ]
    counts = jnp.dot(jnp.concatenate(mine, axis=0).astype(BF16), before, preferred_element_type=F32)
    base = jnp.zeros((devices, LANES), F32)
    order = iota((LANES, slots), 0).astype(F32)
    lows, highs, hots = [], [], []
    place = lane - part_of(row)
    begins = jnp.zeros((devices, LANES), F32)
    for k in range(targets):
        ahead = counts[k * devices : (k + 1) * devices]
        rank = jnp.sum(mine[k] * (ahead[:, :LANES] + base), axis=0, keepdims=True)
        hots.append(jnp.where(order == rank, 1.0, 0.0).astype(BF16))
        lows.append((mine[k] * low[k : k + 1]).astype(BF16))
        highs.append((mine[k] * high[k : k + 1]).astype(BF16))
        base = base + ahead[:, LANES:]
        begins = jnp.where(place == LANES // 2 + k * PARTS, base, begins)
    planes = jnp.concatenate([jnp.concatenate(lows, axis=1), jnp.concatenate(highs, axis=1)], axis=0)
    placed = lax.dot_general(
        planes, jnp.concatenate(hots, axis=1), (((1,), (1,)), ((), ())), preferred_element_type=F32
    )
    packed = (placed[:devices] + LANES * placed[devices:]).astype(I32)
    per_row = min(LANES // cap, PARTS)
    alone = packed
    for i in range(1, per_row):
        packed = jnp.where(lane >= i * cap, turn(pltpu.roll(alone, devices - 2 * i, 0), i * cap), packed)
    lane1 = iota((1, LANES), 1)
    actives = jnp.zeros((1, LANES), I32)
    for k in range(targets):
        actives = jnp.where((lane1 < LANES // 2) & (lane1 % targets == k), active_ref[k], actives)
    size = 2 * PARTS
    width = PARTS // per_row + 1
    for first in range(0, devices, size):
        blocks = []
        for core in range(2):
            begin = jnp.where((row[:size] & 1) == core, begins[first : first + size], 0.0)
            begin = jnp.sum(begin, axis=0, keepdims=True).astype(I32)
            rows = [packed[first + at + core : first + at + core + 1] for at in range(0, size, 2 * per_row)]
            blocks += [begin + actives, *rows]
        for core in range(2):
            block = jnp.concatenate(blocks[core * width : (core + 1) * width], axis=0)
            for device in range(first + core, first + size, 2):
                at = place_of(device, devices) * width
                out_ref[at : at + width] = block


def predict(state_ref, force_ref, mass_ref, elapsed_ref, star_ref, table_ref):
    for block in range(mass_ref.shape[0]):
        cols = slice(block * LANES, (block + 1) * LANES)
        state, force = state_ref[:, cols], force_ref[:, cols]
        mass, step = mass_ref[block : block + 1], elapsed_ref[block : block + 1]
        accel, jerk = force[0:3], force[3:6]
        position = state[0:3] + step * (state[3:6] + step * (0.5 * accel + step * jerk / 6.0))
        velocity = state[3:6] + step * (accel + 0.5 * step * jerk)
        stars = jnp.concatenate([position, velocity, mass, step], axis=0)
        star_ref[:, cols] = stars
        rows = jnp.concatenate([stars, force, jnp.zeros((2, LANES), F32)], axis=0)
        table_ref[block * 16 : (block + 1) * 16] = split3(rows)


def own_kernel(stars_dev, targets, request_ref, table_ref, out_ref):
    devices = out_ref.shape[0] // sent_rows(out_ref)
    lines = devices // PARTS
    width = request_ref.shape[0] // devices
    lane, row = iota((devices, LANES), 1), iota((devices, LANES), 0)
    ids = request_ref[pl.ds(0, devices, stride=width), :]
    ids = ids.astype(F32)
    ids = jnp.where(lane < LANES // 2, ids, turn(ids, LANES // 2))
    per_tile = LANES // targets
    tiles = devices // per_tile
    sender = spaced(row, devices)
    start = (part_of(sender) * lines + line_of(sender)) * targets
    flat = []
    for t in range(tiles):
        offset = lane + t * LANES - start
        here = (offset >= 0) & (offset < targets)
        flat.append(jnp.sum(jnp.where(here, ids, 0.0), axis=0, keepdims=True))
    local = jnp.concatenate(flat, axis=1).astype(I32) - lax.axis_index("stars") * stars_dev
    local = jnp.where((local >= 0) & (local < stars_dev), local, -1)
    own = pick(table_ref[...], local, 16)
    words = own[7:15]
    own = own[0:8]
    span = lines * targets
    last = 6 * span
    lane = iota((per_tile, LANES), 1)
    lane1 = iota((1, LANES), 1)
    rows = sent_rows(out_ref)
    backs = []
    for t in range(tiles):
        back = jnp.zeros((per_tile, LANES), F32)
        tile = pltpu.roll(words[:, t * LANES : (t + 1) * LANES], targets, 1, stride=targets, stride_axis=0)
        tile = turn(tile, last)
        for c in range(7):
            begin = last % LANES + c * targets
            here = (lane >= begin) & (lane < begin + targets)
            spread = jnp.broadcast_to(tile[c : c + 1], (per_tile, LANES))
            back = jnp.where(here, pltpu.roll(spread, 0, 1, stride=targets, stride_axis=0), back)
        backs.append(back)
    piece = min(span, LANES)
    turned = {}
    for part in range(PARTS):
        group = [jnp.zeros((1, LANES), F32) for _ in range(rows)]
        for at in range(0, span, piece):
            tile, source = divmod(part * span + at, LANES)
            for c in range(6):
                to, begin = divmod(c * span + at, LANES)
                shift = (begin - source) % LANES
                if (tile, shift) not in turned:
                    turned[tile, shift] = turn(own[:, tile * LANES : (tile + 1) * LANES], shift)
                here = (lane1 >= begin) & (lane1 < begin + piece)
                group[to] = jnp.where(here, turned[tile, shift][c : c + 1], group[to])
        for line in range(lines):
            at = place_of(device_at(line, part), devices) * rows
            for r in range(rows - 1):
                out_ref[at + r : at + r + 1] = group[r]
            tile, source = divmod(part * span + line * targets, LANES)
            block = per_tile - 1 - source // targets
            out_ref[at + rows - 1 : at + rows] = group[rows - 1] + backs[tile][block : block + 1]


def sent_rows(ref):
    return ref.shape[0] // lax.axis_size("stars")


def listed_kernel(cap, targets, request_ref, *refs):
    star_refs, (all_ref, listed_ref, slot_ref, table_ref) = refs[:PARTS], refs[PARTS:]
    blocks = star_refs[0].shape[1] // LANES
    mine = part_of(lax.axis_index("stars"))
    for mask, star_ref in zip((0, *(3, 2, 1)), star_refs):
        stars = star_ref[...]
        all_ref[mask * 8 : (mask + 1) * 8] = stars
        first = (mine ^ mask) * (blocks * 8)
        for pair in range(blocks // 2):
            tiles = [stars[:, (2 * pair + i) * LANES : (2 * pair + i + 1) * LANES] for i in range(2)]
            start = pl.multiple_of(first + pair * 16, 16)
            table_ref[pl.ds(start, 16), :] = split3(jnp.concatenate(tiles, axis=0))
    devices = lax.axis_size("stars")
    lines = devices // PARTS
    width = request_ref.shape[0] // devices
    rows = width - 1
    per_row = PARTS // rows
    at = [place_of(device_at(line, mine), devices) * width for line in range(lines)]
    begins = jnp.concatenate([request_ref[pl.ds(first, 1), :] for first in at], axis=0)
    lane = iota((lines, LANES), 1)
    for j in range(rows):
        slot = jnp.zeros((lines, LANES), I32)
        for k in range(1, targets + 1):
            for i in range(per_row):
                column = LANES // 2 + (k - 1) * PARTS + j * per_row + i
                begin = begins[:, column : column + 1]
                here = (lane >= begin + i * cap) & (lane >= i * cap) & (lane < (i + 1) * cap)
                slot += jnp.where(here, 1, 0)
        slot_ref[j * lines : (j + 1) * lines] = slot
    lane = iota((1, LANES), 1)
    lane8 = iota((8, LANES), 1)
    for j in range(rows):
        asked = [request_ref[pl.ds(first + 1 + j, 1), :] for first in at]
        found = []
        for i in range(per_row):
            columns = []
            for chunk in range(lines // per_row):
                column = asked[chunk * per_row]
                column = turn(column, -i * cap)
                for b in range(1, per_row):
                    column = jnp.where(lane >= b * cap, turn(asked[chunk * per_row + b], (b - i) * cap), column)
                columns.append(column)
            size = blocks * 8
            table = table_ref[(j * per_row + i) * size : (j * per_row + i + 1) * size]
            found.append(pick(table, jnp.concatenate(columns, axis=1)))
        for line in range(lines):
            chunk, b = divmod(line, per_row)
            cols = slice(chunk * LANES, (chunk + 1) * LANES)
            near = turn(found[0][:, cols], -b * cap)
            for i in range(1, per_row):
                near = jnp.where(lane8 >= i * cap, turn(found[i][:, cols], (i - b) * cap), near)
            listed_ref[(j * lines + line) * 8 : (j * lines + line + 1) * 8] = near


def pair_sums(target, source, mass, softening, sums):
    x, y, z = (source[c] - target[c] for c in range(3))
    u, v, w = (source[c] - target[c] for c in range(3, 6))
    inverse = lax.rsqrt(x * x + y * y + z * z + softening)
    square = inverse * inverse
    strength = mass * inverse * square
    radial = (x * u + y * v + z * w) * (3.0 * square)
    return (
        sums[0] + strength * x,
        sums[1] + strength * y,
        sums[2] + strength * z,
        sums[3] + strength * (u - radial * x),
        sums[4] + strength * (v - radial * y),
        sums[5] + strength * (w - radial * z),
    )


def add_sent(sent_ref, kept_ref, target_ref):
    devices = lax.axis_size("stars")
    span = target_ref.shape[0]
    rows = sent_ref.shape[0] // devices
    height = math.lcm(rows, 8)
    sent = sent_ref[0:height]
    for i in range(1, sent_ref.shape[0] // height):
        sent = sent + sent_ref[i * height : (i + 1) * height]
    block = sent[0:rows]
    for i in range(1, height // rows):
        block = block + sent[i * rows : (i + 1) * rows]
    kept_ref[...] = jnp.zeros(kept_ref.shape, F32)
    kept_ref[0:rows] = block
    piece = min(span, LANES)
    for at in range(0, span, piece):
        places = [divmod(c * span + at, LANES) for c in range(6)]
        tile = [turn(block[r : r + 1], -begin) for r, begin in places]
        tile = jnp.concatenate([*tile, jnp.zeros((2, LANES), F32)], axis=0).T
        target_ref[at : at + piece, 0:8] = tile[0:piece]


def first_force_kernel(softening, targets, group_step, core, masks, sent_ref, all_ref, listed_ref, slot_ref, out_ref, kept_ref, target_ref):
    add_sent(sent_ref, kept_ref, target_ref)
    force_kernel(softening, targets, group_step, core, masks, target_ref, all_ref, listed_ref, slot_ref, out_ref)


def force_kernel(softening, targets, group_step, core, masks, target_ref, all_ref, listed_ref, slot_ref, out_ref):
    lines = lax.axis_size("stars") // PARTS
    me = lax.axis_index("stars")
    side, place = (me + core) & 1, me // (2 * PARTS)
    lane, row = iota((8, LANES), 1), iota((8, LANES), 0)
    zeros = (jnp.zeros((8, LANES), F32),) * 6
    for first in range(0, len(masks), group_step):
        groups = [2 * (place ^ mask) + side for mask in masks[first : first + group_step]]
        held = []
        for group in groups:
            tile = target_ref[pl.ds(pl.multiple_of(group * targets, 8), 8), 0:8]
            held.append([jnp.broadcast_to(tile[:, c : c + 1], (8, LANES)) for c in range(6)])

        def add_stars(part, sums, held=held):
            for s in range(all_ref.shape[1] // LANES):
                tile = all_ref[pl.ds(pl.multiple_of(part * 8, 8), 8), s * LANES : (s + 1) * LANES]
                source = [jnp.broadcast_to(tile[c : c + 1], (8, LANES)) for c in range(7)]
                sums = tuple(pair_sums(held[n], source, source[6], softening, sums[n]) for n in range(len(held)))
            return sums

        sums = lax.fori_loop(0, PARTS, add_stars, (zeros,) * len(held))
        for n, group in enumerate(groups):
            irregular = zeros
            for j in range(slot_ref.shape[0] // lines):
                at = j * lines + group
                near = listed_ref[pl.ds(pl.multiple_of(at * 8, 8), 8), :]
                mass = jnp.where(slot_ref[pl.ds(at, 1), :] == row, near[6:7], 0.0)
                irregular = pair_sums(held[n], [near[c : c + 1] for c in range(6)], mass, softening, irregular)
            result = zeros[0]
            for c, values in enumerate(sums[n] + irregular):
                value = jnp.sum(values, axis=1, keepdims=True)
                result = jnp.where(lane == -c * targets % LANES + row, value, result)
            out_ref[first + n : first + n + 1] = jnp.sum(result, axis=0, keepdims=True)


def share_kernel(mine_ref, partner_ref, *out_refs):
    for n, out_ref in enumerate(out_refs):
        out_ref[...] = mine_ref[n : n + 1] + partner_ref[n + 1 : n + 2]


def unfold(row, targets):
    wide = jnp.broadcast_to(row, (LANES // targets, LANES))
    return pltpu.roll(wide, 0, 1, stride=targets, stride_axis=0)[:, 0:targets]


def correct_kernel(targets, kept_ref, mine_ref, partner_ref, *refs):
    sums_refs, (state_ref, forces_ref, terms_ref) = refs[:-3], refs[-3:]
    lines = 2 * (len(sums_refs) + 1)
    span = lines * targets
    total = mine_ref[0:1] + partner_ref[0:1]
    for sums_ref in sums_refs:
        total = total + sums_ref[...]
    kept = kept_ref[...]
    piece = min(span, LANES)
    at = line_of(lax.axis_index("stars")) * targets
    moved = pltpu.roll(kept, (LANES - at % piece) % LANES, 1)
    turned = {}
    rows = []
    for c in range(6):
        r, begin = divmod(c * span, LANES)
        if begin not in turned:
            turned[begin] = turn(moved, -begin)
        value = turned[begin][r : r + 1]
        for q in range(1, span // piece):
            value = jnp.where(at // piece == q, turned[begin][r + q : r + q + 1], value)
        rows.append(value[:, 0:targets])
    position, velocity = jnp.concatenate(rows[0:3], axis=0), jnp.concatenate(rows[3:6], axis=0)
    r, begin = divmod(6 * span, LANES)
    words = unfold(turn(kept[r : r + 1], -begin), targets)
    step = words[0:1]
    old_accel = jnp.concatenate([words[-c : LANES // targets + 1 - c] for c in (1, 2, 3)], axis=0)
    old_jerk = jnp.concatenate([words[-c : LANES // targets + 1 - c] for c in (4, 5, 6)], axis=0)
    rows = unfold(total, targets)
    accel, jerk, irregular = rows[0:3], rows[3:6], rows[6:12]
    change = accel - old_accel
    second = 3.0 * change - step * (2.0 * old_jerk + jerk)
    third = -2.0 * change + step * (old_jerk + jerk)
    state_ref[0:3] = position + step * step * (second / 12.0 + third / 20.0)
    state_ref[3:6] = velocity + step * (second / 3.0 + third / 4.0)
    forces = jnp.concatenate([irregular, rows[0:6] - irregular, jnp.zeros((4, targets), F32)], axis=0)
    forces_ref[...] = forces.T[:, 0:12]
    terms_ref[0:3] = second
    terms_ref[3:6] = third


def exchange(rows, devices):
    wide = rows.reshape(devices, 1, -1)
    order = [[spaced(place, devices) for place in range(devices)]]
    return lax.all_to_all(wide, "stars", 0, 0, axis_index_groups=order, tiled=True).reshape(rows.shape)


def per_device(star_state, old_force, star_mass, elapsed, active_ids, neighbours, list_length):
    stars_dev = star_state.shape[1]
    devices = lax.axis_size("stars")
    lines = devices // PARTS
    targets, slots = neighbours.shape
    cap = 2 * targets * slots // devices
    blocks = stars_dev // LANES
    request_rows = max(1, PARTS * cap // LANES)
    back_rows = -(-(6 * lines + 7) * targets // LANES)
    softening = 0.25 * math.sqrt(slots) / (stars_dev * devices)

    def shape(*dims, dtype=F32):
        return jax.ShapeDtypeStruct(dims, dtype)

    def cost(flops):
        return pl.CostEstimate(flops=flops, bytes_accessed=1 << 20, transcendentals=0)

    def swap(value, mask):
        return lax.ppermute(value, "stars", [(i, i ^ mask) for i in range(devices)])

    given = (
        active_ids,
        list_length,
        neighbours,
        star_state,
        old_force,
        star_mass.reshape(blocks, LANES),
        elapsed.reshape(blocks, LANES),
    )
    request, stars, table = pl.pallas_call(
        functools.partial(first_kernel, stars_dev, cap),
        out_shape=(
            shape(devices * (request_rows + 1), LANES, dtype=I32),
            pltpu.VMEM((8, stars_dev), F32),
            pltpu.VMEM((blocks * 16, 3 * LANES), BF16),
        ),
        in_specs=[HBM] * 7,
        out_specs=(VMEM,) * 3,
        scratch_shapes=[
            pltpu.SMEM((targets,), I32),
            pltpu.SMEM((targets,), I32),
            *(pltpu.VMEM(value.shape, value.dtype) for value in given[2:]),
            pltpu.SemaphoreType.DMA((7,)),
        ],
        compiler_params=PARAMS,
    )(*(pltpu.with_memory_space_constraint(value, pltpu.HBM) for value in given))
    asked = exchange(request, devices)
    shared = [stars, *(swap(stars, 2 * mask) for mask in (3, 2, 1))]
    sent = pl.pallas_call(
        functools.partial(own_kernel, stars_dev, targets),
        out_shape=shape(devices * back_rows, LANES),
        in_specs=[VMEM] * 2,
        out_specs=VMEM,
        compiler_params=PARAMS,
    )(asked, table)
    sent = exchange(sent, devices)
    every, listed, slot = pl.pallas_call(
        functools.partial(listed_kernel, cap, targets),
        out_shape=(
            shape(PARTS * 8, stars_dev),
            shape(lines * request_rows * 8, LANES),
            shape(lines * request_rows, LANES, dtype=I32),
        ),
        in_specs=[VMEM] * (1 + PARTS),
        out_specs=(VMEM,) * 3,
        scratch_shapes=[pltpu.VMEM((PARTS * blocks * 8, 3 * LANES), BF16)],
        compiler_params=PARAMS,
        cost_estimate=cost(1 << 24),
    )(asked, *shared)
    kept_rows = -(-back_rows // 8) * 8

    places = lines // 2

    def forces_of(kernel, core, masks, given, *kept):
        return pl.pallas_call(
            functools.partial(kernel, softening, targets, 4, core, masks),
            out_shape=(shape(-(-len(masks) // 8) * 8, LANES), *kept),
            in_specs=[VMEM] * 4,
            out_specs=(VMEM,) * (1 + len(kept)),
            compiler_params=PARAMS,
        )(given, every, listed, slot)

    theirs, kept, upright = forces_of(
        first_force_kernel, 1, range(places), sent, shape(kept_rows, LANES), shape(lines * targets, LANES)
    )
    (others,) = forces_of(force_kernel, 0, range(1, places), upright)
    theirs = swap(theirs, 1)
    sums = pl.pallas_call(
        share_kernel,
        out_shape=(shape(1, LANES),) * (places - 1),
        in_specs=[VMEM] * 2,
        out_specs=(VMEM,) * (places - 1),
        compiler_params=PARAMS,
    )(others, theirs)
    sums = [swap(sums[mask - 1], mask * 2 * PARTS) for mask in range(places - 1, 0, -1)]
    (mine,) = forces_of(force_kernel, 0, range(1), upright)
    state, forces, terms = pl.pallas_call(
        functools.partial(correct_kernel, targets),
        out_shape=(shape(6, targets), shape(targets, 12), shape(6, targets)),
        in_specs=[VMEM] * (2 + places),
        out_specs=(VMEM,) * 3,
        compiler_params=PARAMS,
    )(kept, mine, theirs, *sums)
    return state, forces.T, terms


def solution(mesh):
    placed = (
        P(None, "stars"),
        P(None, "stars"),
        P("stars"),
        P("stars"),
        P("stars"),
        P("stars", None),
        P("stars"),
    )
    return jax.shard_map(
        per_device,
        mesh=mesh,
        in_specs=placed,
        out_specs=(P(None, "stars"), P(None, "stars"), P(None, "stars")),
        check_vma=False,
    )
```

```python
import functools
import math

import jax
import jax.numpy as jnp
from jax import lax
from jax.experimental import pallas as pl
from jax.experimental.pallas import tpu as pltpu
from jax.sharding import PartitionSpec as P

LANES = 128
PARTS = 4
SPACING = 11
F32 = jnp.float32
I32 = jnp.int32
BF16 = jnp.bfloat16
VMEM = pl.BlockSpec(memory_space=pltpu.VMEM)
HBM = pl.BlockSpec(memory_space=pltpu.HBM)
PARAMS = pltpu.CompilerParams(vmem_limit_bytes=32 * 1024 * 1024)


def iota(shape, axis):
    return lax.broadcasted_iota(I32, shape, axis)


def part_of(device):
    return (device >> 1) & (PARTS - 1)


def line_of(device):
    return (device >> 3) * 2 + (device & 1)


def device_at(line, part):
    return (line >> 1) * 2 * PARTS + part * 2 + (line & 1)


def spaced(device, devices):
    return device * SPACING & (devices - 1)


def place_of(device, devices):
    return device * pow(SPACING, -1, devices) & (devices - 1)


def turn(value, lanes):
    lanes %= LANES
    return pltpu.roll(value, lanes, 1) if lanes else value


def split3(value):
    high = value.astype(BF16)
    rest = value - high.astype(F32)
    middle = rest.astype(BF16)
    low = (rest - middle.astype(F32)).astype(BF16)
    return jnp.concatenate([high, middle, low], axis=1)


def pick(table, column, rows=8):
    count = column.shape[1]
    low = jnp.where(column < 0, -1, column & (LANES - 1))
    high = lax.shift_right_logical(column, 7)
    hot = jnp.where(iota((LANES, count), 0) == low, 1.0, 0.0).astype(BF16)
    found = jnp.dot(table, jnp.concatenate([hot] * 3, axis=0), preferred_element_type=F32)
    level = [found[first : first + rows] for first in range(0, table.shape[0], rows)]
    bit = 1
    while len(level) > 1:
        odd = (high & bit) != 0
        level = [
            jnp.where(odd, level[i + 1], level[i]) if i + 1 < len(level) else level[i] for i in range(0, len(level), 2)
        ]
        bit *= 2
    return level[0]


def first_kernel(stars_dev, cap, *refs):
    sources, (request_ref, star_ref, table_ref), targets, sems = refs[:7], refs[7:10], refs[10:17], refs[17]
    copies = [pltpu.make_async_copy(*pair, sems.at[i]) for i, pair in enumerate(zip(sources, targets))]
    for copy in copies:
        copy.start()
    for copy in copies[:3]:
        copy.wait()
    sort_requests(stars_dev, cap, *targets[:3], request_ref)
    for copy in copies[3:]:
        copy.wait()
    predict(*targets[3:], star_ref, table_ref)


def sort_requests(stars_dev, cap, active_ref, length_ref, listed_ref, out_ref):
    targets, slots = listed_ref.shape
    devices = lax.axis_size("stars")
    listed = listed_ref[...]
    owner = listed // stars_dev if stars_dev & (stars_dev - 1) else lax.shift_right_logical(listed, stars_dev.bit_length() - 1)
    local = listed - owner * stars_dev
    low = (local & (LANES - 1)).astype(F32)
    high = lax.shift_right_logical(local, 7).astype(F32)
    lane = iota((devices, LANES), 1)
    row = iota((devices, LANES), 0)
    before = jnp.where(iota((slots, 2 * LANES), 0) < iota((slots, 2 * LANES), 1), 1.0, 0.0).astype(BF16)
    mine = [
        jnp.where((owner[k : k + 1] == row) & (lane < length_ref[k]), 1.0, 0.0) for k in range(targets)
    ]
    counts = jnp.dot(jnp.concatenate(mine, axis=0).astype(BF16), before, preferred_element_type=F32)
    base = jnp.zeros((devices, LANES), F32)
    order = iota((LANES, slots), 0).astype(F32)
    lows, highs, hots = [], [], []
    place = lane - part_of(row)
    begins = jnp.zeros((devices, LANES), F32)
    for k in range(targets):
        ahead = counts[k * devices : (k + 1) * devices]
        rank = jnp.sum(mine[k] * (ahead[:, :LANES] + base), axis=0, keepdims=True)
        hots.append(jnp.where(order == rank, 1.0, 0.0).astype(BF16))
        lows.append((mine[k] * low[k : k + 1]).astype(BF16))
        highs.append((mine[k] * high[k : k + 1]).astype(BF16))
        base = base + ahead[:, LANES:]
        begins = jnp.where(place == LANES // 2 + k * PARTS, base, begins)
    planes = jnp.concatenate([jnp.concatenate(lows, axis=1), jnp.concatenate(highs, axis=1)], axis=0)
    placed = lax.dot_general(
        planes, jnp.concatenate(hots, axis=1), (((1,), (1,)), ((), ())), preferred_element_type=F32
    )
    packed = (placed[:devices] + LANES * placed[devices:]).astype(I32)
    per_row = min(LANES // cap, PARTS)
    alone = packed
    for i in range(1, per_row):
        packed = jnp.where(lane >= i * cap, turn(pltpu.roll(alone, devices - 2 * i, 0), i * cap), packed)
    lane1 = iota((1, LANES), 1)
    actives = jnp.zeros((1, LANES), I32)
    for k in range(targets):
        actives = jnp.where((lane1 < LANES // 2) & (lane1 % targets == k), active_ref[k], actives)
    size = 2 * PARTS
    width = PARTS // per_row + 1
    for first in range(0, devices, size):
        blocks = []
        for core in range(2):
            begin = jnp.where((row[:size] & 1) == core, begins[first : first + size], 0.0)
            begin = jnp.sum(begin, axis=0, keepdims=True).astype(I32)
            rows = [packed[first + at + core : first + at + core + 1] for at in range(0, size, 2 * per_row)]
            blocks += [begin + actives, *rows]
        for core in range(2):
            block = jnp.concatenate(blocks[core * width : (core + 1) * width], axis=0)
            for device in range(first + core, first + size, 2):
                at = place_of(device, devices) * width
                out_ref[at : at + width] = block


def predict(state_ref, force_ref, mass_ref, elapsed_ref, star_ref, table_ref):
    for block in range(mass_ref.shape[0]):
        cols = slice(block * LANES, (block + 1) * LANES)
        state, force = state_ref[:, cols], force_ref[:, cols]
        mass, step = mass_ref[block : block + 1], elapsed_ref[block : block + 1]
        accel, jerk = force[0:3], force[3:6]
        position = state[0:3] + step * (state[3:6] + step * (0.5 * accel + step * jerk / 6.0))
        velocity = state[3:6] + step * (accel + 0.5 * step * jerk)
        stars = jnp.concatenate([position, velocity, mass, step], axis=0)
        star_ref[:, cols] = stars
        rows = jnp.concatenate([stars, force, jnp.zeros((2, LANES), F32)], axis=0)
        table_ref[block * 16 : (block + 1) * 16] = split3(rows)


def own_kernel(stars_dev, targets, request_ref, table_ref, out_ref):
    devices = out_ref.shape[0] // sent_rows(out_ref)
    lines = devices // PARTS
    width = request_ref.shape[0] // devices
    lane, row = iota((devices, LANES), 1), iota((devices, LANES), 0)
    ids = request_ref[pl.ds(0, devices, stride=width), :]
    ids = ids.astype(F32)
    ids = jnp.where(lane < LANES // 2, ids, turn(ids, LANES // 2))
    per_tile = LANES // targets
    tiles = devices // per_tile
    sender = spaced(row, devices)
    start = (part_of(sender) * lines + line_of(sender)) * targets
    flat = []
    for t in range(tiles):
        offset = lane + t * LANES - start
        here = (offset >= 0) & (offset < targets)
        flat.append(jnp.sum(jnp.where(here, ids, 0.0), axis=0, keepdims=True))
    local = jnp.concatenate(flat, axis=1).astype(I32) - lax.axis_index("stars") * stars_dev
    local = jnp.where((local >= 0) & (local < stars_dev), local, -1)
    own = pick(table_ref[...], local, 16)
    words = own[7:15]
    own = own[0:8]
    span = lines * targets
    last = 6 * span
    lane = iota((per_tile, LANES), 1)
    lane1 = iota((1, LANES), 1)
    rows = sent_rows(out_ref)
    backs = []
    for t in range(tiles):
        back = jnp.zeros((per_tile, LANES), F32)
        tile = pltpu.roll(words[:, t * LANES : (t + 1) * LANES], targets, 1, stride=targets, stride_axis=0)
        tile = turn(tile, last)
        for c in range(7):
            begin = last % LANES + c * targets
            here = (lane >= begin) & (lane < begin + targets)
            spread = jnp.broadcast_to(tile[c : c + 1], (per_tile, LANES))
            back = jnp.where(here, pltpu.roll(spread, 0, 1, stride=targets, stride_axis=0), back)
        backs.append(back)
    piece = min(span, LANES)
    turned = {}
    for part in range(PARTS):
        group = [jnp.zeros((1, LANES), F32) for _ in range(rows)]
        for at in range(0, span, piece):
            tile, source = divmod(part * span + at, LANES)
            for c in range(6):
                to, begin = divmod(c * span + at, LANES)
                shift = (begin - source) % LANES
                if (tile, shift) not in turned:
                    turned[tile, shift] = turn(own[:, tile * LANES : (tile + 1) * LANES], shift)
                here = (lane1 >= begin) & (lane1 < begin + piece)
                group[to] = jnp.where(here, turned[tile, shift][c : c + 1], group[to])
        for line in range(lines):
            at = place_of(device_at(line, part), devices) * rows
            for r in range(rows - 1):
                out_ref[at + r : at + r + 1] = group[r]
            tile, source = divmod(part * span + line * targets, LANES)
            block = per_tile - 1 - source // targets
            out_ref[at + rows - 1 : at + rows] = group[rows - 1] + backs[tile][block : block + 1]


def sent_rows(ref):
    return ref.shape[0] // lax.axis_size("stars")


def listed_kernel(cap, targets, request_ref, *refs):
    star_refs, (all_ref, listed_ref, slot_ref, table_ref) = refs[:PARTS], refs[PARTS:]
    blocks = star_refs[0].shape[1] // LANES
    mine = part_of(lax.axis_index("stars"))
    for mask, star_ref in zip((0, *(3, 2, 1)), star_refs):
        stars = star_ref[...]
        all_ref[mask * 8 : (mask + 1) * 8] = stars
        first = (mine ^ mask) * (blocks * 8)
        for pair in range(blocks // 2):
            tiles = [stars[:, (2 * pair + i) * LANES : (2 * pair + i + 1) * LANES] for i in range(2)]
            start = pl.multiple_of(first + pair * 16, 16)
            table_ref[pl.ds(start, 16), :] = split3(jnp.concatenate(tiles, axis=0))
    devices = lax.axis_size("stars")
    lines = devices // PARTS
    width = request_ref.shape[0] // devices
    rows = width - 1
    per_row = PARTS // rows
    at = [place_of(device_at(line, mine), devices) * width for line in range(lines)]
    begins = jnp.concatenate([request_ref[pl.ds(first, 1), :] for first in at], axis=0)
    lane = iota((lines, LANES), 1)
    for j in range(rows):
        slot = jnp.zeros((lines, LANES), I32)
        for k in range(1, targets + 1):
            for i in range(per_row):
                column = LANES // 2 + (k - 1) * PARTS + j * per_row + i
                begin = begins[:, column : column + 1]
                here = (lane >= begin + i * cap) & (lane >= i * cap) & (lane < (i + 1) * cap)
                slot += jnp.where(here, 1, 0)
        slot_ref[j * lines : (j + 1) * lines] = slot
    lane = iota((1, LANES), 1)
    lane8 = iota((8, LANES), 1)
    for j in range(rows):
        asked = [request_ref[pl.ds(first + 1 + j, 1), :] for first in at]
        found = []
        for i in range(per_row):
            columns = []
            for chunk in range(lines // per_row):
                column = asked[chunk * per_row]
                column = turn(column, -i * cap)
                for b in range(1, per_row):
                    column = jnp.where(lane >= b * cap, turn(asked[chunk * per_row + b], (b - i) * cap), column)
                columns.append(column)
            size = blocks * 8
            table = table_ref[(j * per_row + i) * size : (j * per_row + i + 1) * size]
            found.append(pick(table, jnp.concatenate(columns, axis=1)))
        for line in range(lines):
            chunk, b = divmod(line, per_row)
            cols = slice(chunk * LANES, (chunk + 1) * LANES)
            near = turn(found[0][:, cols], -b * cap)
            for i in range(1, per_row):
                near = jnp.where(lane8 >= i * cap, turn(found[i][:, cols], (i - b) * cap), near)
            listed_ref[(j * lines + line) * 8 : (j * lines + line + 1) * 8] = near


def pair_sums(target, source, mass, softening, sums):
    x, y, z = (source[c] - target[c] for c in range(3))
    u, v, w = (source[c] - target[c] for c in range(3, 6))
    inverse = lax.rsqrt(x * x + y * y + z * z + softening)
    square = inverse * inverse
    strength = mass * inverse * square
    radial = (x * u + y * v + z * w) * (3.0 * square)
    return (
        sums[0] + strength * x,
        sums[1] + strength * y,
        sums[2] + strength * z,
        sums[3] + strength * (u - radial * x),
        sums[4] + strength * (v - radial * y),
        sums[5] + strength * (w - radial * z),
    )


def add_sent(sent_ref, kept_ref, target_ref):
    devices = lax.axis_size("stars")
    span = target_ref.shape[0]
    rows = sent_ref.shape[0] // devices
    height = math.lcm(rows, 8)
    sent = sent_ref[0:height]
    for i in range(1, sent_ref.shape[0] // height):
        sent = sent + sent_ref[i * height : (i + 1) * height]
    block = sent[0:rows]
    for i in range(1, height // rows):
        block = block + sent[i * rows : (i + 1) * rows]
    kept_ref[...] = jnp.zeros(kept_ref.shape, F32)
    kept_ref[0:rows] = block
    piece = min(span, LANES)
    for at in range(0, span, piece):
        places = [divmod(c * span + at, LANES) for c in range(6)]
        tile = [turn(block[r : r + 1], -begin) for r, begin in places]
        tile = jnp.concatenate([*tile, jnp.zeros((2, LANES), F32)], axis=0).T
        target_ref[at : at + piece, 0:8] = tile[0:piece]


def first_force_kernel(softening, targets, group_step, core, masks, sent_ref, all_ref, listed_ref, slot_ref, out_ref, kept_ref, target_ref):
    add_sent(sent_ref, kept_ref, target_ref)
    force_kernel(softening, targets, group_step, core, masks, target_ref, all_ref, listed_ref, slot_ref, out_ref)


def force_kernel(softening, targets, group_step, core, masks, target_ref, all_ref, listed_ref, slot_ref, out_ref):
    lines = lax.axis_size("stars") // PARTS
    me = lax.axis_index("stars")
    side, place = (me + core) & 1, me // (2 * PARTS)
    lane, row = iota((8, LANES), 1), iota((8, LANES), 0)
    zeros = (jnp.zeros((8, LANES), F32),) * 6
    for first in range(0, len(masks), group_step):
        groups = [2 * (place ^ mask) + side for mask in masks[first : first + group_step]]
        held = []
        for group in groups:
            tile = target_ref[pl.ds(pl.multiple_of(group * targets, 8), 8), 0:8]
            held.append([jnp.broadcast_to(tile[:, c : c + 1], (8, LANES)) for c in range(6)])

        def add_stars(part, sums, held=held):
            for s in range(all_ref.shape[1] // LANES):
                tile = all_ref[pl.ds(pl.multiple_of(part * 8, 8), 8), s * LANES : (s + 1) * LANES]
                source = [jnp.broadcast_to(tile[c : c + 1], (8, LANES)) for c in range(7)]
                sums = tuple(pair_sums(held[n], source, source[6], softening, sums[n]) for n in range(len(held)))
            return sums

        sums = lax.fori_loop(0, PARTS // 2, lambda n, sums: add_stars(2 * n + 1, add_stars(2 * n, sums)), (zeros,) * len(held))
        for n, group in enumerate(groups):
            irregular = zeros
            for j in range(slot_ref.shape[0] // lines):
                at = j * lines + group
                near = listed_ref[pl.ds(pl.multiple_of(at * 8, 8), 8), :]
                mass = jnp.where(slot_ref[pl.ds(at, 1), :] == row, near[6:7], 0.0)
                irregular = pair_sums(held[n], [near[c : c + 1] for c in range(6)], mass, softening, irregular)
            result = zeros[0]
            for c, values in enumerate(sums[n] + irregular):
                value = jnp.sum(values, axis=1, keepdims=True)
                result = jnp.where(lane == -c * targets % LANES + row, value, result)
            out_ref[first + n : first + n + 1] = jnp.sum(result, axis=0, keepdims=True)


def share_kernel(mine_ref, partner_ref, *out_refs):
    for n, out_ref in enumerate(out_refs):
        out_ref[...] = mine_ref[n : n + 1] + partner_ref[n + 1 : n + 2]


def unfold(row, targets):
    wide = jnp.broadcast_to(row, (LANES // targets, LANES))
    return pltpu.roll(wide, 0, 1, stride=targets, stride_axis=0)[:, 0:targets]


def correct_kernel(targets, kept_ref, mine_ref, partner_ref, *refs):
    sums_refs, (state_ref, forces_ref, terms_ref) = refs[:-3], refs[-3:]
    lines = 2 * (len(sums_refs) + 1)
    span = lines * targets
    total = mine_ref[0:1] + partner_ref[0:1]
    for sums_ref in sums_refs:
        total = total + sums_ref[...]
    kept = kept_ref[...]
    piece = min(span, LANES)
    at = line_of(lax.axis_index("stars")) * targets
    moved = pltpu.roll(kept, (LANES - at % piece) % LANES, 1)
    turned = {}
    rows = []
    for c in range(6):
        r, begin = divmod(c * span, LANES)
        if begin not in turned:
            turned[begin] = turn(moved, -begin)
        value = turned[begin][r : r + 1]
        for q in range(1, span // piece):
            value = jnp.where(at // piece == q, turned[begin][r + q : r + q + 1], value)
        rows.append(value[:, 0:targets])
    position, velocity = jnp.concatenate(rows[0:3], axis=0), jnp.concatenate(rows[3:6], axis=0)
    r, begin = divmod(6 * span, LANES)
    words = unfold(turn(kept[r : r + 1], -begin), targets)
    step = words[0:1]
    old_accel = jnp.concatenate([words[-c : LANES // targets + 1 - c] for c in (1, 2, 3)], axis=0)
    old_jerk = jnp.concatenate([words[-c : LANES // targets + 1 - c] for c in (4, 5, 6)], axis=0)
    rows = unfold(total, targets)
    accel, jerk, irregular = rows[0:3], rows[3:6], rows[6:12]
    change = accel - old_accel
    second = 3.0 * change - step * (2.0 * old_jerk + jerk)
    third = -2.0 * change + step * (old_jerk + jerk)
    state_ref[0:3] = position + step * step * (second / 12.0 + third / 20.0)
    state_ref[3:6] = velocity + step * (second / 3.0 + third / 4.0)
    forces = jnp.concatenate([irregular, rows[0:6] - irregular, jnp.zeros((4, targets), F32)], axis=0)
    forces_ref[...] = forces.T[:, 0:12]
    terms_ref[0:3] = second
    terms_ref[3:6] = third


def exchange(rows, devices):
    wide = rows.reshape(devices, 1, -1)
    order = [[spaced(place, devices) for place in range(devices)]]
    return lax.all_to_all(wide, "stars", 0, 0, axis_index_groups=order, tiled=True).reshape(rows.shape)


def per_device(star_state, old_force, star_mass, elapsed, active_ids, neighbours, list_length):
    stars_dev = star_state.shape[1]
    devices = lax.axis_size("stars")
    lines = devices // PARTS
    targets, slots = neighbours.shape
    cap = 2 * targets * slots // devices
    blocks = stars_dev // LANES
    request_rows = max(1, PARTS * cap // LANES)
    back_rows = -(-(6 * lines + 7) * targets // LANES)
    softening = 0.25 * math.sqrt(slots) / (stars_dev * devices)

    def shape(*dims, dtype=F32):
        return jax.ShapeDtypeStruct(dims, dtype)

    def cost(flops):
        return pl.CostEstimate(flops=flops, bytes_accessed=1 << 20, transcendentals=0)

    def swap(value, mask):
        return lax.ppermute(value, "stars", [(i, i ^ mask) for i in range(devices)])

    given = (
        active_ids,
        list_length,
        neighbours,
        star_state,
        old_force,
        star_mass.reshape(blocks, LANES),
        elapsed.reshape(blocks, LANES),
    )
    request, stars, table = pl.pallas_call(
        functools.partial(first_kernel, stars_dev, cap),
        out_shape=(
            shape(devices * (request_rows + 1), LANES, dtype=I32),
            pltpu.VMEM((8, stars_dev), F32),
            pltpu.VMEM((blocks * 16, 3 * LANES), BF16),
        ),
        in_specs=[HBM] * 7,
        out_specs=(VMEM,) * 3,
        scratch_shapes=[
            pltpu.SMEM((targets,), I32),
            pltpu.SMEM((targets,), I32),
            *(pltpu.VMEM(value.shape, value.dtype) for value in given[2:]),
            pltpu.SemaphoreType.DMA((7,)),
        ],
        compiler_params=PARAMS,
    )(*(pltpu.with_memory_space_constraint(value, pltpu.HBM) for value in given))
    asked = exchange(request, devices)
    shared = [stars, *(swap(stars, 2 * mask) for mask in (3, 2, 1))]
    sent = pl.pallas_call(
        functools.partial(own_kernel, stars_dev, targets),
        out_shape=shape(devices * back_rows, LANES),
        in_specs=[VMEM] * 2,
        out_specs=VMEM,
        compiler_params=PARAMS,
    )(asked, table)
    sent = exchange(sent, devices)
    every, listed, slot = pl.pallas_call(
        functools.partial(listed_kernel, cap, targets),
        out_shape=(
            shape(PARTS * 8, stars_dev),
            shape(lines * request_rows * 8, LANES),
            shape(lines * request_rows, LANES, dtype=I32),
        ),
        in_specs=[VMEM] * (1 + PARTS),
        out_specs=(VMEM,) * 3,
        scratch_shapes=[pltpu.VMEM((PARTS * blocks * 8, 3 * LANES), BF16)],
        compiler_params=PARAMS,
        cost_estimate=cost(1 << 24),
    )(asked, *shared)
    kept_rows = -(-back_rows // 8) * 8

    places = lines // 2

    def forces_of(kernel, core, masks, given, *kept):
        return pl.pallas_call(
            functools.partial(kernel, softening, targets, 4, core, masks),
            out_shape=(shape(-(-len(masks) // 8) * 8, LANES), *kept),
            in_specs=[VMEM] * 4,
            out_specs=(VMEM,) * (1 + len(kept)),
            compiler_params=PARAMS,
        )(given, every, listed, slot)

    theirs, kept, upright = forces_of(
        first_force_kernel, 1, range(places), sent, shape(kept_rows, LANES), shape(lines * targets, LANES)
    )
    (others,) = forces_of(force_kernel, 0, range(1, places), upright)
    theirs = swap(theirs, 1)
    sums = pl.pallas_call(
        share_kernel,
        out_shape=(shape(1, LANES),) * (places - 1),
        in_specs=[VMEM] * 2,
        out_specs=(VMEM,) * (places - 1),
        compiler_params=PARAMS,
    )(others, theirs)
    sums = [swap(sums[mask - 1], mask * 2 * PARTS) for mask in range(places - 1, 0, -1)]
    (mine,) = forces_of(force_kernel, 0, range(1), upright)
    state, forces, terms = pl.pallas_call(
        functools.partial(correct_kernel, targets),
        out_shape=(shape(6, targets), shape(targets, 12), shape(6, targets)),
        in_specs=[VMEM] * (2 + places),
        out_specs=(VMEM,) * 3,
        compiler_params=PARAMS,
    )(kept, mine, theirs, *sums)
    return state, forces.T, terms


def solution(mesh):
    placed = (
        P(None, "stars"),
        P(None, "stars"),
        P("stars"),
        P("stars"),
        P("stars"),
        P("stars", None),
        P("stars"),
    )
    return jax.shard_map(
        per_device,
        mesh=mesh,
        in_specs=placed,
        out_specs=(P(None, "stars"), P(None, "stars"), P(None, "stars")),
        check_vma=False,
    )
```
